32 devices in a mesh: px: 8 (over z, x), vx: 4 (over y, core).
Axes of the slice: x: 2, y: 2, z: 4, core: 2. Of those that a mesh axis runs over, the one named last changes fastest.
Arguments:
- value_field: float32 [16, 96, 64, 384], P('px', 'vx'), may hold values from -6 to 6
- cost_field: float32 [16, 96, 64, 384], P('px', 'vx'), may hold values from -6 to 6
- accel_first: float32 [16, 96], P('px', 'vx'), may hold values from -3 to 3
- accel_second: float32 [64, 384], replicated, may hold values from -1 to 1
Outputs:
- final_value: float32 [16, 96, 64, 384], P('px', 'vx')
- funnel_slice: float32 [16, 384], P('px')
The draws below stay inside these ranges and needn't reach their ends.
All inputs are finite; a program needn't handle non-finite values.
Results may differ from the reference program's by a relative error of at most 0.00002.
Values sent between devices are 32-bit elements; how exact they have to be, the bound alone decides.
No kernel may reach another device: no remote copies, remote signals or barrier semaphores. Data moves between devices by JAX's collectives and lax.ppermute only.
A program may use at most 128 MiB of HBM per device.

```python
import jax
import jax.numpy as jnp
from jax import lax

NVY = 64
NY = 384
NX = 16
NVX = 96


def draw_accel_first(key, part):
    rise = 1.0 + 2.0 * jnp.arange(NX, dtype=jnp.float32) / max(NX - 1, 1)
    base = jax.random.uniform(key, (NX, NVX), jnp.float32, -1.0, 1.0)
    return base * rise[:, None]


def shard_levels(stream_key, dims, shards, low, top_value):
    def one(position, blocks):
        steps = jax.random.uniform(jax.random.fold_in(jax.random.fold_in(stream_key, 6), position), (blocks,), jnp.float32, low / len(shards), top_value / len(shards))
        return jnp.repeat(jnp.exp(steps), dims[position] // blocks).reshape((-1,) + (1,) * (len(dims) - position - 1))

    loudness = one(*shards[0])
    for cut in shards[1:]:
        loudness = loudness * one(*cut)
    return loudness


def noise(rng, dims, scale, limit, pieces=(), kind=jnp.bfloat16):
    drawn = scale * jax.random.normal(rng, dims, jnp.float32)
    if pieces:
        drawn = drawn * shard_levels(rng, dims, pieces, -0.22, 0.18)
    return jnp.clip(drawn, -limit, limit).astype(kind)


def setup_inputs(seed: int = 0) -> dict:
    splits = jax.random.split(jax.random.key(seed), 5)
    return {
        "value_field": noise(splits[0], (NX, NVX, NVY, NY), 1.0, 6.0, ((0, 8), (1, 4)), jnp.float32),
        "cost_field": noise(splits[1], (NX, NVX, NVY, NY), 1.0, 6.0, ((0, 8), (1, 4)), jnp.float32),
        "accel_first": draw_accel_first(jax.random.fold_in(splits[4], 71), 0),
        "accel_second": jnp.clip(jax.random.uniform(splits[3], (NVY, NY), jnp.float32, -1.0, 1.0), -1.0, 1.0),
    }


VELOCITY_LIMIT = 1.0
PLANNER_SPEED = 0.3
DISTURBANCE = 0.2
CONTROL_COST = 1.0
COURANT = 0.5


def interior(padded, dimension, offset):
    index_list = []
    for axis_number in range(4):
        size_here = padded.shape[axis_number]
        if axis_number == dimension:
            index_list.append(slice(1 + offset, size_here - 1 + offset))
        else:
            index_list.append(slice(1, size_here - 1))
    return padded[tuple(index_list)]


def slopes(padded, spacings):
    center = interior(padded, 0, 0)
    gradients = []
    curvatures = []
    for dimension in range(4):
        upper = interior(padded, dimension, 1)
        lower = interior(padded, dimension, -1)
        gradients.append((upper - lower) / (2.0 * spacings[dimension]))
        curvatures.append((upper - 2.0 * center + lower) / spacings[dimension])
    return center, gradients, curvatures


def hamiltonian(gradients, curvatures, speed_first, speed_second, push_first, push_second, rates):
    total = gradients[0] * speed_first + gradients[3] * speed_second
    total = total + PLANNER_SPEED * (jnp.abs(gradients[0]) + jnp.abs(gradients[3]))
    total = total + gradients[1] * push_first + gradients[2] * push_second
    total = total + DISTURBANCE * (jnp.abs(gradients[1]) + jnp.abs(gradients[2]))
    total = total - (gradients[1] * gradients[1] + gradients[2] * gradients[2]) / (2.0 * CONTROL_COST)
    damping = rates[0] * curvatures[0] + rates[1] * curvatures[1] + rates[2] * curvatures[2] + rates[3] * curvatures[3]
    return total - 0.5 * damping


def reference(value_field, cost_field, accel_first, accel_second):
    speed_first = ((2.0 * jnp.arange(NVX, dtype=jnp.float32) + 1.0 - NVX) * (VELOCITY_LIMIT / NVX)).reshape(NVX, 1, 1)
    speed_second = ((2.0 * jnp.arange(NVY, dtype=jnp.float32) + 1.0 - NVY) * (VELOCITY_LIMIT / NVY)).reshape(NVY, 1)
    velocity_step_x = 2.0 * VELOCITY_LIMIT / NVX
    velocity_step_y = 2.0 * VELOCITY_LIMIT / NVY
    position_step = velocity_step_x * velocity_step_y
    spacings = (position_step, velocity_step_x, velocity_step_y, position_step)
    push_limit = jnp.max(jnp.abs(accel_first))
    push_second_limit = jnp.max(jnp.abs(accel_second))
    rate_first = VELOCITY_LIMIT * (NVX - 1) / NVX + PLANNER_SPEED
    rate_last = VELOCITY_LIMIT * (NVY - 1) / NVY + PLANNER_SPEED
    indices = jnp.arange(NX, dtype=jnp.int32)

    def rates_of(padded):
        def row_maxima(index):
            block = lax.dynamic_slice_in_dim(padded, index, 3, 0)
            center, gradients, curvatures = slopes(block, spacings)
            return jnp.max(jnp.abs(gradients[1])), jnp.max(jnp.abs(gradients[2]))
        first_max, second_max = lax.map(row_maxima, indices)
        return (rate_first, push_limit + DISTURBANCE + jnp.max(first_max) / CONTROL_COST,
                push_second_limit + DISTURBANCE + jnp.max(second_max) / CONTROL_COST, rate_last)

    def sweep(padded, rates, step_size, base):
        def row_update(index):
            block = lax.dynamic_slice_in_dim(padded, index, 3, 0)
            center, gradients, curvatures = slopes(block, spacings)
            push_row = lax.dynamic_slice_in_dim(accel_first, index, 1, 0).reshape(1, NVX, 1, 1)
            change = hamiltonian(gradients, curvatures, speed_first, speed_second, push_row, accel_second, rates)
            cost_row = lax.dynamic_slice_in_dim(cost_field, index, 1, 0)
            moved = center + step_size * change
            if base is not None:
                base_row = lax.dynamic_slice_in_dim(base, index, 1, 0)
                moved = 0.5 * base_row + 0.5 * moved
            return jnp.maximum(cost_row, moved)[0]
        return lax.map(row_update, indices)

    current = value_field
    for repeat in range(2):
        padded = jnp.pad(current, 1, mode="edge")
        rates = rates_of(padded)
        step_size = COURANT / (rates[0] / spacings[0] + rates[1] / spacings[1] + rates[2] / spacings[2] + rates[3] / spacings[3])
        middle = sweep(padded, rates, step_size, None)
        padded = jnp.pad(middle, 1, mode="edge")
        rates = rates_of(padded)
        current = sweep(padded, rates, step_size, current)
    return current, jnp.min(current, axis=(1, 2))
```

```python
import functools

import jax
import jax.numpy as jnp
from jax import lax
from jax.experimental import pallas as pl
from jax.experimental.pallas import tpu as pltpu
from jax.sharding import PartitionSpec as P

VELOCITY_LIMIT = 1.0
PLANNER_SPEED = 0.3
DISTURBANCE = 0.2
CONTROL_COST = 1.0
COURANT = 0.5

LANES = 128


def compiler_params():
    return pltpu.CompilerParams(vmem_limit_bytes=56 * 1024 * 1024)


def whole():
    return pl.BlockSpec(memory_space=pltpu.VMEM)


def scalars():
    return pl.BlockSpec(memory_space=pltpu.SMEM)


def fold(tile):
    rows = tile.shape[0]
    out = tile[0:8]
    for start in range(8, rows, 8):
        out = jnp.maximum(out, tile[start : start + 8])
    return out


def fold_min(tile):
    rows = tile.shape[0]
    out = tile[0:8]
    for start in range(8, rows, 8):
        out = jnp.minimum(out, tile[start : start + 8])
    return out


def lane_max(ref, lane):
    values = ref[...]
    position = lax.broadcasted_iota(jnp.int32, values.shape, 1)
    return jnp.max(jnp.where(position == lane, values, 0.0))


class Own:
    def __init__(self, array, outer):
        self.array, self.outer = array, outer

    def reader(self, ref, parity, half):
        row = parity if self.outer else 1 - parity
        start = pl.multiple_of(parity * half, half)
        return lambda j: ref[row, j, pl.ds(start, half), :]


class Row:
    def __init__(self, array):
        self.array = array

    def reader(self, ref, parity, half):
        return lambda j: ref[j]


def sweep(sizes, targets, rows, costs, bases, halo_rows, vx_low, vx_high, vy_next, maxima, accel_second, flags, push, speed, with_min=False):
    cells_v, half, width, total_vx, total_vy = sizes
    step_2 = 2.0 * VELOCITY_LIMIT / total_vx
    step_3 = 2.0 * VELOCITY_LIMIT / total_vy
    step_1 = step_2 * step_3
    rate_1 = VELOCITY_LIMIT * (total_vx - 1) / total_vx + PLANNER_SPEED
    rate_4 = VELOCITY_LIMIT * (total_vy - 1) / total_vy + PLANNER_SPEED
    count = len(targets)
    heun = bases is not None

    arrays = []

    def add(array):
        for position, known in enumerate(arrays):
            if known is array:
                return position
        arrays.append(array)
        return len(arrays) - 1

    needed = sorted({k for t in targets for k in (t - 1, t, t + 1) if 0 <= k <= 3})
    row_at = {k: add(rows[k].array) for k in needed}
    halo_at = {k: add(halo_rows[i]) for i, k in enumerate((-1, 4)) if any(abs(t - k) == 1 for t in targets)}
    cost_at = [add(c.array) for c in costs]
    base_at = [add(b.array) for b in bases] if heun else []
    low_at, high_at, vy_at, accel_at = add(vx_low), add(vx_high), add(vy_next), add(accel_second)
    maxima_at = [add(m) for m in maxima]
    n_in = len(arrays)

    def body(flags_ref, push_ref, speed_ref, *refs):
        ins = refs[:n_in]
        outs = refs[n_in:]
        out_rows = outs[:count]
        first_ref, second_ref, before_ref, last_ref, edge_ref, inner_ref, part_ref = outs[count : count + 7]
        min_ref = outs[count + 7] if with_min else None
        adv_up, adv_down, acc_up, acc_down = outs[-4:]
        parity, edge_low, edge_high, vx_first, vx_last = (flags_ref[i] for i in range(5))
        is_even = parity == 0

        limit_1 = lane_max(ins[maxima_at[0]], 2)
        limit_2 = lane_max(ins[maxima_at[0]], 3)

        def rates(ref):
            return (
                limit_1 + DISTURBANCE + lane_max(ref, 0) * (1.0 / (2.0 * step_2 * CONTROL_COST)),
                limit_2 + DISTURBANCE + lane_max(ref, 1) * (1.0 / (2.0 * step_3 * CONTROL_COST)),
            )

        old_2, old_3 = rates(ins[maxima_at[1]])
        rate_2, rate_3 = (old_2, old_3) if maxima_at[2] == maxima_at[1] else rates(ins[maxima_at[2]])
        total_rate = rate_1 / step_1 + old_2 / step_2 + old_3 / step_3 + rate_4 / step_1
        time_step = jnp.max(COURANT / jnp.full((8, LANES), total_rate, jnp.float32))
        scale = 0.5 * time_step if heun else time_step

        damp_1 = scale * (0.5 * rate_1 / step_1)
        damp_2 = scale * (0.5 / step_2) * rate_2
        damp_3 = scale * (0.5 / step_3) * rate_3
        damp_4 = scale * (0.5 * rate_4 / step_1)
        keep = (0.5 if heun else 1.0) + 2.0 * (damp_1 + damp_2 + damp_3 + damp_4)
        planner = scale * (PLANNER_SPEED / (2.0 * step_1))
        disturb_2 = scale * (DISTURBANCE / (2.0 * step_2))
        disturb_3 = scale * (DISTURBANCE / (2.0 * step_3))
        control_2 = scale * (1.0 / (8.0 * CONTROL_COST * step_2 * step_2))
        control_3 = scale * (1.0 / (8.0 * CONTROL_COST * step_3 * step_3))
        to_1 = scale / (2.0 * step_1)
        to_2 = scale / (2.0 * step_2)
        to_3 = scale / (2.0 * step_3)

        start = pl.multiple_of(parity * half, half)
        vy = (parity * half + lax.broadcasted_iota(jnp.int32, (half, width), 0)).astype(jnp.float32)
        speed_y = (2.0 * vy + (1.0 - total_vy)) * (VELOCITY_LIMIT / total_vy) * to_1
        adv_up[...] = speed_y + planner
        adv_down[...] = speed_y - planner
        accel = ins[accel_at][pl.ds(start, half), :] * to_3
        acc_up[...] = accel + disturb_3
        acc_down[...] = accel - disturb_3

        readers = {k: rows[k].reader(ins[row_at[k]], parity, half) for k in needed}
        cost_readers = [c.reader(ins[a], parity, half) for c, a in zip(costs, cost_at)]
        base_readers = [b.reader(ins[a], parity, half) for b, a in zip(bases, base_at)] if heun else None
        vy_row = lax.broadcasted_iota(jnp.int32, (half, width), 0)
        y_lane = lax.broadcasted_iota(jnp.int32, (half, width), 1)
        send_at = jnp.where(is_even, half - 1, 0)
        inner_at = jnp.where(is_even, half - 2, 1)
        wall_at = jnp.where(is_even, 0, half - 1)
        next_at = jnp.where(is_even, 1, half - 2)

        def neighbour(k, j, center):
            if k == -1:
                return jnp.where(edge_low == 1, center, ins[halo_at[-1]][j])
            if k == 4:
                return jnp.where(edge_high == 1, center, ins[halo_at[4]][j])
            return readers[k](j)

        def tile(i, j, low_2, high_2):
            t = targets[i]
            w = readers[t](j)
            low_1 = neighbour(t - 1, j, w)
            high_1 = neighbour(t + 1, j, w)
            if low_2 is None:
                low_2 = jnp.where(vx_first == 1, w, ins[low_at][t])
            else:
                low_2 = readers[t](low_2)
            if high_2 is None:
                high_2 = jnp.where(vx_last == 1, w, ins[high_at][t])
            else:
                high_2 = readers[t](high_2)
            beyond = ins[vy_at][3 - t, pl.ds(j, 1), :]
            below = jnp.where(is_even, w[0:1], beyond)
            above = jnp.where(is_even, beyond, w[half - 1 : half])
            low_3 = jnp.where(vy_row == 0, below, pltpu.roll(w, 1, 0))
            high_3 = jnp.where(vy_row == half - 1, above, pltpu.roll(w, half - 1, 0))
            low_4 = jnp.where(y_lane == 0, w, pltpu.roll(w, 1, 1))
            high_4 = jnp.where(y_lane == width - 1, w, pltpu.roll(w, width - 1, 1))

            flow = speed_ref[j] * to_1
            drift = push_ref[t, j] * to_2
            total = keep * w - damp_1 * (low_1 + high_1) - damp_4 * (low_4 + high_4)
            total = total - damp_2 * (low_2 + high_2) - damp_3 * (low_3 + high_3)
            slope = high_1 - low_1
            total = total + jnp.maximum((flow + planner) * slope, (flow - planner) * slope)
            slope = high_4 - low_4
            total = total + jnp.maximum(adv_up[...] * slope, adv_down[...] * slope)
            slope = high_2 - low_2
            bent = control_2 * slope
            total = total + jnp.maximum((drift + disturb_2 - bent) * slope, (drift - disturb_2 - bent) * slope)
            slope = high_3 - low_3
            bent = control_3 * slope
            total = total + jnp.maximum((acc_up[...] - bent) * slope, (acc_down[...] - bent) * slope)
            if heun:
                total = total + 0.5 * base_readers[i](j)
            y = jnp.maximum(cost_readers[i](j), total)
            out_rows[i][j] = y
            return y

        def finish(i, j, y, most_3):
            edge_ref[i, pl.ds(j, 1), :] = out_rows[i][j, pl.ds(send_at, 1), :]
            inner_ref[i, pl.ds(j, 1), :] = out_rows[i][j, pl.ds(inner_at, 1), :]
            wall = jnp.abs(out_rows[i][j, pl.ds(next_at, 1), :] - out_rows[i][j, pl.ds(wall_at, 1), :])
            bend = jnp.where(vy_row >= 2, jnp.abs(y - pltpu.roll(y, 2, 0)), 0.0)
            return jnp.maximum(most_3, jnp.maximum(fold(bend), wall))

        zero = jnp.zeros((8, width), jnp.float32)
        most_2, most_3 = zero, zero
        least = [jnp.full((8, width), jnp.inf, jnp.float32) for _ in targets]
        for i in range(count):
            y = tile(i, 0, None, 1)
            first_ref[i] = y
            most_3 = finish(i, 0, y, most_3)
            least[i] = jnp.minimum(least[i], fold_min(y))
            y = tile(i, 1, 0, 2)
            second_ref[i] = y
            most_3 = finish(i, 1, y, most_3)
            least[i] = jnp.minimum(least[i], fold_min(y))

        def step(j, carry):
            most_2, most_3, least = carry
            least = list(least)
            for i in range(count):
                y = tile(i, j, j - 1, j + 1)
                most_3 = finish(i, j, y, most_3)
                most_2 = jnp.maximum(most_2, fold(jnp.abs(y - out_rows[i][j - 2])))
                if with_min:
                    least[i] = jnp.minimum(least[i], fold_min(y))
            return most_2, most_3, tuple(least)

        most_2, most_3, least = lax.fori_loop(2, cells_v - 1, step, (most_2, most_3, tuple(least)))
        least = list(least)
        for i in range(count):
            before_ref[i] = out_rows[i][cells_v - 2]
            y = tile(i, cells_v - 1, cells_v - 2, None)
            last_ref[i] = y
            most_3 = finish(i, cells_v - 1, y, most_3)
            most_2 = jnp.maximum(most_2, fold(jnp.abs(y - out_rows[i][cells_v - 3])))
            least[i] = jnp.minimum(least[i], fold_min(y))
        part_ref[0] = most_2
        part_ref[1] = most_3
        if with_min:
            for i in range(count):
                min_ref[pl.ds(i, 1), :] = jnp.min(least[i], axis=0, keepdims=True)

    def f32(*shape):
        return jax.ShapeDtypeStruct(shape, jnp.float32)

    shapes = [f32(cells_v, half, width)] * count + [f32(count, half, width)] * 4 + [f32(count, cells_v, width)] * 2 + [f32(2, 8, width)]
    if with_min:
        shapes.append(f32(count, width))
    cells = count * cells_v * half * width
    result = pl.pallas_call(
        body,
        out_shape=shapes,
        in_specs=[scalars()] * 3 + [whole()] * n_in,
        out_specs=[whole()] * len(shapes),
        scratch_shapes=[pltpu.VMEM((half, width), jnp.float32)] * 4,
        compiler_params=compiler_params(),
        cost_estimate=pl.CostEstimate(flops=60 * cells, bytes_accessed=16 * cells, transcendentals=0),
        name="sweep_" + "".join(str(t) for t in targets),
    )(flags, push, speed, *arrays)
    return result


def spread(shape, lanes):
    position = lax.broadcasted_iota(jnp.int32, shape, 1)
    out = jnp.zeros(shape, jnp.float32)
    for lane, value in enumerate(lanes):
        out = jnp.where(position == lane, value, out)
    return out


def first_maxima(devices, value, vx_low, vx_high, accel_first, accel_second, flags):
    rows, cells_v, total_vy, width = value.shape

    def body(flags_ref, v_ref, low_ref, high_ref, first_ref, second_ref, out_ref):
        vx_first, vx_last = flags_ref[3], flags_ref[4]
        vy_row = lax.broadcasted_iota(jnp.int32, (total_vy, width), 0)

        def of_vy(x):
            inner = jnp.where(vy_row >= 2, jnp.abs(x - pltpu.roll(x, 2, 0)), 0.0)
            wall = jnp.maximum(jnp.abs(x[1:2] - x[0:1]), jnp.abs(x[total_vy - 1 : total_vy] - x[total_vy - 2 : total_vy - 1]))
            return jnp.maximum(fold(inner), wall)

        most_2 = jnp.zeros((8, width), jnp.float32)
        most_3 = jnp.zeros((8, width), jnp.float32)
        for r in range(rows):
            x = v_ref[r, 0]
            most_3 = jnp.maximum(most_3, of_vy(x))
            most_2 = jnp.maximum(most_2, fold(jnp.abs(v_ref[r, 1] - jnp.where(vx_first == 1, x, low_ref[r]))))
            x = v_ref[r, cells_v - 1]
            most_3 = jnp.maximum(most_3, of_vy(x))
            most_2 = jnp.maximum(most_2, fold(jnp.abs(v_ref[r, cells_v - 2] - jnp.where(vx_last == 1, x, high_ref[r]))))

            def step(j, carry, r=r):
                most_2, most_3 = carry
                most_3 = jnp.maximum(most_3, of_vy(v_ref[r, j]))
                most_2 = jnp.maximum(most_2, fold(jnp.abs(v_ref[r, j + 1] - v_ref[r, j - 1])))
                return most_2, most_3

            most_2, most_3 = lax.fori_loop(1, cells_v - 1, step, (most_2, most_3))
        values = (jnp.max(most_2), jnp.max(most_3), jnp.max(jnp.abs(first_ref[...])), jnp.max(jnp.abs(second_ref[...])))
        out_ref[...] = spread((devices, LANES), values)

    return pl.pallas_call(
        body,
        out_shape=jax.ShapeDtypeStruct((devices, LANES), jnp.float32),
        in_specs=[scalars()] + [whole()] * 5,
        out_specs=whole(),
        compiler_params=compiler_params(),
        name="first_maxima",
    )(flags, value, vx_low, vx_high, accel_first, accel_second)


def edge_maxima(devices, parts, edges, vx_low, vx_high, inner, vy_next, flags):
    first, second, before, last = edges
    n_parts = len(parts)

    def body(flags_ref, first_ref, second_ref, before_ref, last_ref, low_ref, high_ref, inner_ref, next_ref, *rest):
        part_refs, out_ref = rest[:n_parts], rest[n_parts]
        vx_first, vx_last = flags_ref[3], flags_ref[4]
        most_2 = functools.reduce(jnp.maximum, [p[0] for p in part_refs])
        most_3 = functools.reduce(jnp.maximum, [p[1] for p in part_refs])
        for t in range(4):
            low = jnp.where(vx_first == 1, first_ref[t], low_ref[t])
            high = jnp.where(vx_last == 1, last_ref[t], high_ref[t])
            most_2 = jnp.maximum(most_2, fold(jnp.abs(second_ref[t] - low)))
            most_2 = jnp.maximum(most_2, fold(jnp.abs(high - before_ref[t])))
            most_3 = jnp.maximum(most_3, fold(jnp.abs(inner_ref[t] - next_ref[3 - t])))
        out_ref[...] = spread((devices, LANES), (jnp.max(most_2), jnp.max(most_3)))

    return pl.pallas_call(
        body,
        out_shape=jax.ShapeDtypeStruct((devices, LANES), jnp.float32),
        in_specs=[scalars()] + [whole()] * (8 + n_parts),
        out_specs=whole(),
        compiler_params=compiler_params(),
        name="edge_maxima",
    )(flags, first, second, before, last, vx_low, vx_high, inner, vy_next, *parts)


def assemble(parity, own, received, shape):
    rows, cells_v, total_vy, width = shape
    half = total_vy // 2
    block = 8 if cells_v % 8 == 0 else cells_v

    def body(parity_ref, own_outer, own_inner, got_outer, got_inner, out_ref):
        parity = parity_ref[0]
        mine = pl.multiple_of(parity * half, half)
        other = pl.multiple_of((1 - parity) * half, half)
        out_ref[parity, :, pl.ds(mine, half), :] = own_outer[...]
        out_ref[1 - parity, :, pl.ds(mine, half), :] = own_inner[...]
        out_ref[parity, :, pl.ds(other, half), :] = got_outer[...]
        out_ref[1 - parity, :, pl.ds(other, half), :] = got_inner[...]

    part = pl.BlockSpec((block, half, width), lambda j: (j, 0, 0))
    return pl.pallas_call(
        body,
        grid=(cells_v // block,),
        out_shape=jax.ShapeDtypeStruct(shape, jnp.float32),
        in_specs=[scalars()] + [part] * 4,
        out_specs=pl.BlockSpec((rows, block, total_vy, width), lambda j: (0, j, 0, 0)),
        compiler_params=compiler_params(),
        name="assemble",
    )(parity, *own, *received)


def per_device(value, cost, accel_first, accel_second):
    n_px, n_vx = lax.axis_size("px"), lax.axis_size("vx")
    devices = n_px * n_vx
    rows, cells_v, total_vy, width = value.shape
    half = total_vy // 2
    total_vx = cells_v * n_vx
    sizes = (cells_v, half, width, total_vx, total_vy)
    px, vx = lax.axis_index("px"), lax.axis_index("vx")
    parity = px % 2
    flags = jnp.stack(
        [
            parity,
            ((px == 0) | (px == n_px - 1)).astype(jnp.int32),
            ((px == 1) | (px == n_px - 2)).astype(jnp.int32),
            (vx == 0).astype(jnp.int32),
            (vx == n_vx - 1).astype(jnp.int32),
        ]
    ).astype(jnp.int32)

    def partner(x):
        return lax.ppermute(x, "px", [(i, i ^ 1) for i in range(n_px)])

    def from_low_vx(x):
        return lax.ppermute(x, "vx", [(i, i + 1) for i in range(n_vx - 1)])

    def from_high_vx(x):
        return lax.ppermute(x, "vx", [(i + 1, i) for i in range(n_vx - 1)])

    def halo_before(outermost):
        moves = [(i, i + 2) for i in range(0, n_px - 2, 2)] + [(i, i - 2) for i in range(3, n_px, 2)]
        return lax.ppermute(outermost, "px", moves)

    def halo_after(outer):
        moves = [(i, i - 2) for i in range(2, n_px, 2)] + [(i, i + 2) for i in range(1, n_px - 2, 2)]
        return lax.ppermute(outer, "px", moves)

    def share(maxima):
        return lax.all_to_all(maxima, ("px", "vx"), 0, 0, tiled=True)

    def half_of(array, row, which):
        return lax.dynamic_slice(array, (row, 0, which * half, 0), (1, cells_v, half, width))[0]

    value_outer_got = partner(half_of(value, parity, 1 - parity))
    value_inner_got = partner(half_of(value, 1 - parity, 1 - parity))
    cost_send = (half_of(cost, parity, 1 - parity), half_of(cost, 1 - parity, 1 - parity))

    low_own = from_low_vx(value[:, cells_v - 1])
    high_own = from_high_vx(value[:, 0])
    shared_first = share(first_maxima(devices, value, low_own, high_own, accel_first, accel_second, flags))

    def chain_halo(own):
        given = lax.dynamic_slice(own, (0, (1 - parity) * half, 0), (rows, half, width))
        mine = lax.dynamic_slice(own, (0, parity * half, 0), (rows, half, width))
        return mine, given

    low_mine, low_given = chain_halo(low_own)
    high_mine, high_given = chain_halo(high_own)
    got = partner(jnp.concatenate([low_given, high_given], axis=0))
    row_given = lax.dynamic_slice(value, (0, 0, half - parity, 0), (rows, cells_v, 1, width))[:, :, 0]
    row_needed = lax.dynamic_slice(value, (0, 0, half - parity, 0), (rows, cells_v, 1, width))[:, :, 0]
    row_given = lax.dynamic_slice(value, (0, 0, half - 1 + parity, 0), (rows, cells_v, 1, width))[:, :, 0]
    row_got = partner(row_given)
    push_got = partner(accel_first)

    def pick(x, which):
        return lax.dynamic_index_in_dim(x, which, 0, keepdims=True)

    def in_chain(mine, others):
        return jnp.concatenate([pick(mine, parity), pick(mine, 1 - parity), pick(others, parity), pick(others, 1 - parity)], axis=0)

    vx_low = in_chain(low_mine, got[:rows])
    vx_high = in_chain(high_mine, got[rows:])
    vy_next = jnp.concatenate([pick(row_got, 1 - parity), pick(row_got, parity), pick(row_needed, 1 - parity), pick(row_needed, parity)], axis=0)
    push = in_chain(accel_first, push_got)
    positions = (vx * cells_v + jnp.arange(cells_v, dtype=jnp.int32)).astype(jnp.float32)
    speed = (2.0 * positions + 1.0 - total_vx) * (VELOCITY_LIMIT / total_vx)
    speed = jnp.where(parity == 0, speed, -speed)

    chain = [Own(value, True), Own(value, False), Row(value_inner_got), Row(value_outer_got)]
    halo_rows = (halo_before(value_outer_got), halo_after(half_of(value, parity, parity)))
    cost_send, _ = lax.optimization_barrier((cost_send, (value_outer_got, value_inner_got)))
    cost_outer_got = partner(cost_send[0])
    cost_inner_got = partner(cost_send[1])
    costs = [Own(cost, True), Own(cost, False), Row(cost_inner_got), Row(cost_outer_got)]

    run = functools.partial(sweep, sizes, accel_second=accel_second, flags=flags, push=push, speed=speed)

    def exchange(outs):
        fields, (first, second, before, last, edge, inner, part) = outs[:4], outs[4:11]
        new_halo = (halo_before(fields[3]), halo_after(fields[0]))
        low, high, row = from_low_vx(last), from_high_vx(first), partner(edge)
        shared = share(edge_maxima(devices, [part], (first, second, before, last), low, high, inner, row, flags))
        return [Row(f) for f in fields], new_halo, low, high, row, shared

    def sub(targets, **kw):
        return run(targets, chain, [costs[t] for t in targets], None, halo_rows, vx_low, vx_high, vy_next, (shared_first,) * 3)

    own_out = sub((0, 1))
    outer_out = sub((3,))
    inner_out = sub((2,))
    joined = [jnp.concatenate([a, b, c], axis=0) for a, b, c in zip(own_out[2:8], inner_out[1:7], outer_out[1:7])]
    first, second, before, last, edge, inner = joined
    fields = [own_out[0], own_out[1], inner_out[0], outer_out[0]]
    halo_rows = (halo_before(fields[3]), halo_after(fields[0]))
    vx_low, vx_high, vy_next = from_low_vx(last), from_high_vx(first), partner(edge)
    shared = share(
        edge_maxima(devices, [own_out[8], inner_out[7], outer_out[7]], (first, second, before, last), vx_low, vx_high, inner, vy_next, flags)
    )
    middle = [Row(f) for f in fields]

    every = (0, 1, 2, 3)
    outs = run(every, middle, costs, chain, halo_rows, vx_low, vx_high, vy_next, (shared_first, shared_first, shared))
    chain, halo_rows, vx_low, vx_high, vy_next, shared_second = exchange(outs)
    outs = run(every, chain, costs, None, halo_rows, vx_low, vx_high, vy_next, (shared_first, shared_second, shared_second))
    middle, halo_rows, vx_low, vx_high, vy_next, shared = exchange(outs)
    outs = run(every, middle, costs, chain, halo_rows, vx_low, vx_high, vy_next, (shared_first, shared_second, shared), with_min=True)

    fields, least = outs[:4], outs[-1]
    least_got = partner(least[2:])
    outer_got = partner(fields[3])
    inner_got = partner(fields[2])
    final = assemble(flags[:1], (fields[0], fields[1]), (outer_got, inner_got), value.shape)
    funnel = jnp.minimum(least[:2], least_got[::-1])
    funnel = jnp.concatenate([pick(funnel, parity), pick(funnel, 1 - parity)], axis=0)
    return final, lax.pmin(funnel, "vx")


def solution(mesh):
    placed = (P("px", "vx", None, None), P("px", "vx", None, None), P("px", "vx"), P())
    return jax.shard_map(
        per_device,
        mesh=mesh,
        in_specs=placed,
        out_specs=(P("px", "vx", None, None), P("px", None)),
        check_vma=False,
    )
```

```python
import functools

import jax
import jax.numpy as jnp
from jax import lax
from jax.experimental import pallas as pl
from jax.experimental.pallas import tpu as pltpu
from jax.sharding import PartitionSpec as P

VELOCITY_LIMIT = 1.0
PLANNER_SPEED = 0.3
DISTURBANCE = 0.2
CONTROL_COST = 1.0
COURANT = 0.5

LANES = 128


def compiler_params():
    return pltpu.CompilerParams(vmem_limit_bytes=8 * 1024 * 1024)


def whole():
    return pl.BlockSpec(memory_space=pltpu.VMEM)


def scalars():
    return pl.BlockSpec(memory_space=pltpu.SMEM)


def fold(tile):
    rows = tile.shape[0]
    out = tile[0:8]
    for start in range(8, rows, 8):
        out = jnp.maximum(out, tile[start : start + 8])
    return out


def fold_min(tile):
    rows = tile.shape[0]
    out = tile[0:8]
    for start in range(8, rows, 8):
        out = jnp.minimum(out, tile[start : start + 8])
    return out


def lane_max(ref, lane):
    values = ref[...]
    position = lax.broadcasted_iota(jnp.int32, values.shape, 1)
    return jnp.max(jnp.where(position == lane, values, 0.0))


class Own:
    def __init__(self, array, outer):
        self.array, self.outer = array, outer

    def reader(self, ref, parity, half):
        row = parity if self.outer else 1 - parity
        start = pl.multiple_of(parity * half, half)
        return lambda j, g: ref[row, j, pl.ds(pl.multiple_of(start + 8 * g, 8), 8), :]


class Row:
    def __init__(self, array):
        self.array = array

    def reader(self, ref, parity, half):
        return lambda j, g: ref[j, pl.ds(8 * g, 8), :]


class Scalars:
    def __init__(self, sizes):
        cells_v, half, width, total_vx, total_vy = sizes
        self.step_2 = 2.0 * VELOCITY_LIMIT / total_vx
        self.step_3 = 2.0 * VELOCITY_LIMIT / total_vy
        self.step_1 = self.step_2 * self.step_3
        self.rate_1 = VELOCITY_LIMIT * (total_vx - 1) / total_vx + PLANNER_SPEED
        self.rate_4 = VELOCITY_LIMIT * (total_vy - 1) / total_vy + PLANNER_SPEED

    def rates(self, limits, maxima):
        rate_2 = lane_max(limits, 2) + DISTURBANCE + lane_max(maxima, 0) * (0.5 / (self.step_2 * CONTROL_COST))
        rate_3 = lane_max(limits, 3) + DISTURBANCE + lane_max(maxima, 1) * (0.5 / (self.step_3 * CONTROL_COST))
        return rate_2 * (1.0 / self.step_2), rate_3 * (1.0 / self.step_3)

    def time_step(self, rates):
        total = rates[0] + rates[1] + (self.rate_1 + self.rate_4) / self.step_1
        return jnp.max(COURANT / jnp.full((8, LANES), total, jnp.float32))


class Operands:
    def __init__(self):
        self.arrays = []

    def add(self, array):
        for position, known in enumerate(self.arrays):
            if known is array:
                return position
        self.arrays.append(array)
        return len(self.arrays) - 1


def f32(*shape):
    return jax.ShapeDtypeStruct(shape, jnp.float32)


def estimate(cells, flops):
    return pl.CostEstimate(flops=flops * cells, bytes_accessed=4 * cells, transcendentals=0)


def slabs(tile):
    return [tile[start : start + 8] for start in range(0, tile.shape[0], 8)]


def advance(sizes, targets, rows, bases, halo_rows, vx_low, vx_high, vy_next, maxima, stepper, accel_second, flags, push, speed):
    cells_v, half, width, total_vx, total_vy = sizes
    count = len(targets)
    heun = bases is not None
    late = stepper is None
    full = not heun and not late
    ops = Operands()
    needed = sorted({k for t in targets for k in (t - 1, t, t + 1) if 0 <= k <= 3})
    row_at = {k: ops.add(rows[k].array) for k in needed}
    halo_at = {k: ops.add(halo_rows[i]) for i, k in enumerate((-1, 4)) if any(abs(t - k) == 1 for t in targets)}
    base_at = [ops.add(b.array) for b in bases] if heun else []
    low_at, high_at, vy_at, accel_at = ops.add(vx_low), ops.add(vx_high), ops.add(vy_next), ops.add(accel_second)
    maxima_at = [] if late else [ops.add(maxima), ops.add(stepper)]
    n_in = len(ops.arrays)
    n_out = count * (1 if full else 3)
    groups = half // 8

    def body(flags_ref, push_ref, speed_ref, *refs):
        ins, outs = refs[:n_in], refs[n_in : n_in + n_out]
        adv_up, adv_down, acc_up, acc_down = refs[n_in + n_out :]
        parity, edge_low, edge_high, vx_first, vx_last = (flags_ref[i] for i in range(5))
        is_even = parity == 0
        known = Scalars(sizes)
        step_1, step_2, step_3 = known.step_1, known.step_2, known.step_3
        if late:
            scale = jnp.float32(1.0)
        else:
            rates = known.rates(ins[maxima_at[0]], ins[maxima_at[1]])
            scale = known.time_step(rates) * (0.5 if heun else 1.0)
        damp_1 = scale * (0.5 * known.rate_1 / step_1)
        damp_4 = scale * (0.5 * known.rate_4 / step_1)
        keep = 2.0 * (damp_1 + damp_4)
        if not late:
            keep = keep + (0.5 if heun else 1.0)
        if full:
            damp_2, damp_3 = scale * 0.5 * rates[0], scale * 0.5 * rates[1]
        planner = scale * (PLANNER_SPEED / (2.0 * step_1))
        disturb_2 = scale * (DISTURBANCE / (2.0 * step_2))
        disturb_3 = scale * (DISTURBANCE / (2.0 * step_3))
        control_2 = scale * (1.0 / (8.0 * CONTROL_COST * step_2 * step_2))
        control_3 = scale * (1.0 / (8.0 * CONTROL_COST * step_3 * step_3))
        to_1, to_2, to_3 = scale / (2.0 * step_1), scale / (2.0 * step_2), scale / (2.0 * step_3)

        start = pl.multiple_of(parity * half, half)
        vy = (parity * half + lax.broadcasted_iota(jnp.int32, (half, LANES), 0)).astype(jnp.float32)
        speed_y = (2.0 * vy + (1.0 - total_vy)) * (VELOCITY_LIMIT / total_vy) * to_1
        adv_up[...] = speed_y + planner
        adv_down[...] = speed_y - planner
        accel = ins[accel_at][pl.ds(start, half), :] * to_3
        acc_up[...] = accel + disturb_3
        acc_down[...] = accel - disturb_3

        readers = {k: rows[k].reader(ins[row_at[k]], parity, half) for k in needed}
        base_readers = [b.reader(ins[a], parity, half) for b, a in zip(bases, base_at)] if heun else None
        sublane = lax.broadcasted_iota(jnp.int32, (8, width), 0)
        lane = lax.broadcasted_iota(jnp.int32, (8, LANES), 1)

        def neighbour(k, j, g, center):
            if k == -1:
                return jnp.where(edge_low == 1, center, ins[halo_at[-1]][j, pl.ds(8 * g, 8), :])
            if k == 4:
                return jnp.where(edge_high == 1, center, ins[halo_at[4]][j, pl.ds(8 * g, 8), :])
            return readers[k](j, g)

        def lane_pieces(x):
            return [x[:, start : start + LANES] for start in range(0, width, LANES)]

        def upwind(up, down, slope):
            return jnp.maximum(up * slope, down * slope)

        def tile(i, j, low_j, high_j):
            t = targets[i]
            flow = speed_ref[j] * to_1
            drift = push_ref[t, j] * to_2
            flow_up, flow_down = flow + planner, flow - planner
            drift_up, drift_down = drift + disturb_2, drift - disturb_2
            beyond = ins[vy_at][3 - t, pl.ds(j, 1), :]
            first = readers[t](j, 0)
            last = readers[t](j, groups - 1)
            below = jnp.broadcast_to(jnp.where(is_even, first[0:1], beyond), (8, width))
            above = jnp.broadcast_to(jnp.where(is_even, beyond, last[7:8]), (8, width))
            ups = [below] + [pltpu.roll(readers[t](j, g), 1, 0) for g in range(groups)]
            downs = [pltpu.roll(readers[t](j, g), 7, 0) for g in range(groups)] + [above]
            for g in range(groups):
                w = readers[t](j, g)
                here = pl.ds(8 * g, 8)
                low_1, high_1 = neighbour(t - 1, j, g, w), neighbour(t + 1, j, g, w)
                total = keep * w - damp_1 * (low_1 + high_1)
                total = total + upwind(flow_up, flow_down, high_1 - low_1)

                pieces = lane_pieces(w)
                right = [pltpu.roll(p, 1, 1) for p in pieces]
                left = [pltpu.roll(p, LANES - 1, 1) for p in pieces]
                parts = []
                for p in range(len(pieces)):
                    low_4 = jnp.where(lane == 0, right[p - 1] if p > 0 else pieces[0], right[p])
                    high_4 = jnp.where(lane == LANES - 1, left[p + 1] if p + 1 < len(pieces) else pieces[p], left[p])
                    parts.append(upwind(adv_up[here, :], adv_down[here, :], high_4 - low_4) - damp_4 * (low_4 + high_4))
                total = total + jnp.concatenate(parts, axis=1)

                if low_j is None:
                    low_2 = jnp.where(vx_first == 1, w, ins[low_at][t, here, :])
                else:
                    low_2 = readers[t](low_j, g)
                if high_j is None:
                    high_2 = jnp.where(vx_last == 1, w, ins[high_at][t, here, :])
                else:
                    high_2 = readers[t](high_j, g)
                slope = high_2 - low_2
                bent = control_2 * slope
                total = total + jnp.maximum((drift_up - bent) * slope, (drift_down - bent) * slope)

                low_3 = jnp.where(sublane == 0, ups[g], ups[g + 1])
                high_3 = jnp.where(sublane == 7, downs[g + 1], downs[g])
                slope = high_3 - low_3
                bent = control_3 * slope
                total = total + jnp.maximum((acc_up[here, :] - bent) * slope, (acc_down[here, :] - bent) * slope)

                twice = w + w
                bend_2 = low_2 + high_2 - twice
                bend_3 = low_3 + high_3 - twice
                if heun:
                    total = total + 0.5 * base_readers[i](j, g)
                if full:
                    total = total - damp_2 * bend_2 - damp_3 * bend_3
                    outs[i][j, here, :] = total
                else:
                    outs[3 * i][j, here, :] = total
                    outs[3 * i + 1][j, here, :] = bend_2
                    outs[3 * i + 2][j, here, :] = bend_3

        for i in range(count):
            tile(i, 0, None, 1)

        @pl.loop(1, cells_v - 1)
        def _(j):
            for i in range(count):
                tile(i, j, j - 1, j + 1)

        for i in range(count):
            tile(i, cells_v - 1, cells_v - 2, None)

    return pl.pallas_call(
        body,
        out_shape=[f32(cells_v, half, width)] * n_out,
        in_specs=[scalars()] * 3 + [whole()] * n_in,
        out_specs=[whole()] * n_out,
        scratch_shapes=[pltpu.VMEM((half, LANES), jnp.float32)] * 2 + [pltpu.VMEM((half, width), jnp.float32)] * 2,
        compiler_params=compiler_params(),
        cost_estimate=estimate(count * cells_v * half * width, 45),
        name="advance_" + "".join(str(t) for t in targets),
    )(flags, push, speed, *ops.arrays)


def settle(sizes, targets, updates, costs, flags, damping=None, fields=None, prior=None, with_edges=True):
    cells_v, half, width, total_vx, total_vy = sizes
    count = len(targets)
    ops = Operands()
    update_at = [[ops.add(a) for a in u] for u in updates]
    cost_at = [ops.add(c.array) for c in costs]
    field_at = [ops.add(f.array) for f in fields] if fields is not None else []
    maxima_at = [ops.add(m) for m in damping[:3]] if damping is not None else []
    before_targets, before_outs = prior if prior is not None else ((), ())
    prior_at = [ops.add(a) for a in before_outs]
    n_in = len(ops.arrays)
    every = sorted(tuple(before_targets) + tuple(targets))
    groups = half // 8

    def body(flags_ref, *refs):
        ins, outs = refs[:n_in], refs[n_in:]
        fields_out = outs[:count]
        parity = flags_ref[0]
        is_even = parity == 0
        if damping is not None:
            known = Scalars(sizes)
            step_rates = known.rates(ins[maxima_at[0]], ins[maxima_at[1]])
            rates = step_rates if maxima_at[1] == maxima_at[2] else known.rates(ins[maxima_at[0]], ins[maxima_at[2]])
            scale = known.time_step(step_rates) * damping[3]
            if fields is None:
                damp_2, damp_3 = scale * 0.5 * rates[0], scale * 0.5 * rates[1]
            else:
                damp_2, damp_3 = 0.5 * rates[0], 0.5 * rates[1]
        cost_readers = [c.reader(ins[a], parity, half) for c, a in zip(costs, cost_at)]
        field_readers = [f.reader(ins[a], parity, half) for f, a in zip(fields or (), field_at)]
        sublane = lax.broadcasted_iota(jnp.int32, (8, width), 0)

        def tile(i, j):
            out = []
            for g in range(groups):
                here = pl.ds(8 * g, 8)
                total = ins[update_at[i][0]][j, here, :]
                if damping is not None:
                    total = total - damp_2 * ins[update_at[i][1]][j, here, :] - damp_3 * ins[update_at[i][2]][j, here, :]
                    if fields is not None:
                        total = field_readers[i](j, g) + scale * total
                y = jnp.maximum(cost_readers[i](j, g), total)
                fields_out[i][j, here, :] = y
                out.append(y)
            return out

        if not with_edges:
            least_ref = outs[count]
            for i in range(count):

                def step(j, least, i=i):
                    return functools.reduce(jnp.minimum, tile(i, j), least)

                least = lax.fori_loop(0, cells_v, step, jnp.full((8, width), jnp.inf, jnp.float32))
                least_ref[pl.ds(i, 1), :] = jnp.min(least, axis=0, keepdims=True)
            return

        first_ref, second_ref, before_ref, last_ref, edge_ref, inner_ref, part_ref = outs[count : count + 7]
        send_at = jnp.where(is_even, half - 1, 0)
        inner_at = jnp.where(is_even, half - 2, 1)
        wall_at = jnp.where(is_even, 0, half - 1)
        next_at = jnp.where(is_even, 1, half - 2)
        for position, t in enumerate(sorted(before_targets)):
            slot = every.index(t)
            for ref, at in zip((first_ref, second_ref, before_ref, last_ref, edge_ref, inner_ref), prior_at):
                ref[slot] = ins[at][position]

        def one(i, j, most_3):
            slot = every.index(targets[i])
            out = tile(i, j)
            edge_ref[slot, pl.ds(j, 1), :] = fields_out[i][j, pl.ds(send_at, 1), :]
            inner_ref[slot, pl.ds(j, 1), :] = fields_out[i][j, pl.ds(inner_at, 1), :]
            wall = jnp.abs(fields_out[i][j, pl.ds(next_at, 1), :] - fields_out[i][j, pl.ds(wall_at, 1), :])
            most_3 = jnp.maximum(most_3, wall)
            rolled = [pltpu.roll(y, 2, 0) for y in out]
            for g in range(groups):
                apart = jnp.where(sublane < 2, rolled[g - 1] if g > 0 else out[0], rolled[g])
                most_3 = jnp.maximum(most_3, jnp.abs(out[g] - apart))
            return out, most_3

        most_2 = jnp.zeros((8, width), jnp.float32)
        most_3 = most_2
        if prior is not None:
            most_2, most_3 = ins[prior_at[6]][0], ins[prior_at[6]][1]
        for i in range(count):
            for j in (0, 1):
                _, most_3 = one(i, j, most_3)

            def step(j, carry, i=i):
                most_2, most_3 = carry
                out, most_3 = one(i, j, most_3)
                for g in range(groups):
                    most_2 = jnp.maximum(most_2, jnp.abs(out[g] - fields_out[i][j - 2, pl.ds(8 * g, 8), :]))
                return most_2, most_3

            most_2, most_3 = lax.fori_loop(2, cells_v, step, (most_2, most_3))
            slot = every.index(targets[i])
            first_ref[slot] = fields_out[i][0]
            second_ref[slot] = fields_out[i][1]
            before_ref[slot] = fields_out[i][cells_v - 2]
            last_ref[slot] = fields_out[i][cells_v - 1]
        part_ref[0] = most_2
        part_ref[1] = most_3

    n = len(every)
    shapes = [f32(cells_v, half, width)] * count
    if with_edges:
        shapes += [f32(n, half, width)] * 4 + [f32(n, cells_v, width)] * 2 + [f32(2, 8, width)]
    else:
        shapes.append(f32(count, width))
    outs = pl.pallas_call(
        body,
        out_shape=shapes,
        in_specs=[scalars()] + [whole()] * n_in,
        out_specs=[whole()] * len(shapes),
        compiler_params=compiler_params(),
        cost_estimate=estimate(count * cells_v * half * width, 15),
        name="settle_" + "".join(str(t) for t in targets),
    )(flags, *ops.arrays)
    return outs[:count], outs[count:]


def spread(shape, lanes):
    position = lax.broadcasted_iota(jnp.int32, shape, 1)
    out = jnp.zeros(shape, jnp.float32)
    for lane, value in enumerate(lanes):
        out = jnp.where(position == lane, value, out)
    return out


def first_maxima(value, vx_low, vx_high, accel_first, accel_second, flags):
    rows, cells_v, total_vy, width = value.shape

    def body(flags_ref, v_ref, low_ref, high_ref, first_ref, second_ref, out_ref):
        vx_first, vx_last = flags_ref[3], flags_ref[4]
        vy_row = lax.broadcasted_iota(jnp.int32, (total_vy, width), 0)

        def of_vy(x):
            inner = jnp.where(vy_row >= 2, jnp.abs(x - pltpu.roll(x, 2, 0)), 0.0)
            wall = jnp.maximum(jnp.abs(x[1:2] - x[0:1]), jnp.abs(x[total_vy - 1 : total_vy] - x[total_vy - 2 : total_vy - 1]))
            return jnp.maximum(fold(inner), wall)

        most_2 = jnp.zeros((8, width), jnp.float32)
        most_3 = jnp.zeros((8, width), jnp.float32)
        for r in range(rows):
            x = v_ref[r, 0]
            most_3 = jnp.maximum(most_3, of_vy(x))
            most_2 = jnp.maximum(most_2, fold(jnp.abs(v_ref[r, 1] - jnp.where(vx_first == 1, x, low_ref[r]))))
            x = v_ref[r, cells_v - 1]
            most_3 = jnp.maximum(most_3, of_vy(x))
            most_2 = jnp.maximum(most_2, fold(jnp.abs(v_ref[r, cells_v - 2] - jnp.where(vx_last == 1, x, high_ref[r]))))

            def step(j, carry, r=r):
                most_2, most_3 = carry
                most_3 = jnp.maximum(most_3, of_vy(v_ref[r, j]))
                most_2 = jnp.maximum(most_2, fold(jnp.abs(v_ref[r, j + 1] - v_ref[r, j - 1])))
                return most_2, most_3

            most_2, most_3 = lax.fori_loop(1, cells_v - 1, step, (most_2, most_3))
        values = (jnp.max(most_2), jnp.max(most_3), jnp.max(jnp.abs(first_ref[...])), jnp.max(jnp.abs(second_ref[...])))
        out_ref[...] = spread((8, LANES), values)

    return pl.pallas_call(
        body,
        out_shape=f32(8, LANES),
        in_specs=[scalars()] + [whole()] * 5,
        out_specs=whole(),
        compiler_params=compiler_params(),
        name="first_maxima",
    )(flags, value, vx_low, vx_high, accel_first, accel_second)


def edge_maxima(edges, vx_low, vx_high, vy_next, flags):
    first, second, before, last, _, inner, part = edges

    def body(flags_ref, first_ref, second_ref, before_ref, last_ref, low_ref, high_ref, inner_ref, next_ref, part_ref, out_ref):
        vx_first, vx_last = flags_ref[3], flags_ref[4]
        most_2, most_3 = part_ref[0], part_ref[1]
        for t in range(4):
            low = jnp.where(vx_first == 1, first_ref[t], low_ref[t])
            high = jnp.where(vx_last == 1, last_ref[t], high_ref[t])
            most_2 = jnp.maximum(most_2, fold(jnp.abs(second_ref[t] - low)))
            most_2 = jnp.maximum(most_2, fold(jnp.abs(high - before_ref[t])))
            most_3 = jnp.maximum(most_3, fold(jnp.abs(inner_ref[t] - next_ref[3 - t])))
        out_ref[...] = spread((8, LANES), (jnp.max(most_2), jnp.max(most_3)))

    return pl.pallas_call(
        body,
        out_shape=f32(8, LANES),
        in_specs=[scalars()] + [whole()] * 9,
        out_specs=whole(),
        compiler_params=compiler_params(),
        name="edge_maxima",
    )(flags, first, second, before, last, vx_low, vx_high, inner, vy_next, part)


def place(flags, pieces, which, result, shape):
    rows, cells_v, total_vy, width = shape
    half = total_vy // 2
    block = 8 if cells_v % 8 == 0 else cells_v
    count = len(pieces)

    def body(flags_ref, *refs):
        out_ref = refs[-1]
        piece = pl.program_id(0)
        for i in range(count):

            @pl.when(piece == i)
            def _(i=i):
                out_ref[0] = refs[i][...]

    def target(i, j, flags_ref):
        outer = functools.reduce(lambda a, b: a + b, [(i == k) * int(p[0]) for k, p in enumerate(pieces)])
        parity = flags_ref[0]
        return (jnp.where(outer == 1, parity, 1 - parity), j, parity if which == 0 else 1 - parity, 0)

    def source(k):
        return lambda i, j, flags_ref: (jnp.where(i == k, j, jnp.where(i < k, 0, cells_v // block - 1)), 0, 0)

    in_specs = [pl.BlockSpec((block, half, width), source(k)) for k in range(count)]
    extra = []
    if result is not None:
        in_specs.append(pl.BlockSpec(memory_space=pl.ANY))
        extra = [result]
    return pl.pallas_call(
        body,
        grid_spec=pltpu.PrefetchScalarGridSpec(
            num_scalar_prefetch=1,
            grid=(count, cells_v // block),
            in_specs=in_specs,
            out_specs=pl.BlockSpec((1, block, half, width), target),
        ),
        out_shape=jax.ShapeDtypeStruct(shape, jnp.float32),
        input_output_aliases={1 + count: 0} if result is not None else {},
        compiler_params=compiler_params(),
        name="place",
    )(flags, *[p[1] for p in pieces], *extra)


def per_device(value, cost, accel_first, accel_second):
    n_px, n_vx = lax.axis_size("px"), lax.axis_size("vx")
    rows, cells_v, total_vy, width = value.shape
    half = total_vy // 2
    total_vx = cells_v * n_vx
    sizes = (cells_v, half, width, total_vx, total_vy)
    px, vx = lax.axis_index("px"), lax.axis_index("vx")
    parity = px % 2
    flags = jnp.stack(
        [
            parity,
            ((px == 0) | (px == n_px - 1)).astype(jnp.int32),
            ((px == 1) | (px == n_px - 2)).astype(jnp.int32),
            (vx == 0).astype(jnp.int32),
            (vx == n_vx - 1).astype(jnp.int32),
        ]
    ).astype(jnp.int32)

    def partner(x):
        return lax.ppermute(x, "px", [(i, i ^ 1) for i in range(n_px)])

    def from_low_vx(x):
        return lax.ppermute(x, "vx", [(i, i + 1) for i in range(n_vx - 1)])

    def from_high_vx(x):
        return lax.ppermute(x, "vx", [(i + 1, i) for i in range(n_vx - 1)])

    def halo_before(outermost):
        moves = [(i, i + 2) for i in range(0, n_px - 2, 2)] + [(i, i - 2) for i in range(3, n_px, 2)]
        return lax.ppermute(outermost, "px", moves)

    def halo_after(outer):
        moves = [(i, i - 2) for i in range(2, n_px, 2)] + [(i, i + 2) for i in range(1, n_px - 2, 2)]
        return lax.ppermute(outer, "px", moves)

    def share(maxima):
        for axis, count in (("vx", n_vx), ("px", n_px)):
            apart = 1
            while apart < count:
                other = lax.ppermute(maxima, axis, [(i, i ^ apart) for i in range(count)])
                maxima = jnp.maximum(maxima, other)
                apart *= 2
        return maxima

    def half_of(array, row, which):
        return lax.dynamic_slice(array, (row, 0, which * half, 0), (1, cells_v, half, width))[0]

    value_outer_got = partner(half_of(value, parity, 1 - parity))
    value_inner_got = partner(half_of(value, 1 - parity, 1 - parity))
    cost_outer, value_outer_got = lax.optimization_barrier((half_of(cost, parity, 1 - parity), value_outer_got))
    cost_inner, value_inner_got = lax.optimization_barrier((half_of(cost, 1 - parity, 1 - parity), value_inner_got))
    cost_outer_got = partner(cost_outer)
    cost_inner_got = partner(cost_inner)

    low_own = from_low_vx(value[:, cells_v - 1])
    high_own = from_high_vx(value[:, 0])
    shared_first = share(first_maxima(value, low_own, high_own, accel_first, accel_second, flags))

    def chain_halo(own):
        given = lax.dynamic_slice(own, (0, (1 - parity) * half, 0), (rows, half, width))
        mine = lax.dynamic_slice(own, (0, parity * half, 0), (rows, half, width))
        return mine, given

    low_mine, low_given = chain_halo(low_own)
    high_mine, high_given = chain_halo(high_own)
    got = partner(jnp.concatenate([low_given, high_given], axis=0))
    row_given = lax.dynamic_slice(value, (0, 0, half - parity, 0), (rows, cells_v, 1, width))[:, :, 0]
    row_needed = lax.dynamic_slice(value, (0, 0, half - parity, 0), (rows, cells_v, 1, width))[:, :, 0]
    row_given = lax.dynamic_slice(value, (0, 0, half - 1 + parity, 0), (rows, cells_v, 1, width))[:, :, 0]
    row_got = partner(row_given)
    push_got = partner(accel_first)

    def pick(x, which):
        return lax.dynamic_index_in_dim(x, which, 0, keepdims=True)

    def in_chain(mine, others):
        return jnp.concatenate([pick(mine, parity), pick(mine, 1 - parity), pick(others, parity), pick(others, 1 - parity)], axis=0)

    vx_low = in_chain(low_mine, got[:rows])
    vx_high = in_chain(high_mine, got[rows:])
    vy_next = jnp.concatenate([pick(row_got, 1 - parity), pick(row_got, parity), pick(row_needed, 1 - parity), pick(row_needed, parity)], axis=0)
    push = in_chain(accel_first, push_got)
    positions = (vx * cells_v + jnp.arange(cells_v, dtype=jnp.int32)).astype(jnp.float32)
    speed = (2.0 * positions + 1.0 - total_vx) * (VELOCITY_LIMIT / total_vx)
    speed = jnp.where(parity == 0, speed, -speed)

    chain = [Own(value, True), Own(value, False), Row(value_inner_got), Row(value_outer_got)]
    costs = [Own(cost, True), Own(cost, False), Row(cost_inner_got), Row(cost_outer_got)]
    halo_rows = (halo_before(value_outer_got), halo_after(half_of(value, parity, parity)))

    def advanced(field, bases, stepper):
        out = {}
        for targets in ((1, 2), (0, 3)):
            some = None if bases is None else [bases[t] for t in targets]
            got = advance(
                sizes, targets, field, some, halo_rows, vx_low, vx_high, vy_next, shared_first, stepper, accel_second, flags, push, speed
            )
            each = len(got) // 2
            out.update({t: got[each * i : each * (i + 1)] for i, t in enumerate(targets)})
        return out

    def settled(targets, updates, **kw):
        return settle(sizes, targets, [updates[t] for t in targets], [costs[t] for t in targets], flags, **kw)

    def exchange(edges):
        first, _, _, last, edge, _, _ = edges
        low, high, row = from_low_vx(last), from_high_vx(first), partner(edge)
        return low, high, row, share(edge_maxima(edges, low, high, row, flags))

    every = (0, 1, 2, 3)

    updates = advanced(chain, None, shared_first)
    (outer, inner), edges = settled((0, 1), updates)
    after = halo_after(outer)
    (far,), edges = settled((3,), updates, prior=((0, 1), edges))
    before = halo_before(far)
    (near,), edges = settled((2,), updates, prior=((0, 1, 3), edges))
    halo_rows = (before, after)
    middle = [Row(f) for f in (outer, inner, near, far)]
    vx_low, vx_high, vy_next, shared = exchange(edges)

    updates = advanced(middle, chain, shared_first)
    fields, edges = settled(every, updates, damping=(shared_first, shared_first, shared, 0.5))
    halo_rows = (halo_before(fields[3]), halo_after(fields[0]))
    chain = [Row(f) for f in fields]
    vx_low, vx_high, vy_next, shared_second = exchange(edges)

    updates = advanced(chain, None, None)
    fields, edges = settled(every, updates, damping=(shared_first, shared_second, shared_second, 1.0), fields=chain)
    halo_rows = (halo_before(fields[3]), halo_after(fields[0]))
    middle = [Row(f) for f in fields]
    vx_low, vx_high, vy_next, shared = exchange(edges)

    updates = advanced(middle, chain, shared_second)
    damping = (shared_first, shared_second, shared, 0.5)
    (inner, near), (least_inner,) = settled((1, 2), updates, damping=damping, with_edges=False)
    inner_got = partner(near)
    (outer, far), (least_outer,) = settled((0, 3), updates, damping=damping, with_edges=False)
    outer_got = partner(far)
    least = lax.pmin(jnp.concatenate([least_outer, least_inner], axis=0), "vx")
    least_got = partner(least[1::2][::-1])
    final = place(flags, [(True, outer), (False, inner)], 0, None, value.shape)
    final = place(flags, [(False, inner_got)], 1, final, value.shape)
    final = place(flags, [(True, outer_got)], 1, final, value.shape)
    funnel = jnp.minimum(least[0::2], least_got[::-1])
    return final, jnp.concatenate([pick(funnel, parity), pick(funnel, 1 - parity)], axis=0)


def solution(mesh):
    placed = (P("px", "vx", None, None), P("px", "vx", None, None), P("px", "vx"), P())
    return jax.shard_map(
        per_device,
        mesh=mesh,
        in_specs=placed,
        out_specs=(P("px", "vx", None, None), P("px", None)),
        check_vma=False,
    )
```

```python
import functools

import jax
import jax.numpy as jnp
from jax import lax
from jax.experimental import pallas as pl
from jax.experimental.pallas import tpu as pltpu
from jax.sharding import PartitionSpec as P

VELOCITY_LIMIT = 1.0
PLANNER_SPEED = 0.3
DISTURBANCE = 0.2
CONTROL_COST = 1.0
COURANT = 0.5

LANES = 128


def compiler_params():
    return pltpu.CompilerParams(vmem_limit_bytes=8 * 1024 * 1024)


def whole():
    return pl.BlockSpec(memory_space=pltpu.VMEM)


def scalars():
    return pl.BlockSpec(memory_space=pltpu.SMEM)


def fold(tile):
    rows = tile.shape[0]
    out = tile[0:8]
    for start in range(8, rows, 8):
        out = jnp.maximum(out, tile[start : start + 8])
    return out


def fold_min(tile):
    rows = tile.shape[0]
    out = tile[0:8]
    for start in range(8, rows, 8):
        out = jnp.minimum(out, tile[start : start + 8])
    return out


def maximum_row(ref, row):
    return jnp.broadcast_to(ref[pl.ds(row, 1), :], (8, LANES))


class Own:
    def __init__(self, array, outer):
        self.array, self.outer = array, outer

    def reader(self, ref, parity, half):
        row = parity if self.outer else 1 - parity
        start = pl.multiple_of(parity * half, half)
        return lambda j, g: ref[row, j, pl.ds(pl.multiple_of(start + 8 * g, 8), 8), :]


class Row:
    def __init__(self, array):
        self.array = array

    def reader(self, ref, parity, half):
        return lambda j, g: ref[j, pl.ds(8 * g, 8), :]


class Rates:
    def __init__(self, sizes):
        cells_v, half, width, total_vx, total_vy = sizes
        self.step_2 = 2.0 * VELOCITY_LIMIT / total_vx
        self.step_3 = 2.0 * VELOCITY_LIMIT / total_vy
        self.step_1 = self.step_2 * self.step_3
        self.rate_1 = VELOCITY_LIMIT * (total_vx - 1) / total_vx + PLANNER_SPEED
        self.rate_4 = VELOCITY_LIMIT * (total_vy - 1) / total_vy + PLANNER_SPEED

    def rates(self, limits, maxima):
        rate_2 = maximum_row(limits, 2) + DISTURBANCE + maximum_row(maxima, 0) * (0.5 / (self.step_2 * CONTROL_COST))
        rate_3 = maximum_row(limits, 3) + DISTURBANCE + maximum_row(maxima, 1) * (0.5 / (self.step_3 * CONTROL_COST))
        return rate_2 * (1.0 / self.step_2), rate_3 * (1.0 / self.step_3)

    def time_step(self, rates):
        total = rates[0] + rates[1] + (self.rate_1 + self.rate_4) / self.step_1
        return COURANT / total


class Operands:
    def __init__(self):
        self.arrays = []

    def add(self, array):
        for position, known in enumerate(self.arrays):
            if known is array:
                return position
        self.arrays.append(array)
        return len(self.arrays) - 1


def f32(*shape):
    return jax.ShapeDtypeStruct(shape, jnp.float32)


def estimate(cells, flops):
    return pl.CostEstimate(flops=flops * cells, bytes_accessed=4 * cells, transcendentals=0)


def slabs(tile):
    return [tile[start : start + 8] for start in range(0, tile.shape[0], 8)]


def advance(sizes, targets, rows, bases, halo_rows, vx_low, vx_high, vy_next, maxima, stepper, accel_second, table):
    cells_v, half, width, total_vx, total_vy = sizes
    count = len(targets)
    heun = bases is not None
    late = stepper is None
    full = not heun and not late
    ops = Operands()
    needed = sorted({k for t in targets for k in (t - 1, t, t + 1) if 0 <= k <= 3})
    row_at = {k: ops.add(rows[k].array) for k in needed}
    halo_at = {k: ops.add(halo_rows[i]) for i, k in enumerate((-1, 4)) if any(abs(t - k) == 1 for t in targets)}
    base_at = [ops.add(b.array) for b in bases] if heun else []
    low_at, high_at, vy_at, accel_at = ops.add(vx_low), ops.add(vx_high), ops.add(vy_next), ops.add(accel_second)
    maxima_at = [] if late else [ops.add(maxima), ops.add(stepper)]
    n_in = len(ops.arrays)
    n_out = count * (1 if full else 3)
    groups = half // 8

    def body(table_ref, *refs):
        ins, outs = refs[:n_in], refs[n_in : n_in + n_out]
        adv_up, adv_down, acc_up, acc_down = refs[n_in + n_out :]
        is_odd, edge_low, edge_high, vx_first, vx_last = (table_ref[5, i] > 0.5 for i in range(5))
        is_even = jnp.logical_not(is_odd)
        parity = jnp.where(is_odd, 1, 0)
        known = Rates(sizes)
        step_1, step_2, step_3 = known.step_1, known.step_2, known.step_3
        if late:
            scale = jnp.ones((8, LANES), jnp.float32)
        else:
            rates = known.rates(ins[maxima_at[0]], ins[maxima_at[1]])
            scale = known.time_step(rates) * (0.5 if heun else 1.0)
        damp_1 = scale * (0.5 * known.rate_1 / step_1)
        damp_4 = scale * (0.5 * known.rate_4 / step_1)
        keep = 2.0 * (damp_1 + damp_4)
        if not late:
            keep = keep + (0.5 if heun else 1.0)
        if full:
            damp_2, damp_3 = scale * 0.5 * rates[0], scale * 0.5 * rates[1]
        planner = scale * (PLANNER_SPEED / (2.0 * step_1))
        disturb_2 = scale * (DISTURBANCE / (2.0 * step_2))
        disturb_3 = scale * (DISTURBANCE / (2.0 * step_3))
        control_2 = scale * (1.0 / (8.0 * CONTROL_COST * step_2 * step_2))
        control_3 = scale * (1.0 / (8.0 * CONTROL_COST * step_3 * step_3))
        to_1, to_2, to_3 = scale / (2.0 * step_1), scale / (2.0 * step_2), scale / (2.0 * step_3)

        def wide(x):
            return jnp.concatenate([x] * (width // LANES), axis=1)

        start = pl.multiple_of(parity * half, half)
        for g in range(groups):
            here = pl.ds(8 * g, 8)
            vy = (parity * half + 8 * g + lax.broadcasted_iota(jnp.int32, (8, LANES), 0)).astype(jnp.float32)
            speed_y = (2.0 * vy + (1.0 - total_vy)) * (VELOCITY_LIMIT / total_vy) * to_1
            adv_up[here, :] = speed_y + planner
            adv_down[here, :] = speed_y - planner
            accel = ins[accel_at][pl.ds(pl.multiple_of(start + 8 * g, 8), 8), :] * wide(to_3)
            acc_up[here, :] = accel + wide(disturb_3)
            acc_down[here, :] = accel - wide(disturb_3)
        keep, damp_1, control_2, control_3 = wide(keep), wide(damp_1), wide(control_2), wide(control_3)
        if full:
            damp_2, damp_3 = wide(damp_2), wide(damp_3)

        readers = {k: rows[k].reader(ins[row_at[k]], parity, half) for k in needed}
        base_readers = [b.reader(ins[a], parity, half) for b, a in zip(bases, base_at)] if heun else None
        sublane = lax.broadcasted_iota(jnp.int32, (8, width), 0)
        lane = lax.broadcasted_iota(jnp.int32, (8, LANES), 1)

        def neighbour(k, j, g, center):
            if k == -1:
                return jnp.where(edge_low, center, ins[halo_at[-1]][j, pl.ds(8 * g, 8), :])
            if k == 4:
                return jnp.where(edge_high, center, ins[halo_at[4]][j, pl.ds(8 * g, 8), :])
            return readers[k](j, g)

        def lane_pieces(x):
            return [x[:, start : start + LANES] for start in range(0, width, LANES)]

        def upwind(up, down, slope):
            return jnp.maximum(up * slope, down * slope)

        def tile(i, j, low_j, high_j):
            t = targets[i]
            flow = table_ref[4, j] * to_1
            drift = table_ref[t, j] * to_2
            flow_up, flow_down = wide(flow + planner), wide(flow - planner)
            drift_up, drift_down = wide(drift + disturb_2), wide(drift - disturb_2)
            beyond = ins[vy_at][3 - t, pl.ds(j, 1), :]
            first = readers[t](j, 0)
            last = readers[t](j, groups - 1)
            below = jnp.broadcast_to(jnp.where(is_even, first[0:1], beyond), (8, width))
            above = jnp.broadcast_to(jnp.where(is_even, beyond, last[7:8]), (8, width))
            ups = [below] + [pltpu.roll(readers[t](j, g), 1, 0) for g in range(groups)]
            downs = [pltpu.roll(readers[t](j, g), 7, 0) for g in range(groups)] + [above]
            for g in range(groups):
                w = readers[t](j, g)
                here = pl.ds(8 * g, 8)
                low_1, high_1 = neighbour(t - 1, j, g, w), neighbour(t + 1, j, g, w)
                total = keep * w - damp_1 * (low_1 + high_1)
                total = total + upwind(flow_up, flow_down, high_1 - low_1)

                pieces = lane_pieces(w)
                right = [pltpu.roll(p, 1, 1) for p in pieces]
                left = [pltpu.roll(p, LANES - 1, 1) for p in pieces]
                parts = []
                for p in range(len(pieces)):
                    low_4 = jnp.where(lane == 0, right[p - 1] if p > 0 else pieces[0], right[p])
                    high_4 = jnp.where(lane == LANES - 1, left[p + 1] if p + 1 < len(pieces) else pieces[p], left[p])
                    parts.append(upwind(adv_up[here, :], adv_down[here, :], high_4 - low_4) - damp_4 * (low_4 + high_4))
                total = total + jnp.concatenate(parts, axis=1)

                if low_j is None:
                    low_2 = jnp.where(vx_first, w, ins[low_at][t, here, :])
                else:
                    low_2 = readers[t](low_j, g)
                if high_j is None:
                    high_2 = jnp.where(vx_last, w, ins[high_at][t, here, :])
                else:
                    high_2 = readers[t](high_j, g)
                slope = high_2 - low_2
                bent = control_2 * slope
                total = total + (jnp.where(slope > 0.0, drift_up, drift_down) - bent) * slope

                low_3 = jnp.where(sublane == 0, ups[g], ups[g + 1])
                high_3 = jnp.where(sublane == 7, downs[g + 1], downs[g])
                slope = high_3 - low_3
                bent = control_3 * slope
                total = total + (jnp.where(slope > 0.0, acc_up[here, :], acc_down[here, :]) - bent) * slope

                twice = w + w
                bend_2 = low_2 + high_2 - twice
                bend_3 = low_3 + high_3 - twice
                if heun:
                    total = total + 0.5 * base_readers[i](j, g)
                if full:
                    total = total - damp_2 * bend_2 - damp_3 * bend_3
                    outs[i][j, here, :] = total
                else:
                    outs[3 * i][j, here, :] = total
                    outs[3 * i + 1][j, here, :] = bend_2
                    outs[3 * i + 2][j, here, :] = bend_3

        for i in range(count):
            tile(i, 0, None, 1)

        together = 2 if count == 1 and cells_v % 2 == 0 else 1

        @pl.loop(1, cells_v - 1, step=together)
        def _(j):
            for ahead in range(together):
                for i in range(count):
                    tile(i, j + ahead, j + ahead - 1, j + ahead + 1)

        for i in range(count):
            tile(i, cells_v - 1, cells_v - 2, None)

    return pl.pallas_call(
        body,
        out_shape=[f32(cells_v, half, width)] * n_out,
        in_specs=[scalars()] + [whole()] * n_in,
        out_specs=[whole()] * n_out,
        scratch_shapes=[pltpu.VMEM((half, LANES), jnp.float32)] * 2 + [pltpu.VMEM((half, width), jnp.float32)] * 2,
        compiler_params=compiler_params(),
        cost_estimate=estimate(count * cells_v * half * width, 45),
        name="advance_" + "".join(str(t) for t in targets),
    )(table, *ops.arrays)


def settle(sizes, targets, updates, costs, flags, damping=None, fields=None, prior=None, with_edges=True):
    cells_v, half, width, total_vx, total_vy = sizes
    count = len(targets)
    ops = Operands()
    update_at = [[ops.add(a) for a in u] for u in updates]
    cost_at = [ops.add(c.array) for c in costs]
    field_at = [ops.add(f.array) for f in fields] if fields is not None else []
    maxima_at = [ops.add(m) for m in damping[:3]] if damping is not None else []
    before_targets, before_outs = prior if prior is not None else ((), ())
    prior_at = [ops.add(a) for a in before_outs]
    n_in = len(ops.arrays)
    every = sorted(tuple(before_targets) + tuple(targets))
    groups = half // 8

    def body(flags_ref, *refs):
        ins, outs = refs[:n_in], refs[n_in:]
        fields_out = outs[:count]
        parity = flags_ref[0]
        is_even = parity == 0
        if damping is not None:
            known = Rates(sizes)
            step_rates = known.rates(ins[maxima_at[0]], ins[maxima_at[1]])
            rates = step_rates if maxima_at[1] == maxima_at[2] else known.rates(ins[maxima_at[0]], ins[maxima_at[2]])
            scale = known.time_step(step_rates) * damping[3]
            if fields is None:
                damp_2, damp_3 = scale * 0.5 * rates[0], scale * 0.5 * rates[1]
            else:
                damp_2, damp_3 = 0.5 * rates[0], 0.5 * rates[1]
            damp_2, damp_3, scale = (jnp.concatenate([x] * (width // LANES), axis=1) for x in (damp_2, damp_3, scale))
        cost_readers = [c.reader(ins[a], parity, half) for c, a in zip(costs, cost_at)]
        field_readers = [f.reader(ins[a], parity, half) for f, a in zip(fields or (), field_at)]
        sublane = lax.broadcasted_iota(jnp.int32, (8, width), 0)

        def tile(i, j):
            out = []
            for g in range(groups):
                here = pl.ds(8 * g, 8)
                total = ins[update_at[i][0]][j, here, :]
                if damping is not None:
                    total = total - damp_2 * ins[update_at[i][1]][j, here, :] - damp_3 * ins[update_at[i][2]][j, here, :]
                    if fields is not None:
                        total = field_readers[i](j, g) + scale * total
                y = jnp.maximum(cost_readers[i](j, g), total)
                fields_out[i][j, here, :] = y
                out.append(y)
            return out

        if not with_edges:
            least_ref = outs[count]
            for i in range(count):

                def step(j, least, i=i):
                    return functools.reduce(jnp.minimum, tile(i, j), least)

                least = lax.fori_loop(0, cells_v, step, jnp.full((8, width), jnp.inf, jnp.float32))
                least_ref[pl.ds(i, 1), :] = jnp.min(least, axis=0, keepdims=True)
            return

        first_ref, second_ref, before_ref, last_ref, edge_ref, inner_ref, part_ref = outs[count : count + 7]
        send_at = jnp.where(is_even, half - 1, 0)
        inner_at = jnp.where(is_even, half - 2, 1)
        wall_at = jnp.where(is_even, 0, half - 1)
        next_at = jnp.where(is_even, 1, half - 2)
        for position, t in enumerate(sorted(before_targets)):
            slot = every.index(t)
            for ref, at in zip((first_ref, second_ref, before_ref, last_ref, edge_ref, inner_ref), prior_at):
                ref[slot] = ins[at][position]

        def one(i, j, most_3):
            slot = every.index(targets[i])
            out = tile(i, j)
            edge_ref[slot, pl.ds(j, 1), :] = fields_out[i][j, pl.ds(send_at, 1), :]
            inner_ref[slot, pl.ds(j, 1), :] = fields_out[i][j, pl.ds(inner_at, 1), :]
            wall = jnp.abs(fields_out[i][j, pl.ds(next_at, 1), :] - fields_out[i][j, pl.ds(wall_at, 1), :])
            most_3 = jnp.maximum(most_3, wall)
            rolled = [pltpu.roll(y, 2, 0) for y in out]
            for g in range(groups):
                apart = jnp.where(sublane < 2, rolled[g - 1] if g > 0 else out[0], rolled[g])
                most_3 = jnp.maximum(most_3, jnp.abs(out[g] - apart))
            return out, most_3

        most_2 = jnp.zeros((8, width), jnp.float32)
        most_3 = most_2
        if prior is not None:
            most_2, most_3 = ins[prior_at[6]][0], ins[prior_at[6]][1]
        for i in range(count):
            for j in (0, 1):
                _, most_3 = one(i, j, most_3)

            def step(j, carry, i=i):
                most_2, most_3 = carry
                out, most_3 = one(i, j, most_3)
                for g in range(groups):
                    most_2 = jnp.maximum(most_2, jnp.abs(out[g] - fields_out[i][j - 2, pl.ds(8 * g, 8), :]))
                return most_2, most_3

            most_2, most_3 = lax.fori_loop(2, cells_v, step, (most_2, most_3))
            slot = every.index(targets[i])
            first_ref[slot] = fields_out[i][0]
            second_ref[slot] = fields_out[i][1]
            before_ref[slot] = fields_out[i][cells_v - 2]
            last_ref[slot] = fields_out[i][cells_v - 1]
        part_ref[0] = most_2
        part_ref[1] = most_3

    n = len(every)
    shapes = [f32(cells_v, half, width)] * count
    if with_edges:
        shapes += [f32(n, half, width)] * 4 + [f32(n, cells_v, width)] * 2 + [f32(2, 8, width)]
    else:
        shapes.append(f32(count, width))
    outs = pl.pallas_call(
        body,
        out_shape=shapes,
        in_specs=[scalars()] + [whole()] * n_in,
        out_specs=[whole()] * len(shapes),
        compiler_params=compiler_params(),
        cost_estimate=estimate(count * cells_v * half * width, 15),
        name="settle_" + "".join(str(t) for t in targets),
    )(flags, *ops.arrays)
    return outs[:count], outs[count:]


def spread(values):
    position = lax.broadcasted_iota(jnp.int32, (8, LANES), 0)
    out = jnp.zeros((8, LANES), jnp.float32)
    for row, value in enumerate(values):
        out = jnp.where(position == row, value, out)
    return out


def first_maxima(value, vx_low, vx_high, accel_first, accel_second, flags):
    rows, cells_v, total_vy, width = value.shape

    def body(flags_ref, v_ref, low_ref, high_ref, first_ref, second_ref, out_ref):
        vx_first, vx_last = flags_ref[3], flags_ref[4]
        vy_row = lax.broadcasted_iota(jnp.int32, (total_vy, width), 0)

        def of_vy(x):
            inner = jnp.where(vy_row >= 2, jnp.abs(x - pltpu.roll(x, 2, 0)), 0.0)
            wall = jnp.maximum(jnp.abs(x[1:2] - x[0:1]), jnp.abs(x[total_vy - 1 : total_vy] - x[total_vy - 2 : total_vy - 1]))
            return jnp.maximum(fold(inner), wall)

        most_2 = jnp.zeros((8, width), jnp.float32)
        most_3 = jnp.zeros((8, width), jnp.float32)
        for r in range(rows):
            x = v_ref[r, 0]
            most_3 = jnp.maximum(most_3, of_vy(x))
            most_2 = jnp.maximum(most_2, fold(jnp.abs(v_ref[r, 1] - jnp.where(vx_first == 1, x, low_ref[r]))))
            x = v_ref[r, cells_v - 1]
            most_3 = jnp.maximum(most_3, of_vy(x))
            most_2 = jnp.maximum(most_2, fold(jnp.abs(v_ref[r, cells_v - 2] - jnp.where(vx_last == 1, x, high_ref[r]))))

            def step(j, carry, r=r):
                most_2, most_3 = carry
                most_3 = jnp.maximum(most_3, of_vy(v_ref[r, j]))
                most_2 = jnp.maximum(most_2, fold(jnp.abs(v_ref[r, j + 1] - v_ref[r, j - 1])))
                return most_2, most_3

            most_2, most_3 = lax.fori_loop(1, cells_v - 1, step, (most_2, most_3))
        values = (jnp.max(most_2), jnp.max(most_3), jnp.max(jnp.abs(first_ref[...])), jnp.max(jnp.abs(second_ref[...])))
        out_ref[...] = spread(values)

    return pl.pallas_call(
        body,
        out_shape=f32(8, LANES),
        in_specs=[scalars()] + [whole()] * 5,
        out_specs=whole(),
        compiler_params=compiler_params(),
        name="first_maxima",
    )(flags, value, vx_low, vx_high, accel_first, accel_second)


def edge_maxima(edges, vx_low, vx_high, vy_next, flags):
    first, second, before, last, _, inner, part = edges

    def body(flags_ref, first_ref, second_ref, before_ref, last_ref, low_ref, high_ref, inner_ref, next_ref, part_ref, out_ref):
        vx_first, vx_last = flags_ref[3], flags_ref[4]
        most_2, most_3 = part_ref[0], part_ref[1]
        for t in range(4):
            low = jnp.where(vx_first == 1, first_ref[t], low_ref[t])
            high = jnp.where(vx_last == 1, last_ref[t], high_ref[t])
            most_2 = jnp.maximum(most_2, fold(jnp.abs(second_ref[t] - low)))
            most_2 = jnp.maximum(most_2, fold(jnp.abs(high - before_ref[t])))
            most_3 = jnp.maximum(most_3, fold(jnp.abs(inner_ref[t] - next_ref[3 - t])))
        out_ref[...] = spread((jnp.max(most_2), jnp.max(most_3)))

    return pl.pallas_call(
        body,
        out_shape=f32(8, LANES),
        in_specs=[scalars()] + [whole()] * 9,
        out_specs=whole(),
        compiler_params=compiler_params(),
        name="edge_maxima",
    )(flags, first, second, before, last, vx_low, vx_high, inner, vy_next, part)


def take(flags, array, outer, which):
    _, cells_v, total_vy, width = array.shape
    half = total_vy // 2

    def body(flags_ref, array_ref, out_ref, sem):
        parity = flags_ref[0]
        start = pl.multiple_of((parity if which == 0 else 1 - parity) * half, half)
        copy = pltpu.make_async_copy(array_ref.at[parity if outer else 1 - parity, :, pl.ds(start, half), :], out_ref, sem)
        copy.start()
        copy.wait()

    return pl.pallas_call(
        body,
        in_specs=[scalars(), pl.BlockSpec(memory_space=pl.ANY)],
        out_specs=whole(),
        out_shape=f32(cells_v, half, width),
        scratch_shapes=[pltpu.SemaphoreType.DMA],
        compiler_params=compiler_params(),
        cost_estimate=estimate(cells_v * half * width, 1),
        name="take",
    )(flags, array)


def place(flags, pieces, which, result, shape):
    half = shape[2] // 2
    count = len(pieces)

    def body(flags_ref, *refs):
        out_ref, sems = refs[-2:]
        parity = flags_ref[0]
        start = pl.multiple_of((parity if which == 0 else 1 - parity) * half, half)
        copies = []
        for i in range(count):
            row = parity if pieces[i][0] else 1 - parity
            copies.append(pltpu.make_async_copy(refs[i], out_ref.at[row, :, pl.ds(start, half), :], sems.at[i]))
        for copy in copies:
            copy.start()
        for copy in copies:
            copy.wait()

    anywhere = pl.BlockSpec(memory_space=pl.ANY)
    extra = [] if result is None else [result]
    return pl.pallas_call(
        body,
        in_specs=[scalars()] + [whole()] * count + [anywhere] * len(extra),
        out_specs=anywhere,
        out_shape=jax.ShapeDtypeStruct(shape, jnp.float32),
        input_output_aliases={} if result is None else {1 + count: 0},
        scratch_shapes=[pltpu.SemaphoreType.DMA((count,))],
        compiler_params=compiler_params(),
        name="place",
    )(flags, *[p[1] for p in pieces], *extra)


def per_device(value, cost, accel_first, accel_second):
    n_px, n_vx = lax.axis_size("px"), lax.axis_size("vx")
    rows, cells_v, total_vy, width = value.shape
    half = total_vy // 2
    total_vx = cells_v * n_vx
    sizes = (cells_v, half, width, total_vx, total_vy)
    px, vx = lax.axis_index("px"), lax.axis_index("vx")
    parity = px % 2
    flags = jnp.stack(
        [
            parity,
            ((px == 0) | (px == n_px - 1)).astype(jnp.int32),
            ((px == 1) | (px == n_px - 2)).astype(jnp.int32),
            (vx == 0).astype(jnp.int32),
            (vx == n_vx - 1).astype(jnp.int32),
        ]
    ).astype(jnp.int32)

    def partner(x):
        return lax.ppermute(x, "px", [(i, i ^ 1) for i in range(n_px)])

    def from_low_vx(x):
        return lax.ppermute(x, "vx", [(i, i + 1) for i in range(n_vx - 1)])

    def from_high_vx(x):
        return lax.ppermute(x, "vx", [(i + 1, i) for i in range(n_vx - 1)])

    def halo_before(outermost):
        moves = [(i, i + 2) for i in range(0, n_px - 2, 2)] + [(i, i - 2) for i in range(3, n_px, 2)]
        return lax.ppermute(outermost, "px", moves)

    def halo_after(outer):
        moves = [(i, i - 2) for i in range(2, n_px, 2)] + [(i, i + 2) for i in range(1, n_px - 2, 2)]
        return lax.ppermute(outer, "px", moves)

    def after(array, *others):
        return lax.optimization_barrier((array, *others))[0]

    def share(maxima, beside=None, partner_done=False):
        steps = [("vx", 1 << k) for k in range((n_vx - 1).bit_length())] + [("px", 1 << k) for k in range((n_px - 1).bit_length())]
        if partner_done:
            steps.remove(("px", 1))
        for place_at, (axis, apart) in enumerate(steps):
            other = lax.ppermute(maxima, axis, [(i, i ^ apart) for i in range(lax.axis_size(axis))])
            if beside is not None and place_at in beside:
                other = after(other, *beside[place_at])
            maxima = jnp.maximum(maxima, other)
        return maxima

    value_outer = take(flags, value, True, 1)
    value_outer_got = partner(value_outer)
    value_inner = after(take(flags, value, False, 1), value_outer)
    value_inner_got = partner(value_inner)
    push_got = partner(after(accel_first, value_outer))

    low_own = from_low_vx(after(value[:, cells_v - 1], value_outer))
    high_own = from_high_vx(after(value[:, 0], value_outer))
    row_needed = lax.dynamic_slice(value, (0, 0, half - parity, 0), (rows, cells_v, 1, width))[:, :, 0]
    row_given = lax.dynamic_slice(value, (0, 0, half - 1 + parity, 0), (rows, cells_v, 1, width))[:, :, 0]
    row_got = partner(after(row_given, value_outer))

    def chain_halo(own):
        given = lax.dynamic_slice(own, (0, (1 - parity) * half, 0), (rows, half, width))
        mine = lax.dynamic_slice(own, (0, parity * half, 0), (rows, half, width))
        return mine, given

    low_mine, low_given = chain_halo(low_own)
    high_mine, high_given = chain_halo(high_own)
    halo_given = jnp.concatenate([low_given, high_given], axis=0)
    got = partner(halo_given)
    maxima = first_maxima(value, low_own, high_own, accel_first, accel_second, flags)
    maxima = jnp.maximum(maxima, partner(maxima))
    ahead = (maxima, got, row_got, push_got)
    cost_outer = after(take(flags, cost, True, 1), *ahead)
    cost_outer_got = partner(cost_outer)
    cost_inner_got = partner(after(take(flags, cost, False, 1), *ahead))
    shared_first = share(maxima, partner_done=True)

    def pick(x, which):
        return lax.dynamic_index_in_dim(x, which, 0, keepdims=True)

    def in_chain(mine, others):
        return jnp.concatenate([pick(mine, parity), pick(mine, 1 - parity), pick(others, parity), pick(others, 1 - parity)], axis=0)

    vx_low = in_chain(low_mine, got[:rows])
    vx_high = in_chain(high_mine, got[rows:])
    vy_next = jnp.concatenate([pick(row_got, 1 - parity), pick(row_got, parity), pick(row_needed, 1 - parity), pick(row_needed, parity)], axis=0)
    push = in_chain(accel_first, push_got)
    positions = (vx * cells_v + jnp.arange(cells_v, dtype=jnp.int32)).astype(jnp.float32)
    speed = (2.0 * positions + 1.0 - total_vx) * (VELOCITY_LIMIT / total_vx)
    speed = jnp.where(parity == 0, speed, -speed)
    table = jnp.concatenate([push, speed[None], jnp.pad(flags.astype(jnp.float32), (0, cells_v - flags.shape[0]))[None]], axis=0)

    chain = [Own(value, True), Own(value, False), Row(value_inner_got), Row(value_outer_got)]
    costs = [Own(cost, True), Own(cost, False), Row(cost_inner_got), Row(cost_outer_got)]
    halo_rows = (halo_before(value_outer_got), halo_after(after(take(flags, value, True, 0), value_inner)))

    def advanced(targets, field, bases, halo_rows, vx_low, vx_high, vy_next, stepper):
        some = None if bases is None else [bases[t] for t in targets]
        got = advance(
            sizes, targets, field, some, halo_rows, vx_low, vx_high, vy_next, shared_first, stepper, accel_second, table
        )
        each = len(got) // len(targets)
        return {t: got[each * i : each * (i + 1)] for i, t in enumerate(targets)}

    def settled(targets, updates, **kw):
        return settle(sizes, targets, [updates[t] for t in targets], [costs[t] for t in targets], flags, **kw)

    def next_updates(field, edges, bases, stepper, halo_rows, halo_early):
        first, _, _, last, edge, _, _ = edges
        low, high, row = from_low_vx(last), from_high_vx(first), partner(edge)
        maxima = edge_maxima(edges, low, high, row, flags)
        updates, beside = {}, {}
        for place_at, t in enumerate((1, 2, 0, 3) if halo_early else (1, 2)):
            updates.update(advanced((t,), field, bases, halo_rows, low, high, row, stepper))
            beside[place_at + 1] = updates[t]
        if not halo_early:
            updates.update(advanced((0, 3), field, bases, halo_rows, low, high, row, stepper))
            beside[4] = updates[0] + updates[3]
        maxima = share(maxima, beside)
        return updates, maxima

    def settled_all(updates, **kw):
        fields = kw.pop("fields", None)
        some = {} if fields is None else {"fields": [fields[0], fields[3]]}
        (outer, far), edges = settled((0, 3), updates, **some, **kw)
        halo_rows = (halo_before(far), halo_after(outer))
        some = {} if fields is None else {"fields": [fields[1], fields[2]]}
        (inner, near), edges = settled((1, 2), updates, prior=((0, 3), edges), **some, **kw)
        return [Row(f) for f in (outer, inner, near, far)], edges, halo_rows

    updates = advanced((1, 2), chain, None, halo_rows, vx_low, vx_high, vy_next, shared_first)
    updates.update(advanced((0, 3), chain, None, halo_rows, vx_low, vx_high, vy_next, shared_first))
    (outer, inner), edges = settled((0, 1), updates)
    beyond = halo_after(outer)
    (far,), edges = settled((3,), updates, prior=((0, 1), edges))
    halo_rows = (halo_before(far), beyond)
    (near,), edges = settled((2,), updates, prior=((0, 1, 3), edges))
    middle = [Row(f) for f in (outer, inner, near, far)]

    updates, shared = next_updates(middle, edges, chain, shared_first, halo_rows, True)
    chain, edges, halo_rows = settled_all(updates, damping=(shared_first, shared_first, shared, 0.5))

    updates, shared_second = next_updates(chain, edges, None, None, halo_rows, False)
    middle, edges, halo_rows = settled_all(updates, damping=(shared_first, shared_second, shared_second, 1.0), fields=chain)

    updates, shared = next_updates(middle, edges, chain, shared_second, halo_rows, False)
    damping = (shared_first, shared_second, shared, 0.5)
    (inner, near), (least_inner,) = settled((1, 2), updates, damping=damping, with_edges=False)
    inner_got = partner(near)
    (outer, far), (least_outer,) = settled((0, 3), updates, damping=damping, with_edges=False)
    outer_got = partner(far)
    least = lax.pmin(jnp.concatenate([least_outer, least_inner], axis=0), "vx")
    least_got = partner(after(least[1::2][::-1], far))
    final = place(flags, [(True, outer), (False, inner)], 0, None, value.shape)
    final = place(flags, [(False, inner_got)], 1, final, value.shape)
    final = place(flags, [(True, outer_got)], 1, final, value.shape)
    funnel = jnp.minimum(least[0::2], after(least_got, final)[::-1])
    return final, jnp.concatenate([pick(funnel, parity), pick(funnel, 1 - parity)], axis=0)


def solution(mesh):
    placed = (P("px", "vx", None, None), P("px", "vx", None, None), P("px", "vx"), P())
    return jax.shard_map(
        per_device,
        mesh=mesh,
        in_specs=placed,
        out_specs=(P("px", "vx", None, None), P("px", None)),
        check_vma=False,
    )
```

```python
import functools

import jax
import jax.numpy as jnp
from jax import lax
from jax.experimental import pallas as pl
from jax.experimental.pallas import tpu as pltpu
from jax.sharding import PartitionSpec as P

VELOCITY_LIMIT = 1.0
PLANNER_SPEED = 0.3
DISTURBANCE = 0.2
CONTROL_COST = 1.0
COURANT = 0.5

LANES = 128


def compiler_params():
    return pltpu.CompilerParams(vmem_limit_bytes=8 * 1024 * 1024)


def whole():
    return pl.BlockSpec(memory_space=pltpu.VMEM)


def scalars():
    return pl.BlockSpec(memory_space=pltpu.SMEM)


def fold(tile):
    rows = tile.shape[0]
    out = tile[0:8]
    for start in range(8, rows, 8):
        out = jnp.maximum(out, tile[start : start + 8])
    return out


def fold_min(tile):
    rows = tile.shape[0]
    out = tile[0:8]
    for start in range(8, rows, 8):
        out = jnp.minimum(out, tile[start : start + 8])
    return out


def maximum_row(ref, row):
    return jnp.broadcast_to(ref[pl.ds(row, 1), :], (8, LANES))


class Own:
    def __init__(self, array, outer):
        self.array, self.outer = array, outer

    def reader(self, ref, parity, half):
        row = parity if self.outer else 1 - parity
        start = pl.multiple_of(parity * half, half)
        return lambda j, g: ref[row, j, pl.ds(pl.multiple_of(start + 8 * g, 8), 8), :]


class Row:
    def __init__(self, array):
        self.array = array

    def reader(self, ref, parity, half):
        return lambda j, g: ref[j, pl.ds(8 * g, 8), :]


class Rates:
    def __init__(self, sizes):
        cells_v, half, width, total_vx, total_vy = sizes
        self.step_2 = 2.0 * VELOCITY_LIMIT / total_vx
        self.step_3 = 2.0 * VELOCITY_LIMIT / total_vy
        self.step_1 = self.step_2 * self.step_3
        self.rate_1 = VELOCITY_LIMIT * (total_vx - 1) / total_vx + PLANNER_SPEED
        self.rate_4 = VELOCITY_LIMIT * (total_vy - 1) / total_vy + PLANNER_SPEED

    def rates(self, limits, maxima):
        rate_2 = maximum_row(limits, 2) + DISTURBANCE + maximum_row(maxima, 0) * (0.5 / (self.step_2 * CONTROL_COST))
        rate_3 = maximum_row(limits, 3) + DISTURBANCE + maximum_row(maxima, 1) * (0.5 / (self.step_3 * CONTROL_COST))
        return rate_2 * (1.0 / self.step_2), rate_3 * (1.0 / self.step_3)

    def time_step(self, rates):
        total = rates[0] + rates[1] + (self.rate_1 + self.rate_4) / self.step_1
        return COURANT / total


class Operands:
    def __init__(self):
        self.arrays = []

    def add(self, array):
        for position, known in enumerate(self.arrays):
            if known is array:
                return position
        self.arrays.append(array)
        return len(self.arrays) - 1


def f32(*shape):
    return jax.ShapeDtypeStruct(shape, jnp.float32)


def estimate():
    return pl.CostEstimate(flops=0, bytes_accessed=0, transcendentals=0)


def advance(sizes, targets, rows, bases, halo_rows, vx_low, vx_high, vy_next, maxima, stepper, accel_second, table):
    cells_v, half, width, total_vx, total_vy = sizes
    count = len(targets)
    heun = bases is not None
    late = stepper is None
    full = not heun and not late
    ops = Operands()
    needed = sorted({k for t in targets for k in (t - 1, t, t + 1) if 0 <= k <= 3})
    row_at = {k: ops.add(rows[k].array) for k in needed}
    halo_at = {k: ops.add(halo_rows[i]) for i, k in enumerate((-1, 4)) if any(abs(t - k) == 1 for t in targets)}
    base_at = [ops.add(b.array) for b in bases] if heun else []
    low_at, high_at, vy_at, accel_at = ops.add(vx_low), ops.add(vx_high), ops.add(vy_next), ops.add(accel_second)
    maxima_at = [] if late else [ops.add(maxima), ops.add(stepper)]
    n_in = len(ops.arrays)
    n_out = count * (1 if full else 3)
    groups = half // 8

    def body(table_ref, *refs):
        ins, outs = refs[:n_in], refs[n_in : n_in + n_out]
        adv_up, adv_down, acc_up, acc_down = refs[n_in + n_out :]
        is_odd, edge_low, edge_high, vx_first, vx_last = (table_ref[5, i] > 0.5 for i in range(5))
        is_even = jnp.logical_not(is_odd)
        parity = jnp.where(is_odd, 1, 0)
        known = Rates(sizes)
        step_1, step_2, step_3 = known.step_1, known.step_2, known.step_3
        if late:
            scale = jnp.ones((8, LANES), jnp.float32)
        else:
            rates = known.rates(ins[maxima_at[0]], ins[maxima_at[1]])
            scale = known.time_step(rates) * (0.5 if heun else 1.0)
        damp_1 = scale * (0.5 * known.rate_1 / step_1)
        damp_4 = scale * (0.5 * known.rate_4 / step_1)
        keep = 2.0 * (damp_1 + damp_4)
        if not late:
            keep = keep + (0.5 if heun else 1.0)
        if full:
            damp_2, damp_3 = scale * 0.5 * rates[0], scale * 0.5 * rates[1]
        planner = scale * (PLANNER_SPEED / (2.0 * step_1))
        disturb_2 = scale * (DISTURBANCE / (2.0 * step_2))
        disturb_3 = scale * (DISTURBANCE / (2.0 * step_3))
        control_2 = scale * (1.0 / (8.0 * CONTROL_COST * step_2 * step_2))
        control_3 = scale * (1.0 / (8.0 * CONTROL_COST * step_3 * step_3))
        to_1, to_2, to_3 = scale / (2.0 * step_1), scale / (2.0 * step_2), scale / (2.0 * step_3)

        def wide(x):
            return jnp.concatenate([x] * (width // LANES), axis=1)

        start = pl.multiple_of(parity * half, half)
        for g in range(groups):
            here = pl.ds(8 * g, 8)
            vy = (parity * half + 8 * g + lax.broadcasted_iota(jnp.int32, (8, LANES), 0)).astype(jnp.float32)
            speed_y = (2.0 * vy + (1.0 - total_vy)) * (VELOCITY_LIMIT / total_vy) * to_1
            adv_up[here, :] = speed_y + planner
            adv_down[here, :] = speed_y - planner
            accel = ins[accel_at][pl.ds(pl.multiple_of(start + 8 * g, 8), 8), :] * wide(to_3)
            acc_up[here, :] = accel + wide(disturb_3)
            acc_down[here, :] = accel - wide(disturb_3)
        keep, damp_1, control_2, control_3 = wide(keep), wide(damp_1), wide(control_2), wide(control_3)
        if full:
            damp_2, damp_3 = wide(damp_2), wide(damp_3)

        readers = {k: rows[k].reader(ins[row_at[k]], parity, half) for k in needed}
        base_readers = [b.reader(ins[a], parity, half) for b, a in zip(bases, base_at)] if heun else None
        sublane = lax.broadcasted_iota(jnp.int32, (8, width), 0)
        lane = lax.broadcasted_iota(jnp.int32, (8, LANES), 1)

        def neighbour(k, j, g, center):
            if k == -1:
                return jnp.where(edge_low, center, ins[halo_at[-1]][j, pl.ds(8 * g, 8), :])
            if k == 4:
                return jnp.where(edge_high, center, ins[halo_at[4]][j, pl.ds(8 * g, 8), :])
            return readers[k](j, g)

        def lane_pieces(x):
            return [x[:, start : start + LANES] for start in range(0, width, LANES)]

        def upwind(up, down, slope):
            return jnp.maximum(up * slope, down * slope)

        def tile(i, j, low_j, high_j):
            t = targets[i]
            flow = table_ref[4, j] * to_1
            drift = table_ref[t, j] * to_2
            flow_up, flow_down = wide(flow + planner), wide(flow - planner)
            drift_up, drift_down = wide(drift + disturb_2), wide(drift - disturb_2)
            beyond = ins[vy_at][3 - t, pl.ds(j, 1), :]
            first = readers[t](j, 0)
            last = readers[t](j, groups - 1)
            below = jnp.broadcast_to(jnp.where(is_even, first[0:1], beyond), (8, width))
            above = jnp.broadcast_to(jnp.where(is_even, beyond, last[7:8]), (8, width))
            ups = [below] + [pltpu.roll(readers[t](j, g), 1, 0) for g in range(groups)]
            downs = [pltpu.roll(readers[t](j, g), 7, 0) for g in range(groups)] + [above]
            for g in range(groups):
                w = readers[t](j, g)
                here = pl.ds(8 * g, 8)
                low_1, high_1 = neighbour(t - 1, j, g, w), neighbour(t + 1, j, g, w)
                total = keep * w - damp_1 * (low_1 + high_1)
                total = total + upwind(flow_up, flow_down, high_1 - low_1)

                pieces = lane_pieces(w)
                right = [pltpu.roll(p, 1, 1) for p in pieces]
                left = [pltpu.roll(p, LANES - 1, 1) for p in pieces]
                parts = []
                for p in range(len(pieces)):
                    low_4 = jnp.where(lane == 0, right[p - 1] if p > 0 else pieces[0], right[p])
                    high_4 = jnp.where(lane == LANES - 1, left[p + 1] if p + 1 < len(pieces) else pieces[p], left[p])
                    parts.append(upwind(adv_up[here, :], adv_down[here, :], high_4 - low_4) - damp_4 * (low_4 + high_4))
                total = total + jnp.concatenate(parts, axis=1)

                if low_j is None:
                    low_2 = jnp.where(vx_first, w, ins[low_at][t, here, :])
                else:
                    low_2 = readers[t](low_j, g)
                if high_j is None:
                    high_2 = jnp.where(vx_last, w, ins[high_at][t, here, :])
                else:
                    high_2 = readers[t](high_j, g)
                slope = high_2 - low_2
                bent = control_2 * slope
                total = total + (jnp.where(slope > 0.0, drift_up, drift_down) - bent) * slope

                low_3 = jnp.where(sublane == 0, ups[g], ups[g + 1])
                high_3 = jnp.where(sublane == 7, downs[g + 1], downs[g])
                slope = high_3 - low_3
                bent = control_3 * slope
                total = total + (jnp.where(slope > 0.0, acc_up[here, :], acc_down[here, :]) - bent) * slope

                twice = w + w
                bend_2 = low_2 + high_2 - twice
                bend_3 = low_3 + high_3 - twice
                if heun:
                    total = total + 0.5 * base_readers[i](j, g)
                if full:
                    total = total - damp_2 * bend_2 - damp_3 * bend_3
                    outs[i][j, here, :] = total
                else:
                    outs[3 * i][j, here, :] = total
                    outs[3 * i + 1][j, here, :] = bend_2
                    outs[3 * i + 2][j, here, :] = bend_3

        for i in range(count):
            tile(i, 0, None, 1)

        together = 2 if count == 1 and cells_v % 2 == 0 else 1

        @pl.loop(1, cells_v - 1, step=together)
        def _(j):
            for ahead in range(together):
                for i in range(count):
                    tile(i, j + ahead, j + ahead - 1, j + ahead + 1)

        for i in range(count):
            tile(i, cells_v - 1, cells_v - 2, None)

    return pl.pallas_call(
        body,
        out_shape=[f32(cells_v, half, width)] * n_out,
        in_specs=[scalars()] + [whole()] * n_in,
        out_specs=[whole()] * n_out,
        scratch_shapes=[pltpu.VMEM((half, LANES), jnp.float32)] * 2 + [pltpu.VMEM((half, width), jnp.float32)] * 2,
        compiler_params=compiler_params(),
        cost_estimate=estimate(),
        name="advance_" + "".join(str(t) for t in targets),
    )(table, *ops.arrays)


def settle(sizes, targets, updates, costs, flags, damping=None, fields=None, prior=None, with_edges=True):
    cells_v, half, width, total_vx, total_vy = sizes
    count = len(targets)
    ops = Operands()
    update_at = [[ops.add(a) for a in u] for u in updates]
    cost_at = [ops.add(c.array) for c in costs]
    field_at = [ops.add(f.array) for f in fields] if fields is not None else []
    maxima_at = [ops.add(m) for m in damping[:3]] if damping is not None else []
    before_targets, before_outs = prior if prior is not None else ((), ())
    prior_at = [ops.add(a) for a in before_outs]
    n_in = len(ops.arrays)
    every = sorted(tuple(before_targets) + tuple(targets))
    groups = half // 8

    def body(flags_ref, *refs):
        ins, outs = refs[:n_in], refs[n_in:]
        fields_out = outs[:count]
        parity = flags_ref[0]
        is_even = parity == 0
        if damping is not None:
            known = Rates(sizes)
            step_rates = known.rates(ins[maxima_at[0]], ins[maxima_at[1]])
            rates = step_rates if maxima_at[1] == maxima_at[2] else known.rates(ins[maxima_at[0]], ins[maxima_at[2]])
            scale = known.time_step(step_rates) * damping[3]
            if fields is None:
                damp_2, damp_3 = scale * 0.5 * rates[0], scale * 0.5 * rates[1]
            else:
                damp_2, damp_3 = 0.5 * rates[0], 0.5 * rates[1]
            damp_2, damp_3, scale = (jnp.concatenate([x] * (width // LANES), axis=1) for x in (damp_2, damp_3, scale))
        cost_readers = [c.reader(ins[a], parity, half) for c, a in zip(costs, cost_at)]
        field_readers = [f.reader(ins[a], parity, half) for f, a in zip(fields or (), field_at)]
        sublane = lax.broadcasted_iota(jnp.int32, (8, width), 0)

        def tile(i, j):
            out = []
            for g in range(groups):
                here = pl.ds(8 * g, 8)
                total = ins[update_at[i][0]][j, here, :]
                if damping is not None:
                    total = total - damp_2 * ins[update_at[i][1]][j, here, :] - damp_3 * ins[update_at[i][2]][j, here, :]
                    if fields is not None:
                        total = field_readers[i](j, g) + scale * total
                y = jnp.maximum(cost_readers[i](j, g), total)
                fields_out[i][j, here, :] = y
                out.append(y)
            return out

        if not with_edges:
            least_ref = outs[count]
            for i in range(count):

                def step(j, least, i=i):
                    return functools.reduce(jnp.minimum, tile(i, j), least)

                least = lax.fori_loop(0, cells_v, step, jnp.full((8, width), jnp.inf, jnp.float32))
                least_ref[pl.ds(i, 1), :] = jnp.min(least, axis=0, keepdims=True)
            return

        first_ref, second_ref, before_ref, last_ref, edge_ref, inner_ref, part_ref = outs[count : count + 7]
        send_at = jnp.where(is_even, half - 1, 0)
        inner_at = jnp.where(is_even, half - 2, 1)
        wall_at = jnp.where(is_even, 0, half - 1)
        next_at = jnp.where(is_even, 1, half - 2)
        for position, t in enumerate(sorted(before_targets)):
            slot = every.index(t)
            for ref, at in zip((first_ref, second_ref, before_ref, last_ref, edge_ref, inner_ref), prior_at):
                ref[slot] = ins[at][position]

        def one(i, j, most_3):
            slot = every.index(targets[i])
            out = tile(i, j)
            edge_ref[slot, pl.ds(j, 1), :] = fields_out[i][j, pl.ds(send_at, 1), :]
            inner_ref[slot, pl.ds(j, 1), :] = fields_out[i][j, pl.ds(inner_at, 1), :]
            wall = jnp.abs(fields_out[i][j, pl.ds(next_at, 1), :] - fields_out[i][j, pl.ds(wall_at, 1), :])
            most_3 = jnp.maximum(most_3, wall)
            rolled = [pltpu.roll(y, 2, 0) for y in out]
            for g in range(groups):
                apart = jnp.where(sublane < 2, rolled[g - 1] if g > 0 else out[0], rolled[g])
                most_3 = jnp.maximum(most_3, jnp.abs(out[g] - apart))
            return out, most_3

        most_2 = jnp.zeros((8, width), jnp.float32)
        most_3 = most_2
        if prior is not None:
            most_2, most_3 = ins[prior_at[6]][0], ins[prior_at[6]][1]
        for i in range(count):
            for j in (0, 1):
                _, most_3 = one(i, j, most_3)

            def step(j, carry, i=i):
                most_2, most_3 = carry
                out, most_3 = one(i, j, most_3)
                for g in range(groups):
                    most_2 = jnp.maximum(most_2, jnp.abs(out[g] - fields_out[i][j - 2, pl.ds(8 * g, 8), :]))
                return most_2, most_3

            most_2, most_3 = lax.fori_loop(2, cells_v, step, (most_2, most_3))
            slot = every.index(targets[i])
            first_ref[slot] = fields_out[i][0]
            second_ref[slot] = fields_out[i][1]
            before_ref[slot] = fields_out[i][cells_v - 2]
            last_ref[slot] = fields_out[i][cells_v - 1]
        part_ref[0] = most_2
        part_ref[1] = most_3

    n = len(every)
    shapes = [f32(cells_v, half, width)] * count
    if with_edges:
        shapes += [f32(n, half, width)] * 4 + [f32(n, cells_v, width)] * 2 + [f32(2, 8, width)]
    else:
        shapes.append(f32(count, width))
    outs = pl.pallas_call(
        body,
        out_shape=shapes,
        in_specs=[scalars()] + [whole()] * n_in,
        out_specs=[whole()] * len(shapes),
        compiler_params=compiler_params(),
        cost_estimate=estimate(),
        name="settle_" + "".join(str(t) for t in targets),
    )(flags, *ops.arrays)
    return outs[:count], outs[count:]


def spread(values):
    position = lax.broadcasted_iota(jnp.int32, (8, LANES), 0)
    out = jnp.zeros((8, LANES), jnp.float32)
    for row, value in enumerate(values):
        out = jnp.where(position == row, value, out)
    return out


def first_maxima(value, vx_low, vx_high, accel_first, accel_second, flags):
    rows, cells_v, total_vy, width = value.shape

    def body(flags_ref, v_ref, low_ref, high_ref, first_ref, second_ref, out_ref):
        vx_first, vx_last = flags_ref[3], flags_ref[4]
        vy_row = lax.broadcasted_iota(jnp.int32, (total_vy, width), 0)

        def of_vy(x):
            inner = jnp.where(vy_row >= 2, jnp.abs(x - pltpu.roll(x, 2, 0)), 0.0)
            wall = jnp.maximum(jnp.abs(x[1:2] - x[0:1]), jnp.abs(x[total_vy - 1 : total_vy] - x[total_vy - 2 : total_vy - 1]))
            return jnp.maximum(fold(inner), wall)

        most_2 = jnp.zeros((8, width), jnp.float32)
        most_3 = jnp.zeros((8, width), jnp.float32)
        for r in range(rows):
            x = v_ref[r, 0]
            most_3 = jnp.maximum(most_3, of_vy(x))
            most_2 = jnp.maximum(most_2, fold(jnp.abs(v_ref[r, 1] - jnp.where(vx_first == 1, x, low_ref[r]))))
            x = v_ref[r, cells_v - 1]
            most_3 = jnp.maximum(most_3, of_vy(x))
            most_2 = jnp.maximum(most_2, fold(jnp.abs(v_ref[r, cells_v - 2] - jnp.where(vx_last == 1, x, high_ref[r]))))

            def step(j, carry, r=r):
                most_2, most_3 = carry
                most_3 = jnp.maximum(most_3, of_vy(v_ref[r, j]))
                most_2 = jnp.maximum(most_2, fold(jnp.abs(v_ref[r, j + 1] - v_ref[r, j - 1])))
                return most_2, most_3

            most_2, most_3 = lax.fori_loop(1, cells_v - 1, step, (most_2, most_3))
        values = (jnp.max(most_2), jnp.max(most_3), jnp.max(jnp.abs(first_ref[...])), jnp.max(jnp.abs(second_ref[...])))
        out_ref[...] = spread(values)

    return pl.pallas_call(
        body,
        out_shape=f32(8, LANES),
        in_specs=[scalars()] + [whole()] * 5,
        out_specs=whole(),
        compiler_params=compiler_params(),
        cost_estimate=estimate(),
        name="first_maxima",
    )(flags, value, vx_low, vx_high, accel_first, accel_second)


def edge_maxima(edges, vx_low, vx_high, vy_next, flags):
    first, second, before, last, _, inner, part = edges

    def body(flags_ref, first_ref, second_ref, before_ref, last_ref, low_ref, high_ref, inner_ref, next_ref, part_ref, out_ref):
        vx_first, vx_last = flags_ref[3], flags_ref[4]
        most_2, most_3 = part_ref[0], part_ref[1]
        for t in range(4):
            low = jnp.where(vx_first == 1, first_ref[t], low_ref[t])
            high = jnp.where(vx_last == 1, last_ref[t], high_ref[t])
            most_2 = jnp.maximum(most_2, fold(jnp.abs(second_ref[t] - low)))
            most_2 = jnp.maximum(most_2, fold(jnp.abs(high - before_ref[t])))
            most_3 = jnp.maximum(most_3, fold(jnp.abs(inner_ref[t] - next_ref[3 - t])))
        out_ref[...] = spread((jnp.max(most_2), jnp.max(most_3)))

    return pl.pallas_call(
        body,
        out_shape=f32(8, LANES),
        in_specs=[scalars()] + [whole()] * 9,
        out_specs=whole(),
        compiler_params=compiler_params(),
        cost_estimate=estimate(),
        name="edge_maxima",
    )(flags, first, second, before, last, vx_low, vx_high, inner, vy_next, part)


def copies(flags_ref, pieces, out_ref, sems, which):
    parity = flags_ref[0]
    half = out_ref.shape[2] // 2
    start = pl.multiple_of((parity if which == 0 else 1 - parity) * half, half)
    return [
        pltpu.make_async_copy(ref, out_ref.at[parity if outer else 1 - parity, :, pl.ds(start, half), :], sems.at[i])
        for i, (outer, ref) in enumerate(pieces)
    ]


def place(flags, pieces, result, shape, which=0):
    count = len(pieces)

    def body(flags_ref, *refs):
        moves = copies(flags_ref, [(pieces[i][0], refs[i]) for i in range(count)], refs[-2], refs[-1], which)
        for move in moves:
            move.start()
        for move in moves:
            move.wait()

    anywhere = pl.BlockSpec(memory_space=pl.ANY)
    extra = [] if result is None else [result]
    return pl.pallas_call(
        body,
        in_specs=[scalars()] + [whole()] * count + [anywhere] * len(extra),
        out_specs=anywhere,
        out_shape=f32(*shape),
        input_output_aliases={} if result is None else {1 + count: 0},
        scratch_shapes=[pltpu.SemaphoreType.DMA((count,))],
        compiler_params=compiler_params(),
        cost_estimate=estimate(),
        name="place",
    )(flags, *[p[1] for p in pieces], *extra)


def finish(flags, outer, least, least_got, result):
    def body(flags_ref, outer_ref, least_ref, got_ref, _, out_ref, funnel_ref, sems):
        parity = flags_ref[0]
        (move,) = copies(flags_ref, [(True, outer_ref)], out_ref, sems, 1)
        move.start()
        funnel_ref[pl.ds(parity, 1), :] = jnp.minimum(least_ref[0:1], got_ref[1:2])
        funnel_ref[pl.ds(1 - parity, 1), :] = jnp.minimum(least_ref[1:2], got_ref[0:1])
        move.wait()

    anywhere = pl.BlockSpec(memory_space=pl.ANY)
    return pl.pallas_call(
        body,
        in_specs=[scalars()] + [whole()] * 3 + [anywhere],
        out_specs=[anywhere, whole()],
        out_shape=[f32(*result.shape), f32(2, result.shape[3])],
        input_output_aliases={4: 0},
        scratch_shapes=[pltpu.SemaphoreType.DMA((1,))],
        compiler_params=compiler_params(),
        cost_estimate=estimate(),
        name="finish",
    )(flags, outer, least, least_got, result)


def per_device(value, cost, accel_first, accel_second):
    n_px, n_vx = lax.axis_size("px"), lax.axis_size("vx")
    rows, cells_v, total_vy, width = value.shape
    half = total_vy // 2
    total_vx = cells_v * n_vx
    sizes = (cells_v, half, width, total_vx, total_vy)
    px, vx = lax.axis_index("px"), lax.axis_index("vx")
    parity = px % 2
    flags = jnp.stack(
        [
            parity,
            ((px == 0) | (px == n_px - 1)).astype(jnp.int32),
            ((px == 1) | (px == n_px - 2)).astype(jnp.int32),
            (vx == 0).astype(jnp.int32),
            (vx == n_vx - 1).astype(jnp.int32),
        ]
    ).astype(jnp.int32)

    def partner(x):
        return lax.ppermute(x, "px", [(i, i ^ 1) for i in range(n_px)])

    def from_low_vx(x):
        return lax.ppermute(x, "vx", [(i, i + 1) for i in range(n_vx - 1)])

    def from_high_vx(x):
        return lax.ppermute(x, "vx", [(i + 1, i) for i in range(n_vx - 1)])

    def halo_before(outermost):
        moves = [(i, i + 2) for i in range(0, n_px - 2, 2)] + [(i, i - 2) for i in range(3, n_px, 2)]
        return lax.ppermute(outermost, "px", moves)

    def halo_after(outer):
        moves = [(i, i - 2) for i in range(2, n_px, 2)] + [(i, i + 2) for i in range(1, n_px - 2, 2)]
        return lax.ppermute(outer, "px", moves)

    def after(array, *others):
        return lax.optimization_barrier((array, *others))[0]

    def share(maxima, beside=None, partner_done=False):
        steps = [("vx", 1 << k) for k in range((n_vx - 1).bit_length())] + [("px", 1 << k) for k in range((n_px - 1).bit_length())]
        if partner_done:
            steps.remove(("px", 1))
        for place_at, (axis, apart) in enumerate(steps):
            other = lax.ppermute(maxima, axis, [(i, i ^ apart) for i in range(lax.axis_size(axis))])
            if beside is not None and place_at in beside:
                other = after(other, *beside[place_at])
            maxima = jnp.maximum(maxima, other)
        return maxima

    def half_of(array, row, which):
        return lax.dynamic_slice(array, (row, 0, which * half, 0), (1, cells_v, half, width))[0]

    value_outer = half_of(value, parity, 1 - parity)
    late = after(parity, value_outer)
    value_outer_got = partner(value_outer)
    push_got = partner(after(accel_first, value_outer))

    low_own = from_low_vx(after(value[:, cells_v - 1], value_outer))
    high_own = from_high_vx(after(value[:, 0], value_outer))
    row_needed = lax.dynamic_slice(value, (0, 0, half - parity, 0), (rows, cells_v, 1, width))[:, :, 0]
    row_given = lax.dynamic_slice(value, (0, 0, half - 1 + parity, 0), (rows, cells_v, 1, width))[:, :, 0]
    row_got = partner(after(row_given, value_outer))

    maxima = first_maxima(value, low_own, high_own, accel_first, accel_second, flags)
    maxima = jnp.maximum(maxima, partner(maxima))
    ahead = (maxima, row_got, push_got)
    value_inner_got = partner(after(half_of(value, 1 - late, 1 - late), *ahead))
    cost_outer_got = partner(after(half_of(cost, late, 1 - late), *ahead))
    cost_inner_got = partner(after(half_of(cost, 1 - late, 1 - late), *ahead))
    shared_first = share(maxima, partner_done=True)

    def pick(x, which):
        return lax.dynamic_index_in_dim(x, which, 0, keepdims=True)

    def in_chain(mine, others):
        return jnp.concatenate([pick(mine, parity), pick(mine, 1 - parity), pick(others, parity), pick(others, 1 - parity)], axis=0)

    def halo_chain(own, received):
        mine = lax.dynamic_slice(own, (0, parity * half, 0), (rows, half, width))
        return jnp.concatenate([pick(mine, parity), pick(mine, 1 - parity), received], axis=0)

    vx_low = halo_chain(low_own, from_low_vx(jnp.stack([value_inner_got[cells_v - 1], value_outer_got[cells_v - 1]])))
    vx_high = halo_chain(high_own, from_high_vx(jnp.stack([value_inner_got[0], value_outer_got[0]])))
    vy_next = jnp.concatenate([pick(row_got, 1 - parity), pick(row_got, parity), pick(row_needed, 1 - parity), pick(row_needed, parity)], axis=0)
    push = in_chain(accel_first, push_got)
    positions = (vx * cells_v + jnp.arange(cells_v, dtype=jnp.int32)).astype(jnp.float32)
    speed = (2.0 * positions + 1.0 - total_vx) * (VELOCITY_LIMIT / total_vx)
    speed = jnp.where(parity == 0, speed, -speed)
    table = jnp.concatenate([push, speed[None], jnp.pad(flags.astype(jnp.float32), (0, cells_v - flags.shape[0]))[None]], axis=0)

    chain = [Own(value, True), Own(value, False), Row(value_inner_got), Row(value_outer_got)]
    costs = [Own(cost, True), Own(cost, False), Row(cost_inner_got), Row(cost_outer_got)]
    halo_rows = (halo_before(value_outer_got), halo_after(half_of(value, late, late)))

    def advanced(targets, field, bases, halo_rows, vx_low, vx_high, vy_next, stepper):
        some = None if bases is None else [bases[t] for t in targets]
        got = advance(
            sizes, targets, field, some, halo_rows, vx_low, vx_high, vy_next, shared_first, stepper, accel_second, table
        )
        each = len(got) // len(targets)
        return {t: got[each * i : each * (i + 1)] for i, t in enumerate(targets)}

    def settled(targets, updates, **kw):
        return settle(sizes, targets, [updates[t] for t in targets], [costs[t] for t in targets], flags, **kw)

    def next_updates(field, edges, bases, stepper, halo_rows, halo_early):
        first, _, _, last, edge, _, _ = edges
        low, high, row = from_low_vx(last), from_high_vx(first), partner(edge)
        maxima = edge_maxima(edges, low, high, row, flags)
        updates, beside = {}, {}
        for place_at, t in enumerate((1, 2, 0, 3) if halo_early else (1, 2)):
            updates.update(advanced((t,), field, bases, halo_rows, low, high, row, stepper))
            beside[place_at + 1] = updates[t]
        if not halo_early:
            updates.update(advanced((0, 3), field, bases, halo_rows, low, high, row, stepper))
            beside[4] = updates[0] + updates[3]
        maxima = share(maxima, beside)
        return updates, maxima

    def settled_all(updates, **kw):
        fields = kw.pop("fields", None)
        some = {} if fields is None else {"fields": [fields[0], fields[3]]}
        (outer, far), edges = settled((0, 3), updates, **some, **kw)
        halo_rows = (halo_before(far), halo_after(outer))
        some = {} if fields is None else {"fields": [fields[1], fields[2]]}
        (inner, near), edges = settled((1, 2), updates, prior=((0, 3), edges), **some, **kw)
        return [Row(f) for f in (outer, inner, near, far)], edges, halo_rows

    updates = advanced((1, 2), chain, None, halo_rows, vx_low, vx_high, vy_next, shared_first)
    updates.update(advanced((0, 3), chain, None, halo_rows, vx_low, vx_high, vy_next, shared_first))
    (outer, inner), edges = settled((0, 1), updates)
    beyond = halo_after(outer)
    (far,), edges = settled((3,), updates, prior=((0, 1), edges))
    halo_rows = (halo_before(far), beyond)
    (near,), edges = settled((2,), updates, prior=((0, 1, 3), edges))
    middle = [Row(f) for f in (outer, inner, near, far)]

    updates, shared = next_updates(middle, edges, chain, shared_first, halo_rows, True)
    chain, edges, halo_rows = settled_all(updates, damping=(shared_first, shared_first, shared, 0.5))

    updates, shared_second = next_updates(chain, edges, None, None, halo_rows, False)
    middle, edges, halo_rows = settled_all(updates, damping=(shared_first, shared_second, shared_second, 1.0), fields=chain)

    updates, shared = next_updates(middle, edges, chain, shared_second, halo_rows, False)
    damping = (shared_first, shared_second, shared, 0.5)
    (near,), (least_near,) = settled((2,), updates, damping=damping, with_edges=False)
    inner_got = partner(near)
    (outer, inner, far), (least,) = settled((0, 1, 3), updates, damping=damping, with_edges=False)
    outer_got = partner(far)
    least = lax.pmin(jnp.concatenate([least[:2], least_near, least[2:]], axis=0), "vx")
    least_got = partner(after(least[2:], far))
    final = place(flags, [(True, outer), (False, inner)], None, value.shape)
    return finish(flags, outer_got, least, least_got, place(flags, [(False, inner_got)], final, value.shape, 1))


def solution(mesh):
    placed = (P("px", "vx", None, None), P("px", "vx", None, None), P("px", "vx"), P())
    return jax.shard_map(
        per_device,
        mesh=mesh,
        in_specs=placed,
        out_specs=(P("px", "vx", None, None), P("px", None)),
        check_vma=False,
    )
```

```python
import functools

import jax
import jax.numpy as jnp
from jax import lax
from jax.experimental import pallas as pl
from jax.experimental.pallas import tpu as pltpu
from jax.sharding import PartitionSpec as P

VELOCITY_LIMIT = 1.0
PLANNER_SPEED = 0.3
DISTURBANCE = 0.2
CONTROL_COST = 1.0
COURANT = 0.5

LANES = 128


def compiler_params():
    return pltpu.CompilerParams(vmem_limit_bytes=8 * 1024 * 1024)


def whole():
    return pl.BlockSpec(memory_space=pltpu.VMEM)


def scalars():
    return pl.BlockSpec(memory_space=pltpu.SMEM)


def fold(tile):
    rows = tile.shape[0]
    out = tile[0:8]
    for start in range(8, rows, 8):
        out = jnp.maximum(out, tile[start : start + 8])
    return out


def fold_min(tile):
    rows = tile.shape[0]
    out = tile[0:8]
    for start in range(8, rows, 8):
        out = jnp.minimum(out, tile[start : start + 8])
    return out


def maximum_row(ref, row):
    return jnp.broadcast_to(ref[pl.ds(row, 1), :], (8, LANES))


class Own:
    def __init__(self, array, outer):
        self.array, self.outer = array, outer

    def reader(self, ref, parity, half):
        row = parity if self.outer else 1 - parity
        start = pl.multiple_of(parity * half, half)
        return lambda j, g: ref[row, j, pl.ds(pl.multiple_of(start + 8 * g, 8), 8), :]


class Row:
    def __init__(self, array):
        self.array = array

    def reader(self, ref, parity, half):
        return lambda j, g: ref[j, pl.ds(8 * g, 8), :]


class Rates:
    def __init__(self, sizes):
        cells_v, half, width, total_vx, total_vy = sizes
        self.step_2 = 2.0 * VELOCITY_LIMIT / total_vx
        self.step_3 = 2.0 * VELOCITY_LIMIT / total_vy
        self.step_1 = self.step_2 * self.step_3
        self.rate_1 = VELOCITY_LIMIT * (total_vx - 1) / total_vx + PLANNER_SPEED
        self.rate_4 = VELOCITY_LIMIT * (total_vy - 1) / total_vy + PLANNER_SPEED

    def rates(self, limits, maxima):
        rate_2 = maximum_row(limits, 2) + DISTURBANCE + maximum_row(maxima, 0) * (0.5 / (self.step_2 * CONTROL_COST))
        rate_3 = maximum_row(limits, 3) + DISTURBANCE + maximum_row(maxima, 1) * (0.5 / (self.step_3 * CONTROL_COST))
        return rate_2 * (1.0 / self.step_2), rate_3 * (1.0 / self.step_3)

    def time_step(self, rates):
        total = rates[0] + rates[1] + (self.rate_1 + self.rate_4) / self.step_1
        return COURANT / total


class Operands:
    def __init__(self):
        self.arrays = []

    def add(self, array):
        for position, known in enumerate(self.arrays):
            if known is array:
                return position
        self.arrays.append(array)
        return len(self.arrays) - 1


def f32(*shape):
    return jax.ShapeDtypeStruct(shape, jnp.float32)


def estimate():
    return pl.CostEstimate(flops=0, bytes_accessed=0, transcendentals=0)


def advance(sizes, targets, rows, bases, halos, maxima, stepper, accel_second, table):
    cells_v, half, width, total_vx, total_vy = sizes
    count = len(targets)
    heun = bases is not None
    late = stepper is None
    full = halos is not None
    ops = Operands()
    needed = sorted({k for t in targets for k in (t - 1, t, t + 1) if 0 <= k <= 3})
    row_at = {k: ops.add(rows[k].array) for k in needed}
    base_at = [ops.add(b.array) for b in bases] if heun else []
    accel_at = ops.add(accel_second)
    if full:
        halo_rows, vx_low, vx_high, vy_next = halos
        halo_at = {k: ops.add(halo_rows[i]) for i, k in enumerate((-1, 4)) if any(abs(t - k) == 1 for t in targets)}
        low_at, high_at, vy_at = ops.add(vx_low), ops.add(vx_high), ops.add(vy_next)
    maxima_at = [] if late else [ops.add(maxima), ops.add(stepper)]
    n_in = len(ops.arrays)
    n_out = count * (1 if full else 3)
    groups = half // 8

    def body(table_ref, *refs):
        ins, outs = refs[:n_in], refs[n_in : n_in + n_out]
        adv_up, adv_down, acc_up, acc_down = refs[n_in + n_out :]
        is_odd, edge_low, edge_high, vx_first, vx_last = (table_ref[5, i] > 0.5 for i in range(5))
        is_even = jnp.logical_not(is_odd)
        parity = jnp.where(is_odd, 1, 0)
        known = Rates(sizes)
        step_1, step_2, step_3 = known.step_1, known.step_2, known.step_3
        if late:
            scale = jnp.ones((8, LANES), jnp.float32)
        else:
            rates = known.rates(ins[maxima_at[0]], ins[maxima_at[1]])
            scale = known.time_step(rates) * (0.5 if heun else 1.0)
        damp_1 = scale * (0.5 * known.rate_1 / step_1)
        damp_4 = scale * (0.5 * known.rate_4 / step_1)
        keep = 2.0 * (damp_1 + damp_4)
        if not late:
            keep = keep + (0.5 if heun else 1.0)
        if full:
            damp_2, damp_3 = scale * 0.5 * rates[0], scale * 0.5 * rates[1]
        planner = scale * (PLANNER_SPEED / (2.0 * step_1))
        disturb_2 = scale * (DISTURBANCE / (2.0 * step_2))
        disturb_3 = scale * (DISTURBANCE / (2.0 * step_3))
        control_2 = scale * (1.0 / (8.0 * CONTROL_COST * step_2 * step_2))
        control_3 = scale * (1.0 / (8.0 * CONTROL_COST * step_3 * step_3))
        to_1, to_2, to_3 = scale / (2.0 * step_1), scale / (2.0 * step_2), scale / (2.0 * step_3)

        def wide(x):
            return jnp.concatenate([x] * (width // LANES), axis=1)

        start = pl.multiple_of(parity * half, half)
        for g in range(groups):
            here = pl.ds(8 * g, 8)
            vy = (parity * half + 8 * g + lax.broadcasted_iota(jnp.int32, (8, LANES), 0)).astype(jnp.float32)
            speed_y = (2.0 * vy + (1.0 - total_vy)) * (VELOCITY_LIMIT / total_vy) * to_1
            adv_up[here, :] = speed_y + planner
            adv_down[here, :] = speed_y - planner
            accel = ins[accel_at][pl.ds(pl.multiple_of(start + 8 * g, 8), 8), :] * wide(to_3)
            acc_up[here, :] = accel + wide(disturb_3)
            acc_down[here, :] = accel - wide(disturb_3)
        keep_outer = wide(keep - 2.0 * damp_1)
        keep, damp_1, control_2, control_3 = wide(keep), wide(damp_1), wide(control_2), wide(control_3)
        if full:
            damp_2, damp_3 = wide(damp_2), wide(damp_3)

        readers = {k: rows[k].reader(ins[row_at[k]], parity, half) for k in needed}
        base_readers = [b.reader(ins[a], parity, half) for b, a in zip(bases, base_at)] if heun else None
        sublane = lax.broadcasted_iota(jnp.int32, (8, width), 0)
        lane = lax.broadcasted_iota(jnp.int32, (8, LANES), 1)

        def neighbour(k, j, g, center):
            if k == -1:
                return jnp.where(edge_low, center, ins[halo_at[-1]][j, pl.ds(8 * g, 8), :])
            if k == 4:
                return jnp.where(edge_high, center, ins[halo_at[4]][j, pl.ds(8 * g, 8), :])
            return readers[k](j, g)

        def lane_pieces(x):
            return [x[:, start : start + LANES] for start in range(0, width, LANES)]

        def upwind(up, down, slope):
            return jnp.maximum(up * slope, down * slope)

        def tile(i, j, low_j, high_j):
            t = targets[i]
            flow = table_ref[4, j] * to_1
            drift = table_ref[t, j] * to_2
            flow_up, flow_down = wide(flow + planner), wide(flow - planner)
            drift_up, drift_down = wide(drift + disturb_2), wide(drift - disturb_2)
            below = readers[t](j, 0)[0:1]
            above = readers[t](j, groups - 1)[7:8]
            if full:
                beyond = ins[vy_at][3 - t, pl.ds(j, 1), :]
                below, above = jnp.where(is_even, below, beyond), jnp.where(is_even, beyond, above)
            below, above = jnp.broadcast_to(below, (8, width)), jnp.broadcast_to(above, (8, width))
            ups = [below] + [pltpu.roll(readers[t](j, g), 1, 0) for g in range(groups)]
            downs = [pltpu.roll(readers[t](j, g), 7, 0) for g in range(groups)] + [above]
            for g in range(groups):
                w = readers[t](j, g)
                here = pl.ds(8 * g, 8)
                if full or t in (1, 2):
                    low_1, high_1 = neighbour(t - 1, j, g, w), neighbour(t + 1, j, g, w)
                    total = keep * w - damp_1 * (low_1 + high_1)
                    total = total + upwind(flow_up, flow_down, high_1 - low_1)
                else:
                    total = keep_outer * w

                pieces = lane_pieces(w)
                right = [pltpu.roll(p, 1, 1) for p in pieces]
                left = [pltpu.roll(p, LANES - 1, 1) for p in pieces]
                parts = []
                for p in range(len(pieces)):
                    low_4 = jnp.where(lane == 0, right[p - 1] if p > 0 else pieces[0], right[p])
                    high_4 = jnp.where(lane == LANES - 1, left[p + 1] if p + 1 < len(pieces) else pieces[p], left[p])
                    parts.append(upwind(adv_up[here, :], adv_down[here, :], high_4 - low_4) - damp_4 * (low_4 + high_4))
                total = total + jnp.concatenate(parts, axis=1)

                if low_j is None:
                    low_2 = jnp.where(vx_first, w, ins[low_at][t, here, :]) if full else w
                else:
                    low_2 = readers[t](low_j, g)
                if high_j is None:
                    high_2 = jnp.where(vx_last, w, ins[high_at][t, here, :]) if full else w
                else:
                    high_2 = readers[t](high_j, g)
                slope = high_2 - low_2
                bent = control_2 * slope
                total = total + (jnp.where(slope > 0.0, drift_up, drift_down) - bent) * slope

                low_3 = jnp.where(sublane == 0, ups[g], ups[g + 1])
                high_3 = jnp.where(sublane == 7, downs[g + 1], downs[g])
                slope = high_3 - low_3
                bent = control_3 * slope
                total = total + (jnp.where(slope > 0.0, acc_up[here, :], acc_down[here, :]) - bent) * slope

                twice = w + w
                bend_2 = low_2 + high_2 - twice
                bend_3 = low_3 + high_3 - twice
                if heun:
                    total = total + 0.5 * base_readers[i](j, g)
                if full:
                    total = total - damp_2 * bend_2 - damp_3 * bend_3
                    outs[i][j, here, :] = total
                else:
                    outs[3 * i][j, here, :] = total
                    outs[3 * i + 1][j, here, :] = bend_2
                    outs[3 * i + 2][j, here, :] = bend_3

        for i in range(count):
            tile(i, 0, None, 1)

        together = 2 if count == 1 and cells_v % 2 == 0 else 1

        @pl.loop(1, cells_v - 1, step=together)
        def _(j):
            for ahead in range(together):
                for i in range(count):
                    tile(i, j + ahead, j + ahead - 1, j + ahead + 1)

        for i in range(count):
            tile(i, cells_v - 1, cells_v - 2, None)

    return pl.pallas_call(
        body,
        out_shape=[f32(cells_v, half, width)] * n_out,
        in_specs=[scalars()] + [whole()] * n_in,
        out_specs=[whole()] * n_out,
        scratch_shapes=[pltpu.VMEM((half, LANES), jnp.float32)] * 2 + [pltpu.VMEM((half, width), jnp.float32)] * 2,
        compiler_params=compiler_params(),
        cost_estimate=estimate(),
        name="advance_" + "".join(str(t) for t in targets),
    )(table, *ops.arrays)


def outer_terms(sizes, rows, halo_rows, maxima, stepper, heun, table):
    cells_v, half, width, _, _ = sizes
    groups = half // 8
    late = stepper is None
    arrays = [r.array for r in rows] + list(halo_rows) + ([] if late else [maxima, stepper])

    def body(table_ref, *refs):
        row_refs, before_ref, after_ref, out_refs = refs[:4], refs[4], refs[5], refs[-2:]
        edge_low, edge_high = table_ref[5, 1] > 0.5, table_ref[5, 2] > 0.5
        known = Rates(sizes)
        if late:
            scale = jnp.ones((8, LANES), jnp.float32)
        else:
            scale = known.time_step(known.rates(refs[6], refs[7])) * (0.5 if heun else 1.0)

        def wide(x):
            return jnp.concatenate([x] * (width // LANES), axis=1)

        damp = wide(scale * (0.5 * known.rate_1 / known.step_1))
        planner = scale * (PLANNER_SPEED / (2.0 * known.step_1))
        to_1 = scale / (2.0 * known.step_1)

        @pl.loop(0, cells_v)
        def _(j):
            flow = table_ref[4, j] * to_1
            up, down = wide(flow + planner), wide(flow - planner)
            for g in range(groups):
                here = pl.ds(8 * g, 8)
                for i in range(2):
                    w = row_refs[3 * i][j, here, :]
                    inside = row_refs[1 + i][j, here, :]
                    if i == 0:
                        low, high = jnp.where(edge_low, w, before_ref[j, here, :]), inside
                    else:
                        low, high = inside, jnp.where(edge_high, w, after_ref[j, here, :])
                    slope = high - low
                    out_refs[i][j, here, :] = jnp.maximum(up * slope, down * slope) - damp * (low + high - (w + w))

    return pl.pallas_call(
        body,
        out_shape=[f32(cells_v, half, width)] * 2,
        in_specs=[scalars()] + [whole()] * len(arrays),
        out_specs=[whole()] * 2,
        compiler_params=compiler_params(),
        cost_estimate=estimate(),
        name="outer_terms",
    )(table, *arrays)


def mend(sizes, edges, vx_low, vx_high, vy_next, maxima, stepper, heun, accel_second, table):
    cells_v, half, width, _, _ = sizes
    late = stepper is None
    first, second, before, last, edge, inner, _ = edges
    arrays = [first, second, before, last, edge, inner, vx_low, vx_high, vy_next, accel_second] + ([] if late else [maxima, stepper])

    def body(table_ref, *refs):
        first_ref, second_ref, before_ref, last_ref, edge_ref, inner_ref, low_ref, high_ref, next_ref, accel_ref = refs[:10]
        update_2, bend_2, update_3, bend_3 = refs[-4:]
        is_odd, _, _, vx_first, vx_last = (table_ref[5, i] > 0.5 for i in range(5))
        is_even = jnp.logical_not(is_odd)
        known = Rates(sizes)
        if late:
            scale = jnp.ones((8, LANES), jnp.float32)
        else:
            scale = known.time_step(known.rates(refs[10], refs[11])) * (0.5 if heun else 1.0)

        def wide(x):
            return jnp.concatenate([x] * (width // LANES), axis=1)

        disturb_2 = scale * (DISTURBANCE / (2.0 * known.step_2))
        disturb_3 = wide(scale * (DISTURBANCE / (2.0 * known.step_3)))
        control_2 = wide(scale * (1.0 / (8.0 * CONTROL_COST * known.step_2 * known.step_2)))
        control_3 = wide(scale * (1.0 / (8.0 * CONTROL_COST * known.step_3 * known.step_3)))
        to_2, to_3 = scale / (2.0 * known.step_2), wide(scale / (2.0 * known.step_3))

        def term(up, down, control, slope):
            return (jnp.where(slope > 0.0, up, down) - control * slope) * slope

        for t in range(4):
            for e, j in ((0, 0), (1, cells_v - 1)):
                drift = table_ref[t, j] * to_2
                up, down = wide(drift + disturb_2), wide(drift - disturb_2)
                for start in range(0, half, 8):
                    here = pl.ds(start, 8)
                    if e == 0:
                        own, inside = first_ref[t, here, :], second_ref[t, here, :]
                        halo = jnp.where(vx_first, own, low_ref[t, here, :])
                        right, wrong = inside - halo, inside - own
                    else:
                        own, inside = last_ref[t, here, :], before_ref[t, here, :]
                        halo = jnp.where(vx_last, own, high_ref[t, here, :])
                        right, wrong = halo - inside, own - inside
                    update_2[t, e, here, :] = term(up, down, control_2, right) - term(up, down, control_2, wrong)
                    bend_2[t, e, here, :] = halo - own
        at = jnp.where(is_even, half - 1, half)
        accel = jnp.broadcast_to(accel_ref[pl.ds(at, 1), :], (8, width)) * to_3
        up, down = accel + disturb_3, accel - disturb_3
        for t in range(4):
            for start in range(0, cells_v, 8):
                here = pl.ds(start, 8)
                own, inside, halo = edge_ref[t, here, :], inner_ref[t, here, :], next_ref[3 - t, here, :]
                right = jnp.where(is_even, halo - inside, inside - halo)
                wrong = jnp.where(is_even, own - inside, inside - own)
                update_3[t, here, :] = term(up, down, control_3, right) - term(up, down, control_3, wrong)
                bend_3[t, here, :] = halo - own

    return pl.pallas_call(
        body,
        out_shape=[f32(4, 2, half, width)] * 2 + [f32(4, cells_v, width)] * 2,
        in_specs=[scalars()] + [whole()] * len(arrays),
        out_specs=[whole()] * 4,
        compiler_params=compiler_params(),
        cost_estimate=estimate(),
        name="mend",
    )(table, *arrays)


def settle(sizes, targets, updates, costs, flags, damping=None, fields=None, prior=None, with_edges=True, mended=None):
    cells_v, half, width, total_vx, total_vy = sizes
    count = len(targets)
    ops = Operands()
    update_at = [[ops.add(a) for a in u] for u in updates]
    cost_at = [ops.add(c.array) for c in costs]
    field_at = [ops.add(f.array) for f in fields] if fields is not None else []
    mended_at = [ops.add(m) for m in mended] if mended is not None else []
    maxima_at = [ops.add(m) for m in damping[:3]] if damping is not None else []
    before_targets, before_outs = prior if prior is not None else ((), ())
    prior_at = [ops.add(a) for a in before_outs]
    n_in = len(ops.arrays)
    every = sorted(tuple(before_targets) + tuple(targets))
    groups = half // 8

    def body(flags_ref, *refs):
        ins, outs = refs[:n_in], refs[n_in:]
        fields_out = outs[:count]
        parity = flags_ref[0]
        is_even = parity == 0
        if damping is not None:
            known = Rates(sizes)
            step_rates = known.rates(ins[maxima_at[0]], ins[maxima_at[1]])
            rates = step_rates if maxima_at[1] == maxima_at[2] else known.rates(ins[maxima_at[0]], ins[maxima_at[2]])
            scale = known.time_step(step_rates) * damping[3]
            if fields is None:
                damp_2, damp_3 = scale * 0.5 * rates[0], scale * 0.5 * rates[1]
            else:
                damp_2, damp_3 = 0.5 * rates[0], 0.5 * rates[1]
            damp_2, damp_3, scale = (jnp.concatenate([x] * (width // LANES), axis=1) for x in (damp_2, damp_3, scale))
        cost_readers = [c.reader(ins[a], parity, half) for c, a in zip(costs, cost_at)]
        field_readers = [f.reader(ins[a], parity, half) for f, a in zip(fields or (), field_at)]
        sublane = lax.broadcasted_iota(jnp.int32, (8, width), 0)

        row_low = jnp.where(is_even, -1, 0)
        row_high = jnp.where(is_even, 7, -1)

        def tile(i, j, end=None):
            t = targets[i]
            out = []
            if mended is not None:
                along_2, twice_2, along_3, twice_3 = (ins[a] for a in mended_at)
                here = pl.ds(j, 1)
                beside = jnp.broadcast_to(along_3[t, here, :] - damp_3[0:1] * twice_3[t, here, :], (8, width))
            for g in range(groups):
                here = pl.ds(8 * g, 8)
                total = ins[update_at[i][0]][j, here, :]
                if len(update_at[i]) > 3:
                    total = total + ins[update_at[i][3]][j, here, :]
                if damping is not None:
                    total = total - damp_2 * ins[update_at[i][1]][j, here, :] - damp_3 * ins[update_at[i][2]][j, here, :]
                if mended is not None:
                    if g == 0:
                        total = total + jnp.where(sublane == row_low, beside, 0.0)
                    if g == groups - 1:
                        total = total + jnp.where(sublane == row_high, beside, 0.0)
                    if end is not None:
                        total = total + along_2[t, end, here, :] - damp_2 * twice_2[t, end, here, :]
                if fields is not None:
                    total = field_readers[i](j, g) + scale * total
                y = jnp.maximum(cost_readers[i](j, g), total)
                fields_out[i][j, here, :] = y
                out.append(y)
            return out

        if not with_edges:
            least_ref = outs[count]
            for i in range(count):

                def step(j, least, i=i):
                    return functools.reduce(jnp.minimum, tile(i, j), least)

                least = functools.reduce(jnp.minimum, tile(i, 0, 0) + tile(i, cells_v - 1, 1))
                least = lax.fori_loop(1, cells_v - 1, step, least)
                least_ref[pl.ds(i, 1), :] = jnp.min(least, axis=0, keepdims=True)
            return

        first_ref, second_ref, before_ref, last_ref, edge_ref, inner_ref, part_ref = outs[count : count + 7]
        send_at = jnp.where(is_even, half - 1, 0)
        inner_at = jnp.where(is_even, half - 2, 1)
        wall_at = jnp.where(is_even, 0, half - 1)
        next_at = jnp.where(is_even, 1, half - 2)
        for position, t in enumerate(sorted(before_targets)):
            slot = every.index(t)
            for ref, at in zip((first_ref, second_ref, before_ref, last_ref, edge_ref, inner_ref), prior_at):
                ref[slot] = ins[at][position]

        def one(i, j, most_3, end=None):
            slot = every.index(targets[i])
            out = tile(i, j, end)
            edge_ref[slot, pl.ds(j, 1), :] = fields_out[i][j, pl.ds(send_at, 1), :]
            inner_ref[slot, pl.ds(j, 1), :] = fields_out[i][j, pl.ds(inner_at, 1), :]
            wall = jnp.abs(fields_out[i][j, pl.ds(next_at, 1), :] - fields_out[i][j, pl.ds(wall_at, 1), :])
            most_3 = jnp.maximum(most_3, wall)
            rolled = [pltpu.roll(y, 2, 0) for y in out]
            for g in range(groups):
                apart = jnp.where(sublane < 2, rolled[g - 1] if g > 0 else out[0], rolled[g])
                most_3 = jnp.maximum(most_3, jnp.abs(out[g] - apart))
            return out, most_3

        most_2 = jnp.zeros((8, width), jnp.float32)
        most_3 = most_2
        if prior is not None:
            most_2, most_3 = ins[prior_at[6]][0], ins[prior_at[6]][1]
        for i in range(count):
            _, most_3 = one(i, 0, most_3, 0)
            _, most_3 = one(i, 1, most_3)

            def step(j, carry, i=i, end=None):
                most_2, most_3 = carry
                out, most_3 = one(i, j, most_3, end)
                for g in range(groups):
                    most_2 = jnp.maximum(most_2, jnp.abs(out[g] - fields_out[i][j - 2, pl.ds(8 * g, 8), :]))
                return most_2, most_3

            most_2, most_3 = lax.fori_loop(2, cells_v - 1, step, (most_2, most_3))
            most_2, most_3 = step(cells_v - 1, (most_2, most_3), end=1)
            slot = every.index(targets[i])
            first_ref[slot] = fields_out[i][0]
            second_ref[slot] = fields_out[i][1]
            before_ref[slot] = fields_out[i][cells_v - 2]
            last_ref[slot] = fields_out[i][cells_v - 1]
        part_ref[0] = most_2
        part_ref[1] = most_3

    n = len(every)
    shapes = [f32(cells_v, half, width)] * count
    if with_edges:
        shapes += [f32(n, half, width)] * 4 + [f32(n, cells_v, width)] * 2 + [f32(2, 8, width)]
    else:
        shapes.append(f32(count, width))
    outs = pl.pallas_call(
        body,
        out_shape=shapes,
        in_specs=[scalars()] + [whole()] * n_in,
        out_specs=[whole()] * len(shapes),
        compiler_params=compiler_params(),
        cost_estimate=estimate(),
        name="settle_" + "".join(str(t) for t in targets),
    )(flags, *ops.arrays)
    return outs[:count], outs[count:]


def spread(values):
    position = lax.broadcasted_iota(jnp.int32, (8, LANES), 0)
    out = jnp.zeros((8, LANES), jnp.float32)
    for row, value in enumerate(values):
        out = jnp.where(position == row, value, out)
    return out


def first_maxima(value, vx_low, vx_high, accel_first, accel_second, flags):
    rows, cells_v, total_vy, width = value.shape

    def body(flags_ref, v_ref, low_ref, high_ref, first_ref, second_ref, out_ref):
        vx_first, vx_last = flags_ref[3], flags_ref[4]
        vy_row = lax.broadcasted_iota(jnp.int32, (total_vy, width), 0)

        def of_vy(x):
            inner = jnp.where(vy_row >= 2, jnp.abs(x - pltpu.roll(x, 2, 0)), 0.0)
            wall = jnp.maximum(jnp.abs(x[1:2] - x[0:1]), jnp.abs(x[total_vy - 1 : total_vy] - x[total_vy - 2 : total_vy - 1]))
            return jnp.maximum(fold(inner), wall)

        most_2 = jnp.zeros((8, width), jnp.float32)
        most_3 = jnp.zeros((8, width), jnp.float32)
        for r in range(rows):
            x = v_ref[r, 0]
            most_3 = jnp.maximum(most_3, of_vy(x))
            most_2 = jnp.maximum(most_2, fold(jnp.abs(v_ref[r, 1] - jnp.where(vx_first == 1, x, low_ref[r]))))
            x = v_ref[r, cells_v - 1]
            most_3 = jnp.maximum(most_3, of_vy(x))
            most_2 = jnp.maximum(most_2, fold(jnp.abs(v_ref[r, cells_v - 2] - jnp.where(vx_last == 1, x, high_ref[r]))))

            def step(j, carry, r=r):
                most_2, most_3 = carry
                most_3 = jnp.maximum(most_3, of_vy(v_ref[r, j]))
                most_2 = jnp.maximum(most_2, fold(jnp.abs(v_ref[r, j + 1] - v_ref[r, j - 1])))
                return most_2, most_3

            most_2, most_3 = lax.fori_loop(1, cells_v - 1, step, (most_2, most_3))
        values = (jnp.max(most_2), jnp.max(most_3), jnp.max(jnp.abs(first_ref[...])), jnp.max(jnp.abs(second_ref[...])))
        out_ref[...] = spread(values)

    return pl.pallas_call(
        body,
        out_shape=f32(8, LANES),
        in_specs=[scalars()] + [whole()] * 5,
        out_specs=whole(),
        compiler_params=compiler_params(),
        cost_estimate=estimate(),
        name="first_maxima",
    )(flags, value, vx_low, vx_high, accel_first, accel_second)


def edge_maxima(edges, vx_low, vx_high, vy_next, flags):
    first, second, before, last, _, inner, part = edges

    def body(flags_ref, first_ref, second_ref, before_ref, last_ref, low_ref, high_ref, inner_ref, next_ref, part_ref, out_ref):
        vx_first, vx_last = flags_ref[3], flags_ref[4]
        most_2, most_3 = part_ref[0], part_ref[1]
        for t in range(4):
            low = jnp.where(vx_first == 1, first_ref[t], low_ref[t])
            high = jnp.where(vx_last == 1, last_ref[t], high_ref[t])
            most_2 = jnp.maximum(most_2, fold(jnp.abs(second_ref[t] - low)))
            most_2 = jnp.maximum(most_2, fold(jnp.abs(high - before_ref[t])))
            most_3 = jnp.maximum(most_3, fold(jnp.abs(inner_ref[t] - next_ref[3 - t])))
        out_ref[...] = spread((jnp.max(most_2), jnp.max(most_3)))

    return pl.pallas_call(
        body,
        out_shape=f32(8, LANES),
        in_specs=[scalars()] + [whole()] * 9,
        out_specs=whole(),
        compiler_params=compiler_params(),
        cost_estimate=estimate(),
        name="edge_maxima",
    )(flags, first, second, before, last, vx_low, vx_high, inner, vy_next, part)


def copies(flags_ref, pieces, out_ref, sems, which):
    parity = flags_ref[0]
    half = out_ref.shape[2] // 2
    start = pl.multiple_of((parity if which == 0 else 1 - parity) * half, half)
    return [
        pltpu.make_async_copy(ref, out_ref.at[parity if outer else 1 - parity, :, pl.ds(start, half), :], sems.at[i])
        for i, (outer, ref) in enumerate(pieces)
    ]


def place(flags, pieces, result, shape, which=0):
    count = len(pieces)

    def body(flags_ref, *refs):
        moves = copies(flags_ref, [(pieces[i][0], refs[i]) for i in range(count)], refs[-2], refs[-1], which)
        for move in moves:
            move.start()
        for move in moves:
            move.wait()

    anywhere = pl.BlockSpec(memory_space=pl.ANY)
    extra = [] if result is None else [result]
    return pl.pallas_call(
        body,
        in_specs=[scalars()] + [whole()] * count + [anywhere] * len(extra),
        out_specs=anywhere,
        out_shape=f32(*shape),
        input_output_aliases={} if result is None else {1 + count: 0},
        scratch_shapes=[pltpu.SemaphoreType.DMA((count,))],
        compiler_params=compiler_params(),
        cost_estimate=estimate(),
        name="place",
    )(flags, *[p[1] for p in pieces], *extra)


def finish(flags, outer, least, least_got, result):
    def body(flags_ref, outer_ref, least_ref, got_ref, _, out_ref, funnel_ref, sems):
        parity = flags_ref[0]
        (move,) = copies(flags_ref, [(True, outer_ref)], out_ref, sems, 1)
        move.start()
        funnel_ref[pl.ds(parity, 1), :] = jnp.minimum(least_ref[0:1], got_ref[1:2])
        funnel_ref[pl.ds(1 - parity, 1), :] = jnp.minimum(least_ref[1:2], got_ref[0:1])
        move.wait()

    anywhere = pl.BlockSpec(memory_space=pl.ANY)
    return pl.pallas_call(
        body,
        in_specs=[scalars()] + [whole()] * 3 + [anywhere],
        out_specs=[anywhere, whole()],
        out_shape=[f32(*result.shape), f32(2, result.shape[3])],
        input_output_aliases={4: 0},
        scratch_shapes=[pltpu.SemaphoreType.DMA((1,))],
        compiler_params=compiler_params(),
        cost_estimate=estimate(),
        name="finish",
    )(flags, outer, least, least_got, result)


def per_device(value, cost, accel_first, accel_second):
    n_px, n_vx = lax.axis_size("px"), lax.axis_size("vx")
    rows, cells_v, total_vy, width = value.shape
    half = total_vy // 2
    total_vx = cells_v * n_vx
    sizes = (cells_v, half, width, total_vx, total_vy)
    px, vx = lax.axis_index("px"), lax.axis_index("vx")
    parity = px % 2
    flags = jnp.stack(
        [
            parity,
            ((px == 0) | (px == n_px - 1)).astype(jnp.int32),
            ((px == 1) | (px == n_px - 2)).astype(jnp.int32),
            (vx == 0).astype(jnp.int32),
            (vx == n_vx - 1).astype(jnp.int32),
        ]
    ).astype(jnp.int32)

    def partner(x):
        return lax.ppermute(x, "px", [(i, i ^ 1) for i in range(n_px)])

    def from_low_vx(x):
        return lax.ppermute(x, "vx", [(i, i + 1) for i in range(n_vx - 1)])

    def from_high_vx(x):
        return lax.ppermute(x, "vx", [(i + 1, i) for i in range(n_vx - 1)])

    def halo_before(outermost):
        moves = [(i, i + 2) for i in range(0, n_px - 2, 2)] + [(i, i - 2) for i in range(3, n_px, 2)]
        return lax.ppermute(outermost, "px", moves)

    def halo_after(outer):
        moves = [(i, i - 2) for i in range(2, n_px, 2)] + [(i, i + 2) for i in range(1, n_px - 2, 2)]
        return lax.ppermute(outer, "px", moves)

    def after(array, *others):
        return lax.optimization_barrier((array, *others))[0]

    def share(maxima, beside=None, partner_done=False):
        steps = [("vx", 1 << k) for k in range((n_vx - 1).bit_length())] + [("px", 1 << k) for k in range((n_px - 1).bit_length())]
        if partner_done:
            steps.remove(("px", 1))
        for place_at, (axis, apart) in enumerate(steps):
            other = lax.ppermute(maxima, axis, [(i, i ^ apart) for i in range(lax.axis_size(axis))])
            if beside is not None and place_at in beside:
                other = after(other, *beside[place_at])
            maxima = jnp.maximum(maxima, other)
        return maxima

    def half_of(array, row, which):
        return lax.dynamic_slice(array, (row, 0, which * half, 0), (1, cells_v, half, width))[0]

    value_outer = half_of(value, parity, 1 - parity)
    late = after(parity, value_outer)
    value_outer_got = partner(value_outer)
    push_got = partner(after(accel_first, value_outer))

    low_own = from_low_vx(after(value[:, cells_v - 1], value_outer))
    high_own = from_high_vx(after(value[:, 0], value_outer))
    row_needed = lax.dynamic_slice(value, (0, 0, half - parity, 0), (rows, cells_v, 1, width))[:, :, 0]
    row_given = lax.dynamic_slice(value, (0, 0, half - 1 + parity, 0), (rows, cells_v, 1, width))[:, :, 0]
    row_got = partner(after(row_given, value_outer))

    maxima = first_maxima(value, low_own, high_own, accel_first, accel_second, flags)
    maxima = jnp.maximum(maxima, partner(maxima))
    ahead = (maxima, row_got, push_got)
    value_inner_got = partner(after(half_of(value, 1 - late, 1 - late), *ahead))
    cost_outer_got = partner(after(half_of(cost, late, 1 - late), *ahead))
    cost_inner_got = partner(after(half_of(cost, 1 - late, 1 - late), *ahead))
    shared_first = share(maxima, partner_done=True)

    def pick(x, which):
        return lax.dynamic_index_in_dim(x, which, 0, keepdims=True)

    def in_chain(mine, others):
        return jnp.concatenate([pick(mine, parity), pick(mine, 1 - parity), pick(others, parity), pick(others, 1 - parity)], axis=0)

    def halo_chain(own, received):
        mine = lax.dynamic_slice(own, (0, parity * half, 0), (rows, half, width))
        return jnp.concatenate([pick(mine, parity), pick(mine, 1 - parity), received], axis=0)

    vx_low = halo_chain(low_own, from_low_vx(jnp.stack([value_inner_got[cells_v - 1], value_outer_got[cells_v - 1]])))
    vx_high = halo_chain(high_own, from_high_vx(jnp.stack([value_inner_got[0], value_outer_got[0]])))
    vy_next = jnp.concatenate([pick(row_got, 1 - parity), pick(row_got, parity), pick(row_needed, 1 - parity), pick(row_needed, parity)], axis=0)
    push = in_chain(accel_first, push_got)
    positions = (vx * cells_v + jnp.arange(cells_v, dtype=jnp.int32)).astype(jnp.float32)
    speed = (2.0 * positions + 1.0 - total_vx) * (VELOCITY_LIMIT / total_vx)
    speed = jnp.where(parity == 0, speed, -speed)
    table = jnp.concatenate([push, speed[None], jnp.pad(flags.astype(jnp.float32), (0, cells_v - flags.shape[0]))[None]], axis=0)

    chain = [Own(value, True), Own(value, False), Row(value_inner_got), Row(value_outer_got)]
    costs = [Own(cost, True), Own(cost, False), Row(cost_inner_got), Row(cost_outer_got)]
    halo_rows = (halo_before(value_outer_got), halo_after(half_of(value, late, late)))

    every = (0, 1, 2, 3)

    def advanced(targets, field, bases, halos, stepper):
        got = advance(sizes, targets, field, bases, halos, shared_first, stepper, accel_second, table)
        each = len(got) // len(targets)
        return {t: got[each * i : each * (i + 1)] for i, t in enumerate(targets)}

    def settled(targets, updates, **kw):
        return settle(sizes, targets, [updates[t] for t in targets], [costs[t] for t in targets], flags, **kw)

    def next_updates(field, edges, bases, stepper, halo_rows):
        first, _, _, last, edge, _, _ = edges
        low, high, row = from_low_vx(last), from_high_vx(first), partner(edge)
        def ahead(targets):
            return advanced(targets, field, None if bases is None else [bases[t] for t in targets], None, stepper)

        updates = ahead((1, 2))
        low, high, row = lax.optimization_barrier((low, high, row, updates))[:3]
        heun = bases is not None
        mended = mend(sizes, edges, low, high, row, shared_first, stepper, heun, accel_second, table)
        updates.update(ahead((0,)))
        updates.update(ahead((3,)))
        outer = outer_terms(sizes, field, halo_rows, shared_first, stepper, heun, table)
        maxima = share(edge_maxima(edges, low, high, row, flags), {1: mended, 2: updates[0], 3: updates[3], 4: outer})
        return {**updates, 0: updates[0] + outer[:1], 3: updates[3] + outer[1:]}, mended, maxima

    def settled_all(updates, **kw):
        fields = kw.pop("fields", None)
        some = {} if fields is None else {"fields": [fields[0], fields[3]]}
        (outer, far), edges = settled((0, 3), updates, **some, **kw)
        halo_rows = (halo_before(far), halo_after(outer))
        some = {} if fields is None else {"fields": [fields[1], fields[2]]}
        (inner, near), edges = settled((1, 2), updates, prior=((0, 3), edges), **some, **kw)
        return [Row(f) for f in (outer, inner, near, far)], edges, halo_rows

    halos = (halo_rows, vx_low, vx_high, vy_next)
    updates = advanced((1, 2), chain, None, halos, shared_first)
    updates.update(advanced((0, 3), chain, None, halos, shared_first))
    (outer, inner), edges = settled((0, 1), updates)
    beyond = halo_after(outer)
    (far,), edges = settled((3,), updates, prior=((0, 1), edges))
    halo_rows = (halo_before(far), beyond)
    (near,), edges = settled((2,), updates, prior=((0, 1, 3), edges))
    middle = [Row(f) for f in (outer, inner, near, far)]

    updates, mended, shared = next_updates(middle, edges, chain, shared_first, halo_rows)
    chain, edges, halo_rows = settled_all(updates, mended=mended, damping=(shared_first, shared_first, shared, 0.5))

    updates, mended, shared_second = next_updates(chain, edges, None, None, halo_rows)
    middle, edges, halo_rows = settled_all(updates, mended=mended, damping=(shared_first, shared_second, shared_second, 1.0), fields=chain)

    updates, mended, shared = next_updates(middle, edges, chain, shared_second, halo_rows)
    damping = (shared_first, shared_second, shared, 0.5)
    (near,), (least_near,) = settled((2,), updates, damping=damping, mended=mended, with_edges=False)
    inner_got = partner(near)
    (outer, inner, far), (least,) = settled((0, 1, 3), updates, damping=damping, mended=mended, with_edges=False)
    outer_got = partner(far)
    least = lax.pmin(jnp.concatenate([least[:2], least_near, least[2:]], axis=0), "vx")
    least_got = partner(after(least[2:], far))
    final = place(flags, [(True, outer), (False, inner)], None, value.shape)
    return finish(flags, outer_got, least, least_got, place(flags, [(False, inner_got)], final, value.shape, 1))


def solution(mesh):
    placed = (P("px", "vx", None, None), P("px", "vx", None, None), P("px", "vx"), P())
    return jax.shard_map(
        per_device,
        mesh=mesh,
        in_specs=placed,
        out_specs=(P("px", "vx", None, None), P("px", None)),
        check_vma=False,
    )
```

```python
import functools

import jax
import jax.numpy as jnp
from jax import lax
from jax.experimental import pallas as pl
from jax.experimental.pallas import tpu as pltpu
from jax.sharding import PartitionSpec as P

VELOCITY_LIMIT = 1.0
PLANNER_SPEED = 0.3
DISTURBANCE = 0.2
CONTROL_COST = 1.0
COURANT = 0.5

LANES = 128


def compiler_params():
    return pltpu.CompilerParams(vmem_limit_bytes=8 * 1024 * 1024)


def whole():
    return pl.BlockSpec(memory_space=pltpu.VMEM)


def scalars():
    return pl.BlockSpec(memory_space=pltpu.SMEM)


def fold(tile):
    rows = tile.shape[0]
    out = tile[0:8]
    for start in range(8, rows, 8):
        out = jnp.maximum(out, tile[start : start + 8])
    return out


def fold_min(tile):
    rows = tile.shape[0]
    out = tile[0:8]
    for start in range(8, rows, 8):
        out = jnp.minimum(out, tile[start : start + 8])
    return out


def maximum_row(ref, row):
    return jnp.broadcast_to(ref[pl.ds(row, 1), :], (8, LANES))


class Own:
    def __init__(self, array, outer):
        self.array, self.outer = array, outer

    def reader(self, ref, parity, half):
        row = parity if self.outer else 1 - parity
        start = pl.multiple_of(parity * half, half)
        return lambda j, g: ref[row, j, pl.ds(pl.multiple_of(start + 8 * g, 8), 8), :]


class Row:
    def __init__(self, array):
        self.array = array

    def reader(self, ref, parity, half):
        return lambda j, g: ref[j, pl.ds(8 * g, 8), :]


class Rates:
    def __init__(self, sizes):
        cells_v, half, width, total_vx, total_vy = sizes
        self.step_2 = 2.0 * VELOCITY_LIMIT / total_vx
        self.step_3 = 2.0 * VELOCITY_LIMIT / total_vy
        self.step_1 = self.step_2 * self.step_3
        self.rate_1 = VELOCITY_LIMIT * (total_vx - 1) / total_vx + PLANNER_SPEED
        self.rate_4 = VELOCITY_LIMIT * (total_vy - 1) / total_vy + PLANNER_SPEED

    def rates(self, limits, maxima):
        rate_2 = maximum_row(limits, 2) + DISTURBANCE + maximum_row(maxima, 0) * (0.5 / (self.step_2 * CONTROL_COST))
        rate_3 = maximum_row(limits, 3) + DISTURBANCE + maximum_row(maxima, 1) * (0.5 / (self.step_3 * CONTROL_COST))
        return rate_2 * (1.0 / self.step_2), rate_3 * (1.0 / self.step_3)

    def time_step(self, rates):
        total = rates[0] + rates[1] + (self.rate_1 + self.rate_4) / self.step_1
        return COURANT / total


class Operands:
    def __init__(self):
        self.arrays = []

    def add(self, array):
        for position, known in enumerate(self.arrays):
            if known is array:
                return position
        self.arrays.append(array)
        return len(self.arrays) - 1


def f32(*shape):
    return jax.ShapeDtypeStruct(shape, jnp.float32)


def estimate():
    return pl.CostEstimate(flops=0, bytes_accessed=0, transcendentals=0)


def advance(sizes, targets, rows, bases, halos, maxima, stepper, accel_second, table):
    cells_v, half, width, total_vx, total_vy = sizes
    count = len(targets)
    heun = bases is not None
    late = stepper is None
    full = halos is not None
    ops = Operands()
    needed = sorted({k for t in targets for k in (t - 1, t, t + 1) if 0 <= k <= 3})
    row_at = {k: ops.add(rows[k].array) for k in needed}
    base_at = [ops.add(b.array) for b in bases] if heun else []
    accel_at = ops.add(accel_second)
    if full:
        halo_rows, vx_low, vx_high, vy_next = halos
        halo_at = {k: ops.add(halo_rows[i]) for i, k in enumerate((-1, 4)) if any(abs(t - k) == 1 for t in targets)}
        low_at, high_at, vy_at = ops.add(vx_low), ops.add(vx_high), ops.add(vy_next)
    maxima_at = [] if late else [ops.add(maxima), ops.add(stepper)]
    n_in = len(ops.arrays)
    n_out = count * (1 if full else 3)
    groups = half // 8

    def body(table_ref, *refs):
        ins, outs = refs[:n_in], refs[n_in : n_in + n_out]
        adv_up, adv_down, acc_up, acc_down = refs[n_in + n_out :]
        is_odd, edge_low, edge_high, vx_first, vx_last = (table_ref[5, i] > 0.5 for i in range(5))
        is_even = jnp.logical_not(is_odd)
        parity = jnp.where(is_odd, 1, 0)
        known = Rates(sizes)
        step_1, step_2, step_3 = known.step_1, known.step_2, known.step_3
        if late:
            scale = jnp.ones((8, LANES), jnp.float32)
        else:
            rates = known.rates(ins[maxima_at[0]], ins[maxima_at[1]])
            scale = known.time_step(rates) * (0.5 if heun else 1.0)
        damp_1 = scale * (0.5 * known.rate_1 / step_1)
        damp_4 = scale * (0.5 * known.rate_4 / step_1)
        keep = 2.0 * (damp_1 + damp_4)
        if not late:
            keep = keep + (0.5 if heun else 1.0)
        if full:
            damp_2, damp_3 = scale * 0.5 * rates[0], scale * 0.5 * rates[1]
        planner = scale * (PLANNER_SPEED / (2.0 * step_1))
        disturb_2 = scale * (DISTURBANCE / (2.0 * step_2))
        disturb_3 = scale * (DISTURBANCE / (2.0 * step_3))
        control_2 = scale * (1.0 / (8.0 * CONTROL_COST * step_2 * step_2))
        control_3 = scale * (1.0 / (8.0 * CONTROL_COST * step_3 * step_3))
        to_1, to_2, to_3 = scale / (2.0 * step_1), scale / (2.0 * step_2), scale / (2.0 * step_3)

        def wide(x):
            return jnp.concatenate([x] * (width // LANES), axis=1)

        start = pl.multiple_of(parity * half, half)
        for g in range(groups):
            here = pl.ds(8 * g, 8)
            vy = (parity * half + 8 * g + lax.broadcasted_iota(jnp.int32, (8, LANES), 0)).astype(jnp.float32)
            speed_y = (2.0 * vy + (1.0 - total_vy)) * (VELOCITY_LIMIT / total_vy) * to_1
            adv_up[here, :] = speed_y + planner
            adv_down[here, :] = speed_y - planner
            accel = ins[accel_at][pl.ds(pl.multiple_of(start + 8 * g, 8), 8), :] * wide(to_3)
            acc_up[here, :] = accel + wide(disturb_3)
            acc_down[here, :] = accel - wide(disturb_3)
        keep_outer = wide(keep - 2.0 * damp_1)
        keep, damp_1, control_2, control_3 = wide(keep), wide(damp_1), wide(control_2), wide(control_3)
        if full:
            damp_2, damp_3 = wide(damp_2), wide(damp_3)

        readers = {k: rows[k].reader(ins[row_at[k]], parity, half) for k in needed}
        base_readers = [b.reader(ins[a], parity, half) for b, a in zip(bases, base_at)] if heun else None
        sublane = lax.broadcasted_iota(jnp.int32, (8, width), 0)
        lane = lax.broadcasted_iota(jnp.int32, (8, LANES), 1)

        def neighbour(k, j, g, center):
            if k == -1:
                return jnp.where(edge_low, center, ins[halo_at[-1]][j, pl.ds(8 * g, 8), :])
            if k == 4:
                return jnp.where(edge_high, center, ins[halo_at[4]][j, pl.ds(8 * g, 8), :])
            return readers[k](j, g)

        def lane_pieces(x):
            return [x[:, start : start + LANES] for start in range(0, width, LANES)]

        def upwind(up, down, slope):
            return jnp.maximum(up * slope, down * slope)

        def tile(i, j, low_j, high_j):
            t = targets[i]
            flow = table_ref[4, j] * to_1
            drift = table_ref[t, j] * to_2
            flow_up, flow_down = wide(flow + planner), wide(flow - planner)
            drift_up, drift_down = wide(drift + disturb_2), wide(drift - disturb_2)
            below = readers[t](j, 0)[0:1]
            above = readers[t](j, groups - 1)[7:8]
            if full:
                beyond = ins[vy_at][3 - t, pl.ds(j, 1), :]
                below, above = jnp.where(is_even, below, beyond), jnp.where(is_even, beyond, above)
            below, above = jnp.broadcast_to(below, (8, width)), jnp.broadcast_to(above, (8, width))
            ups = [below] + [pltpu.roll(readers[t](j, g), 1, 0) for g in range(groups)]
            downs = [pltpu.roll(readers[t](j, g), 7, 0) for g in range(groups)] + [above]
            for g in range(groups):
                w = readers[t](j, g)
                here = pl.ds(8 * g, 8)
                if full or t in (1, 2):
                    low_1, high_1 = neighbour(t - 1, j, g, w), neighbour(t + 1, j, g, w)
                    total = keep * w - damp_1 * (low_1 + high_1)
                    total = total + upwind(flow_up, flow_down, high_1 - low_1)
                else:
                    total = keep_outer * w

                pieces = lane_pieces(w)
                right = [pltpu.roll(p, 1, 1) for p in pieces]
                left = [pltpu.roll(p, LANES - 1, 1) for p in pieces]
                parts = []
                for p in range(len(pieces)):
                    low_4 = jnp.where(lane == 0, right[p - 1] if p > 0 else pieces[0], right[p])
                    high_4 = jnp.where(lane == LANES - 1, left[p + 1] if p + 1 < len(pieces) else pieces[p], left[p])
                    parts.append(upwind(adv_up[here, :], adv_down[here, :], high_4 - low_4) - damp_4 * (low_4 + high_4))
                total = total + jnp.concatenate(parts, axis=1)

                if low_j is None:
                    low_2 = jnp.where(vx_first, w, ins[low_at][t, here, :]) if full else w
                else:
                    low_2 = readers[t](low_j, g)
                if high_j is None:
                    high_2 = jnp.where(vx_last, w, ins[high_at][t, here, :]) if full else w
                else:
                    high_2 = readers[t](high_j, g)
                slope = high_2 - low_2
                bent = control_2 * slope
                total = total + (jnp.where(slope > 0.0, drift_up, drift_down) - bent) * slope

                low_3 = jnp.where(sublane == 0, ups[g], ups[g + 1])
                high_3 = jnp.where(sublane == 7, downs[g + 1], downs[g])
                slope = high_3 - low_3
                bent = control_3 * slope
                total = total + (jnp.where(slope > 0.0, acc_up[here, :], acc_down[here, :]) - bent) * slope

                twice = w + w
                bend_2 = low_2 + high_2 - twice
                bend_3 = low_3 + high_3 - twice
                if heun:
                    total = total + 0.5 * base_readers[i](j, g)
                if full:
                    total = total - damp_2 * bend_2 - damp_3 * bend_3
                    outs[i][j, here, :] = total
                else:
                    outs[3 * i][j, here, :] = total
                    outs[3 * i + 1][j, here, :] = bend_2
                    outs[3 * i + 2][j, here, :] = bend_3

        for i in range(count):
            tile(i, 0, None, 1)

        together = 2 if count == 1 and cells_v % 2 == 0 else 1

        @pl.loop(1, cells_v - 1, step=together)
        def _(j):
            for ahead in range(together):
                for i in range(count):
                    tile(i, j + ahead, j + ahead - 1, j + ahead + 1)

        for i in range(count):
            tile(i, cells_v - 1, cells_v - 2, None)

    return pl.pallas_call(
        body,
        out_shape=[f32(cells_v, half, width)] * n_out,
        in_specs=[scalars()] + [whole()] * n_in,
        out_specs=[whole()] * n_out,
        scratch_shapes=[pltpu.VMEM((half, LANES), jnp.float32)] * 2 + [pltpu.VMEM((half, width), jnp.float32)] * 2,
        compiler_params=compiler_params(),
        cost_estimate=estimate(),
        name="advance_" + "".join(str(t) for t in targets),
    )(table, *ops.arrays)


def outer_terms(sizes, rows, halo_rows, maxima, stepper, heun, table):
    cells_v, half, width, _, _ = sizes
    groups = half // 8
    late = stepper is None
    arrays = [r.array for r in rows] + list(halo_rows) + ([] if late else [maxima, stepper])

    def body(table_ref, *refs):
        row_refs, before_ref, after_ref, out_refs = refs[:4], refs[4], refs[5], refs[-2:]
        edge_low, edge_high = table_ref[5, 1] > 0.5, table_ref[5, 2] > 0.5
        known = Rates(sizes)
        if late:
            scale = jnp.ones((8, LANES), jnp.float32)
        else:
            scale = known.time_step(known.rates(refs[6], refs[7])) * (0.5 if heun else 1.0)

        def wide(x):
            return jnp.concatenate([x] * (width // LANES), axis=1)

        damp = wide(scale * (0.5 * known.rate_1 / known.step_1))
        planner = scale * (PLANNER_SPEED / (2.0 * known.step_1))
        to_1 = scale / (2.0 * known.step_1)

        together = 2 if cells_v % 2 == 0 else 1

        @pl.loop(0, cells_v, step=together)
        def _(start):
            for j, g in [(start + ahead, g) for ahead in range(together) for g in range(groups)]:
                here = pl.ds(8 * g, 8)
                flow = table_ref[4, j] * to_1
                up, down = wide(flow + planner), wide(flow - planner)
                for i in range(2):
                    w = row_refs[3 * i][j, here, :]
                    inside = row_refs[1 + i][j, here, :]
                    if i == 0:
                        low, high = jnp.where(edge_low, w, before_ref[j, here, :]), inside
                    else:
                        low, high = inside, jnp.where(edge_high, w, after_ref[j, here, :])
                    slope = high - low
                    out_refs[i][j, here, :] = jnp.maximum(up * slope, down * slope) - damp * (low + high - (w + w))

    return pl.pallas_call(
        body,
        out_shape=[f32(cells_v, half, width)] * 2,
        in_specs=[scalars()] + [whole()] * len(arrays),
        out_specs=[whole()] * 2,
        compiler_params=compiler_params(),
        cost_estimate=estimate(),
        name="outer_terms",
    )(table, *arrays)


def mend(sizes, edges, vx_low, vx_high, vy_next, maxima, stepper, heun, accel_second, table):
    cells_v, half, width, _, _ = sizes
    late = stepper is None
    first, second, before, last, edge, inner, _ = edges
    arrays = [first, second, before, last, edge, inner, vx_low, vx_high, vy_next, accel_second] + ([] if late else [maxima, stepper])

    def body(table_ref, *refs):
        first_ref, second_ref, before_ref, last_ref, edge_ref, inner_ref, low_ref, high_ref, next_ref, accel_ref = refs[:10]
        update_2, bend_2, update_3, bend_3 = refs[-4:]
        is_odd, _, _, vx_first, vx_last = (table_ref[5, i] > 0.5 for i in range(5))
        is_even = jnp.logical_not(is_odd)
        known = Rates(sizes)
        if late:
            scale = jnp.ones((8, LANES), jnp.float32)
        else:
            scale = known.time_step(known.rates(refs[10], refs[11])) * (0.5 if heun else 1.0)

        def wide(x):
            return jnp.concatenate([x] * (width // LANES), axis=1)

        disturb_2 = scale * (DISTURBANCE / (2.0 * known.step_2))
        disturb_3 = wide(scale * (DISTURBANCE / (2.0 * known.step_3)))
        control_2 = wide(scale * (1.0 / (8.0 * CONTROL_COST * known.step_2 * known.step_2)))
        control_3 = wide(scale * (1.0 / (8.0 * CONTROL_COST * known.step_3 * known.step_3)))
        to_2, to_3 = scale / (2.0 * known.step_2), wide(scale / (2.0 * known.step_3))

        def term(up, down, control, slope):
            return (jnp.where(slope > 0.0, up, down) - control * slope) * slope

        for t in range(4):
            for e, j in ((0, 0), (1, cells_v - 1)):
                drift = table_ref[t, j] * to_2
                up, down = wide(drift + disturb_2), wide(drift - disturb_2)
                for start in range(0, half, 8):
                    here = pl.ds(start, 8)
                    if e == 0:
                        own, inside = first_ref[t, here, :], second_ref[t, here, :]
                        halo = jnp.where(vx_first, own, low_ref[t, here, :])
                        right, wrong = inside - halo, inside - own
                    else:
                        own, inside = last_ref[t, here, :], before_ref[t, here, :]
                        halo = jnp.where(vx_last, own, high_ref[t, here, :])
                        right, wrong = halo - inside, own - inside
                    update_2[t, e, here, :] = term(up, down, control_2, right) - term(up, down, control_2, wrong)
                    bend_2[t, e, here, :] = halo - own
        at = jnp.where(is_even, half - 1, half)
        accel = jnp.broadcast_to(accel_ref[pl.ds(at, 1), :], (8, width)) * to_3
        up, down = accel + disturb_3, accel - disturb_3
        for t in range(4):
            for start in range(0, cells_v, 8):
                here = pl.ds(start, 8)
                own, inside, halo = edge_ref[t, here, :], inner_ref[t, here, :], next_ref[3 - t, here, :]
                right = jnp.where(is_even, halo - inside, inside - halo)
                wrong = jnp.where(is_even, own - inside, inside - own)
                update_3[t, here, :] = term(up, down, control_3, right) - term(up, down, control_3, wrong)
                bend_3[t, here, :] = halo - own

    return pl.pallas_call(
        body,
        out_shape=[f32(4, 2, half, width)] * 2 + [f32(4, cells_v, width)] * 2,
        in_specs=[scalars()] + [whole()] * len(arrays),
        out_specs=[whole()] * 4,
        compiler_params=compiler_params(),
        cost_estimate=estimate(),
        name="mend",
    )(table, *arrays)


def settle(sizes, targets, updates, costs, flags, damping=None, fields=None, prior=None, with_edges=True, mended=None):
    cells_v, half, width, total_vx, total_vy = sizes
    count = len(targets)
    ops = Operands()
    update_at = [[ops.add(a) for a in u] for u in updates]
    cost_at = [ops.add(c.array) for c in costs]
    field_at = [ops.add(f.array) for f in fields] if fields is not None else []
    mended_at = [ops.add(m) for m in mended] if mended is not None else []
    maxima_at = [ops.add(m) for m in damping[:3]] if damping is not None else []
    before_targets, before_outs = prior if prior is not None else ((), ())
    prior_at = [ops.add(a) for a in before_outs]
    n_in = len(ops.arrays)
    every = sorted(tuple(before_targets) + tuple(targets))
    groups = half // 8

    def body(flags_ref, *refs):
        ins, outs = refs[:n_in], refs[n_in:]
        fields_out = outs[:count]
        parity = flags_ref[0]
        is_even = parity == 0
        if damping is not None:
            known = Rates(sizes)
            step_rates = known.rates(ins[maxima_at[0]], ins[maxima_at[1]])
            rates = step_rates if maxima_at[1] == maxima_at[2] else known.rates(ins[maxima_at[0]], ins[maxima_at[2]])
            scale = known.time_step(step_rates) * damping[3]
            if fields is None:
                damp_2, damp_3 = scale * 0.5 * rates[0], scale * 0.5 * rates[1]
            else:
                damp_2, damp_3 = 0.5 * rates[0], 0.5 * rates[1]
            damp_2, damp_3, scale = (jnp.concatenate([x] * (width // LANES), axis=1) for x in (damp_2, damp_3, scale))
        cost_readers = [c.reader(ins[a], parity, half) for c, a in zip(costs, cost_at)]
        field_readers = [f.reader(ins[a], parity, half) for f, a in zip(fields or (), field_at)]
        sublane = lax.broadcasted_iota(jnp.int32, (8, width), 0)

        row_low = jnp.where(is_even, -1, 0)
        row_high = jnp.where(is_even, 7, -1)

        def tile(i, j, end=None):
            t = targets[i]
            out = []
            if mended is not None:
                along_2, twice_2, along_3, twice_3 = (ins[a] for a in mended_at)
                here = pl.ds(j, 1)
                beside = jnp.broadcast_to(along_3[t, here, :] - damp_3[0:1] * twice_3[t, here, :], (8, width))
            for g in range(groups):
                here = pl.ds(8 * g, 8)
                total = ins[update_at[i][0]][j, here, :]
                if len(update_at[i]) > 3:
                    total = total + ins[update_at[i][3]][j, here, :]
                if damping is not None:
                    total = total - damp_2 * ins[update_at[i][1]][j, here, :] - damp_3 * ins[update_at[i][2]][j, here, :]
                if mended is not None:
                    if g == 0:
                        total = total + jnp.where(sublane == row_low, beside, 0.0)
                    if g == groups - 1:
                        total = total + jnp.where(sublane == row_high, beside, 0.0)
                    if end is not None:
                        total = total + along_2[t, end, here, :] - damp_2 * twice_2[t, end, here, :]
                if fields is not None:
                    total = field_readers[i](j, g) + scale * total
                y = jnp.maximum(cost_readers[i](j, g), total)
                fields_out[i][j, here, :] = y
                out.append(y)
            return out

        if not with_edges:
            least_ref = outs[count]
            least = [functools.reduce(jnp.minimum, tile(i, 0, 0) + tile(i, cells_v - 1, 1)) for i in range(count)]

            def lower(j, least):
                return tuple(jnp.minimum(least[i], functools.reduce(jnp.minimum, tile(i, j))) for i in range(count))

            least = lax.fori_loop(1, cells_v - 1, lower, tuple(least))
            for i in range(count):
                least_ref[pl.ds(i, 1), :] = jnp.min(least[i], axis=0, keepdims=True)
            return

        first_ref, second_ref, before_ref, last_ref, edge_ref, inner_ref, part_ref = outs[count : count + 7]
        send_at = jnp.where(is_even, half - 1, 0)
        inner_at = jnp.where(is_even, half - 2, 1)
        wall_at = jnp.where(is_even, 0, half - 1)
        next_at = jnp.where(is_even, 1, half - 2)
        for position, t in enumerate(sorted(before_targets)):
            slot = every.index(t)
            for ref, at in zip((first_ref, second_ref, before_ref, last_ref, edge_ref, inner_ref), prior_at):
                ref[slot] = ins[at][position]

        def one(i, j, end=None):
            slot = every.index(targets[i])
            out = tile(i, j, end)
            edge_ref[slot, pl.ds(j, 1), :] = fields_out[i][j, pl.ds(send_at, 1), :]
            inner_ref[slot, pl.ds(j, 1), :] = fields_out[i][j, pl.ds(inner_at, 1), :]
            wall = jnp.abs(fields_out[i][j, pl.ds(next_at, 1), :] - fields_out[i][j, pl.ds(wall_at, 1), :])
            rolled = [pltpu.roll(y, 2, 0) for y in out]
            slopes_3 = [jnp.broadcast_to(wall, (8, width))]
            for g in range(groups):
                apart = jnp.where(sublane < 2, rolled[g - 1] if g > 0 else out[0], rolled[g])
                slopes_3.append(jnp.abs(out[g] - apart))
            return out, functools.reduce(jnp.maximum, slopes_3)

        def both(i, j, end=None):
            out, most_3 = one(i, j, end)
            slopes_2 = [jnp.abs(out[g] - fields_out[i][j - 2, pl.ds(8 * g, 8), :]) for g in range(groups)]
            return functools.reduce(jnp.maximum, slopes_2), most_3

        starts = [jnp.maximum(one(i, 0, 0)[1], one(i, 1)[1]) for i in range(count)]
        zero = jnp.zeros((8, width), jnp.float32)

        def step(j, carry):
            found = [both(i, j) for i in range(count)]
            return tuple((jnp.maximum(carry[i][0], found[i][0]), jnp.maximum(carry[i][1], found[i][1])) for i in range(count))

        most = lax.fori_loop(2, cells_v - 1, step, tuple((zero, start) for start in starts))
        most = list(most) + [both(i, cells_v - 1, 1) for i in range(count)]
        if prior is not None:
            most.append((ins[prior_at[6]][0], ins[prior_at[6]][1]))
        part_ref[0] = functools.reduce(jnp.maximum, [m[0] for m in most])
        part_ref[1] = functools.reduce(jnp.maximum, [m[1] for m in most])
        for i in range(count):
            slot = every.index(targets[i])
            first_ref[slot] = fields_out[i][0]
            second_ref[slot] = fields_out[i][1]
            before_ref[slot] = fields_out[i][cells_v - 2]
            last_ref[slot] = fields_out[i][cells_v - 1]

    n = len(every)
    shapes = [f32(cells_v, half, width)] * count
    if with_edges:
        shapes += [f32(n, half, width)] * 4 + [f32(n, cells_v, width)] * 2 + [f32(2, 8, width)]
    else:
        shapes.append(f32(count, width))
    outs = pl.pallas_call(
        body,
        out_shape=shapes,
        in_specs=[scalars()] + [whole()] * n_in,
        out_specs=[whole()] * len(shapes),
        compiler_params=compiler_params(),
        cost_estimate=estimate(),
        name="settle_" + "".join(str(t) for t in targets),
    )(flags, *ops.arrays)
    return outs[:count], outs[count:]


def spread(values):
    position = lax.broadcasted_iota(jnp.int32, (8, LANES), 0)
    out = jnp.zeros((8, LANES), jnp.float32)
    for row, value in enumerate(values):
        out = jnp.where(position == row, value, out)
    return out


def first_maxima(value, vx_low, vx_high, accel_first, accel_second, flags):
    rows, cells_v, total_vy, width = value.shape

    def body(flags_ref, v_ref, low_ref, high_ref, first_ref, second_ref, out_ref):
        vx_first, vx_last = flags_ref[3], flags_ref[4]
        vy_row = lax.broadcasted_iota(jnp.int32, (total_vy, width), 0)

        def of_vy(x):
            inner = jnp.where(vy_row >= 2, jnp.abs(x - pltpu.roll(x, 2, 0)), 0.0)
            wall = jnp.maximum(jnp.abs(x[1:2] - x[0:1]), jnp.abs(x[total_vy - 1 : total_vy] - x[total_vy - 2 : total_vy - 1]))
            return jnp.maximum(fold(inner), wall)

        most_2 = jnp.zeros((8, width), jnp.float32)
        most_3 = jnp.zeros((8, width), jnp.float32)
        for r in range(rows):
            x = v_ref[r, 0]
            most_3 = jnp.maximum(most_3, of_vy(x))
            most_2 = jnp.maximum(most_2, fold(jnp.abs(v_ref[r, 1] - jnp.where(vx_first == 1, x, low_ref[r]))))
            x = v_ref[r, cells_v - 1]
            most_3 = jnp.maximum(most_3, of_vy(x))
            most_2 = jnp.maximum(most_2, fold(jnp.abs(v_ref[r, cells_v - 2] - jnp.where(vx_last == 1, x, high_ref[r]))))

            def step(j, carry, r=r):
                most_2, most_3 = carry
                most_3 = jnp.maximum(most_3, of_vy(v_ref[r, j]))
                most_2 = jnp.maximum(most_2, fold(jnp.abs(v_ref[r, j + 1] - v_ref[r, j - 1])))
                return most_2, most_3

            most_2, most_3 = lax.fori_loop(1, cells_v - 1, step, (most_2, most_3))
        values = (jnp.max(most_2), jnp.max(most_3), jnp.max(jnp.abs(first_ref[...])), jnp.max(jnp.abs(second_ref[...])))
        out_ref[...] = spread(values)

    return pl.pallas_call(
        body,
        out_shape=f32(8, LANES),
        in_specs=[scalars()] + [whole()] * 5,
        out_specs=whole(),
        compiler_params=compiler_params(),
        cost_estimate=estimate(),
        name="first_maxima",
    )(flags, value, vx_low, vx_high, accel_first, accel_second)


def edge_maxima(edges, vx_low, vx_high, vy_next, flags):
    first, second, before, last, _, inner, part = edges

    def body(flags_ref, first_ref, second_ref, before_ref, last_ref, low_ref, high_ref, inner_ref, next_ref, part_ref, out_ref):
        vx_first, vx_last = flags_ref[3], flags_ref[4]
        most_2, most_3 = part_ref[0], part_ref[1]
        for t in range(4):
            low = jnp.where(vx_first == 1, first_ref[t], low_ref[t])
            high = jnp.where(vx_last == 1, last_ref[t], high_ref[t])
            most_2 = jnp.maximum(most_2, fold(jnp.abs(second_ref[t] - low)))
            most_2 = jnp.maximum(most_2, fold(jnp.abs(high - before_ref[t])))
            most_3 = jnp.maximum(most_3, fold(jnp.abs(inner_ref[t] - next_ref[3 - t])))
        out_ref[...] = spread((jnp.max(most_2), jnp.max(most_3)))

    return pl.pallas_call(
        body,
        out_shape=f32(8, LANES),
        in_specs=[scalars()] + [whole()] * 9,
        out_specs=whole(),
        compiler_params=compiler_params(),
        cost_estimate=estimate(),
        name="edge_maxima",
    )(flags, first, second, before, last, vx_low, vx_high, inner, vy_next, part)


def copies(flags_ref, pieces, out_ref, sems, which):
    parity = flags_ref[0]
    half = out_ref.shape[2] // 2
    start = pl.multiple_of((parity if which == 0 else 1 - parity) * half, half)
    return [
        pltpu.make_async_copy(ref, out_ref.at[parity if outer else 1 - parity, :, pl.ds(start, half), :], sems.at[i])
        for i, (outer, ref) in enumerate(pieces)
    ]


def place(flags, pieces, result, shape, which=0):
    count = len(pieces)

    def body(flags_ref, *refs):
        moves = copies(flags_ref, [(pieces[i][0], refs[i]) for i in range(count)], refs[-2], refs[-1], which)
        for move in moves:
            move.start()
        for move in moves:
            move.wait()

    anywhere = pl.BlockSpec(memory_space=pl.ANY)
    extra = [] if result is None else [result]
    return pl.pallas_call(
        body,
        in_specs=[scalars()] + [whole()] * count + [anywhere] * len(extra),
        out_specs=anywhere,
        out_shape=f32(*shape),
        input_output_aliases={} if result is None else {1 + count: 0},
        scratch_shapes=[pltpu.SemaphoreType.DMA((count,))],
        compiler_params=compiler_params(),
        cost_estimate=estimate(),
        name="place",
    )(flags, *[p[1] for p in pieces], *extra)


def finish(flags, outer, least, least_got, result):
    def body(flags_ref, outer_ref, least_ref, got_ref, _, out_ref, funnel_ref, sems):
        parity = flags_ref[0]
        (move,) = copies(flags_ref, [(True, outer_ref)], out_ref, sems, 1)
        move.start()
        funnel_ref[pl.ds(parity, 1), :] = jnp.minimum(least_ref[0:1], got_ref[1:2])
        funnel_ref[pl.ds(1 - parity, 1), :] = jnp.minimum(least_ref[1:2], got_ref[0:1])
        move.wait()

    anywhere = pl.BlockSpec(memory_space=pl.ANY)
    return pl.pallas_call(
        body,
        in_specs=[scalars()] + [whole()] * 3 + [anywhere],
        out_specs=[anywhere, whole()],
        out_shape=[f32(*result.shape), f32(2, result.shape[3])],
        input_output_aliases={4: 0},
        scratch_shapes=[pltpu.SemaphoreType.DMA((1,))],
        compiler_params=compiler_params(),
        cost_estimate=estimate(),
        name="finish",
    )(flags, outer, least, least_got, result)


def per_device(value, cost, accel_first, accel_second):
    n_px, n_vx = lax.axis_size("px"), lax.axis_size("vx")
    rows, cells_v, total_vy, width = value.shape
    half = total_vy // 2
    total_vx = cells_v * n_vx
    sizes = (cells_v, half, width, total_vx, total_vy)
    px, vx = lax.axis_index("px"), lax.axis_index("vx")
    parity = px % 2
    flags = jnp.stack(
        [
            parity,
            ((px == 0) | (px == n_px - 1)).astype(jnp.int32),
            ((px == 1) | (px == n_px - 2)).astype(jnp.int32),
            (vx == 0).astype(jnp.int32),
            (vx == n_vx - 1).astype(jnp.int32),
        ]
    ).astype(jnp.int32)

    def partner(x):
        return lax.ppermute(x, "px", [(i, i ^ 1) for i in range(n_px)])

    def from_low_vx(x):
        return lax.ppermute(x, "vx", [(i, i + 1) for i in range(n_vx - 1)])

    def from_high_vx(x):
        return lax.ppermute(x, "vx", [(i + 1, i) for i in range(n_vx - 1)])

    def halo_before(outermost):
        moves = [(i, i + 2) for i in range(0, n_px - 2, 2)] + [(i, i - 2) for i in range(3, n_px, 2)]
        return lax.ppermute(outermost, "px", moves)

    def halo_after(outer):
        moves = [(i, i - 2) for i in range(2, n_px, 2)] + [(i, i + 2) for i in range(1, n_px - 2, 2)]
        return lax.ppermute(outer, "px", moves)

    def after(array, *others):
        return lax.optimization_barrier((array, *others))[0]

    def share(maxima, beside=None, partner_done=False):
        steps = [("vx", 1 << k) for k in range((n_vx - 1).bit_length())] + [("px", 1 << k) for k in range((n_px - 1).bit_length())]
        if partner_done:
            steps.remove(("px", 1))
        for place_at, (axis, apart) in enumerate(steps):
            other = lax.ppermute(maxima, axis, [(i, i ^ apart) for i in range(lax.axis_size(axis))])
            if beside is not None and place_at in beside:
                other = after(other, *beside[place_at])
            maxima = jnp.maximum(maxima, other)
        return maxima

    def half_of(array, row, which):
        return lax.dynamic_slice(array, (row, 0, which * half, 0), (1, cells_v, half, width))[0]

    value_outer = half_of(value, parity, 1 - parity)
    late = after(parity, value_outer)
    value_outer_got = partner(value_outer)
    push_got = partner(after(accel_first, value_outer))

    low_own = from_low_vx(after(value[:, cells_v - 1], value_outer))
    high_own = from_high_vx(after(value[:, 0], value_outer))
    row_needed = lax.dynamic_slice(value, (0, 0, half - parity, 0), (rows, cells_v, 1, width))[:, :, 0]
    row_given = lax.dynamic_slice(value, (0, 0, half - 1 + parity, 0), (rows, cells_v, 1, width))[:, :, 0]
    row_got = partner(after(row_given, value_outer))

    maxima = first_maxima(value, low_own, high_own, accel_first, accel_second, flags)
    maxima = jnp.maximum(maxima, partner(maxima))
    ahead = (maxima, row_got, push_got)
    value_inner_got = partner(after(half_of(value, 1 - late, 1 - late), *ahead))
    cost_outer_got = partner(after(half_of(cost, late, 1 - late), *ahead))
    cost_inner_got = partner(after(half_of(cost, 1 - late, 1 - late), *ahead))
    shared_first = share(maxima, partner_done=True)

    def pick(x, which):
        return lax.dynamic_index_in_dim(x, which, 0, keepdims=True)

    def in_chain(mine, others):
        return jnp.concatenate([pick(mine, parity), pick(mine, 1 - parity), pick(others, parity), pick(others, 1 - parity)], axis=0)

    def halo_chain(own, received):
        mine = lax.dynamic_slice(own, (0, parity * half, 0), (rows, half, width))
        return jnp.concatenate([pick(mine, parity), pick(mine, 1 - parity), received], axis=0)

    vx_low = halo_chain(low_own, from_low_vx(jnp.stack([value_inner_got[cells_v - 1], value_outer_got[cells_v - 1]])))
    vx_high = halo_chain(high_own, from_high_vx(jnp.stack([value_inner_got[0], value_outer_got[0]])))
    vy_next = jnp.concatenate([pick(row_got, 1 - parity), pick(row_got, parity), pick(row_needed, 1 - parity), pick(row_needed, parity)], axis=0)
    push = in_chain(accel_first, push_got)
    positions = (vx * cells_v + jnp.arange(cells_v, dtype=jnp.int32)).astype(jnp.float32)
    speed = (2.0 * positions + 1.0 - total_vx) * (VELOCITY_LIMIT / total_vx)
    speed = jnp.where(parity == 0, speed, -speed)
    table = jnp.concatenate([push, speed[None], jnp.pad(flags.astype(jnp.float32), (0, cells_v - flags.shape[0]))[None]], axis=0)

    chain = [Own(value, True), Own(value, False), Row(value_inner_got), Row(value_outer_got)]
    costs = [Own(cost, True), Own(cost, False), Row(cost_inner_got), Row(cost_outer_got)]
    halo_rows = (halo_before(value_outer_got), halo_after(half_of(value, late, late)))

    every = (0, 1, 2, 3)

    def advanced(targets, field, bases, halos, stepper, table=table):
        got = advance(sizes, targets, field, bases, halos, shared_first, stepper, accel_second, table)
        each = len(got) // len(targets)
        return {t: got[each * i : each * (i + 1)] for i, t in enumerate(targets)}

    def settled(targets, updates, **kw):
        return settle(sizes, targets, [updates[t] for t in targets], [costs[t] for t in targets], flags, **kw)

    def next_updates(field, edges, bases, stepper, halo_rows, outer_later=False):
        first, _, _, last, edge, _, _ = edges
        low, high, row = from_low_vx(last), from_high_vx(first), partner(edge)
        heun = bases is not None

        def ahead(targets, table=table):
            return advanced(targets, field, [bases[t] for t in targets] if heun else None, None, stepper, table)

        def terms(table=table):
            return outer_terms(sizes, field, halo_rows, shared_first, stepper, heun, table)

        updates = ahead((1, 2))
        low, high, row = lax.optimization_barrier((low, high, row, updates))[:3]
        mended = mend(sizes, edges, low, high, row, shared_first, stepper, heun, accel_second, table)
        maxima = edge_maxima(edges, low, high, row, flags)
        if outer_later:

            def outer_updates(settled):
                late_table = after(table, settled)
                got, outer = ahead((0, 3), late_table), terms(late_table)
                return {0: got[0] + outer[:1], 3: got[3] + outer[1:]}

            return updates, outer_updates, mended, share(maxima, {1: mended})
        updates.update(ahead((0,)))
        updates.update(ahead((3,)))
        outer = terms()
        maxima = share(maxima, {1: mended, 2: updates[0], 3: updates[3], 4: outer})
        return {**updates, 0: updates[0] + outer[:1], 3: updates[3] + outer[1:]}, mended, maxima

    def settled_all(updates, **kw):
        fields = kw.pop("fields", None)
        some = {} if fields is None else {"fields": [fields[0], fields[3]]}
        (outer, far), edges = settled((0, 3), updates, **some, **kw)
        halo_rows = (halo_before(far), halo_after(outer))
        some = {} if fields is None else {"fields": [fields[1], fields[2]]}
        (inner, near), edges = settled((1, 2), updates, prior=((0, 3), edges), **some, **kw)
        return [Row(f) for f in (outer, inner, near, far)], edges, halo_rows

    halos = (halo_rows, vx_low, vx_high, vy_next)
    updates = advanced((1, 2), chain, None, halos, shared_first)
    updates.update(advanced((0, 3), chain, None, halos, shared_first))
    (outer, inner), edges = settled((0, 1), updates)
    beyond = halo_after(outer)
    (far,), edges = settled((3,), updates, prior=((0, 1), edges))
    halo_rows = (halo_before(far), beyond)
    (near,), edges = settled((2,), updates, prior=((0, 1, 3), edges))
    middle = [Row(f) for f in (outer, inner, near, far)]

    updates, mended, shared = next_updates(middle, edges, chain, shared_first, halo_rows)
    chain, edges, halo_rows = settled_all(updates, mended=mended, damping=(shared_first, shared_first, shared, 0.5))

    updates, mended, shared_second = next_updates(chain, edges, None, None, halo_rows)
    middle, edges, halo_rows = settled_all(updates, mended=mended, damping=(shared_first, shared_second, shared_second, 1.0), fields=chain)

    updates, outer_updates, mended, shared = next_updates(middle, edges, chain, shared_second, halo_rows, outer_later=True)
    damping = (shared_first, shared_second, shared, 0.5)
    (near,), (least_near,) = settled((2,), updates, damping=damping, mended=mended, with_edges=False)
    inner_got = partner(near)
    updates.update(outer_updates(near))
    (outer, inner, far), (least,) = settled((0, 1, 3), updates, damping=damping, mended=mended, with_edges=False)
    outer_got = partner(far)
    least = lax.pmin(jnp.concatenate([least[:2], least_near, least[2:]], axis=0), "vx")
    least_got = partner(after(least[2:], far))
    final = place(flags, [(True, outer), (False, inner)], None, value.shape)
    return finish(flags, outer_got, least, least_got, place(flags, [(False, inner_got)], final, value.shape, 1))


def solution(mesh):
    placed = (P("px", "vx", None, None), P("px", "vx", None, None), P("px", "vx"), P())
    return jax.shard_map(
        per_device,
        mesh=mesh,
        in_specs=placed,
        out_specs=(P("px", "vx", None, None), P("px", None)),
        check_vma=False,
    )
```

```python
import functools

import jax
import jax.numpy as jnp
from jax import lax
from jax.experimental import pallas as pl
from jax.experimental.pallas import tpu as pltpu
from jax.sharding import PartitionSpec as P

VELOCITY_LIMIT = 1.0
PLANNER_SPEED = 0.3
DISTURBANCE = 0.2
CONTROL_COST = 1.0
COURANT = 0.5

LANES = 128


def compiler_params():
    return pltpu.CompilerParams(vmem_limit_bytes=8 * 1024 * 1024)


def whole():
    return pl.BlockSpec(memory_space=pltpu.VMEM)


def scalars():
    return pl.BlockSpec(memory_space=pltpu.SMEM)


def fold(tile):
    rows = tile.shape[0]
    out = tile[0:8]
    for start in range(8, rows, 8):
        out = jnp.maximum(out, tile[start : start + 8])
    return out


def fold_min(tile):
    rows = tile.shape[0]
    out = tile[0:8]
    for start in range(8, rows, 8):
        out = jnp.minimum(out, tile[start : start + 8])
    return out


def maximum_row(ref, row):
    return jnp.broadcast_to(ref[pl.ds(row, 1), :], (8, LANES))


class Own:
    def __init__(self, array, outer):
        self.array, self.outer = array, outer

    def reader(self, ref, parity, half):
        row = parity if self.outer else 1 - parity
        start = pl.multiple_of(parity * half, half)
        return lambda j, g: ref[row, j, pl.ds(pl.multiple_of(start + 8 * g, 8), 8), :]


class Row:
    def __init__(self, array):
        self.array = array

    def reader(self, ref, parity, half):
        return lambda j, g: ref[j, pl.ds(8 * g, 8), :]


class Rates:
    def __init__(self, sizes):
        cells_v, half, width, total_vx, total_vy = sizes
        self.step_2 = 2.0 * VELOCITY_LIMIT / total_vx
        self.step_3 = 2.0 * VELOCITY_LIMIT / total_vy
        self.step_1 = self.step_2 * self.step_3
        self.rate_1 = VELOCITY_LIMIT * (total_vx - 1) / total_vx + PLANNER_SPEED
        self.rate_4 = VELOCITY_LIMIT * (total_vy - 1) / total_vy + PLANNER_SPEED

    def rates(self, limits, maxima):
        rate_2 = maximum_row(limits, 2) + DISTURBANCE + maximum_row(maxima, 0) * (0.5 / (self.step_2 * CONTROL_COST))
        rate_3 = maximum_row(limits, 3) + DISTURBANCE + maximum_row(maxima, 1) * (0.5 / (self.step_3 * CONTROL_COST))
        return rate_2 * (1.0 / self.step_2), rate_3 * (1.0 / self.step_3)

    def time_step(self, rates):
        total = rates[0] + rates[1] + (self.rate_1 + self.rate_4) / self.step_1
        return COURANT / total


class Operands:
    def __init__(self):
        self.arrays = []

    def add(self, array):
        for position, known in enumerate(self.arrays):
            if known is array:
                return position
        self.arrays.append(array)
        return len(self.arrays) - 1


def f32(*shape):
    return jax.ShapeDtypeStruct(shape, jnp.float32)


def estimate():
    return pl.CostEstimate(flops=0, bytes_accessed=0, transcendentals=0)


def advance(sizes, targets, rows, bases, halos, maxima, stepper, accel_second, table):
    cells_v, half, width, total_vx, total_vy = sizes
    count = len(targets)
    heun = bases is not None
    late = stepper is None
    full = halos is not None
    ops = Operands()
    needed = sorted({k for t in targets for k in (t - 1, t, t + 1) if 0 <= k <= 3})
    row_at = {k: ops.add(rows[k].array) for k in needed}
    base_at = [ops.add(b.array) for b in bases] if heun else []
    accel_at = ops.add(accel_second)
    if full:
        halo_rows, vx_low, vx_high, vy_next = halos
        halo_at = {k: ops.add(halo_rows[i]) for i, k in enumerate((-1, 4)) if any(abs(t - k) == 1 for t in targets)}
        low_at, high_at, vy_at = ops.add(vx_low), ops.add(vx_high), ops.add(vy_next)
    maxima_at = [] if late else [ops.add(maxima), ops.add(stepper)]
    n_in = len(ops.arrays)
    n_out = count * (1 if full else 3)
    groups = half // 8

    def body(table_ref, *refs):
        ins, outs = refs[:n_in], refs[n_in : n_in + n_out]
        adv_up, adv_down, acc_up, acc_down = refs[n_in + n_out :]
        is_odd, edge_low, edge_high, vx_first, vx_last = (table_ref[5, i] > 0.5 for i in range(5))
        is_even = jnp.logical_not(is_odd)
        parity = jnp.where(is_odd, 1, 0)
        known = Rates(sizes)
        step_1, step_2, step_3 = known.step_1, known.step_2, known.step_3
        if late:
            scale = jnp.ones((8, LANES), jnp.float32)
        else:
            rates = known.rates(ins[maxima_at[0]], ins[maxima_at[1]])
            scale = known.time_step(rates) * (0.5 if heun else 1.0)
        damp_1 = scale * (0.5 * known.rate_1 / step_1)
        damp_4 = scale * (0.5 * known.rate_4 / step_1)
        keep = 2.0 * (damp_1 + damp_4)
        if not late:
            keep = keep + (0.5 if heun else 1.0)
        if full:
            damp_2, damp_3 = scale * 0.5 * rates[0], scale * 0.5 * rates[1]
        planner = scale * (PLANNER_SPEED / (2.0 * step_1))
        disturb_2 = scale * (DISTURBANCE / (2.0 * step_2))
        disturb_3 = scale * (DISTURBANCE / (2.0 * step_3))
        control_2 = scale * (1.0 / (8.0 * CONTROL_COST * step_2 * step_2))
        control_3 = scale * (1.0 / (8.0 * CONTROL_COST * step_3 * step_3))
        to_1, to_2, to_3 = scale / (2.0 * step_1), scale / (2.0 * step_2), scale / (2.0 * step_3)

        def wide(x):
            return jnp.concatenate([x] * (width // LANES), axis=1)

        start = pl.multiple_of(parity * half, half)
        for g in range(groups):
            here = pl.ds(8 * g, 8)
            vy = (parity * half + 8 * g + lax.broadcasted_iota(jnp.int32, (8, LANES), 0)).astype(jnp.float32)
            speed_y = (2.0 * vy + (1.0 - total_vy)) * (VELOCITY_LIMIT / total_vy) * to_1
            adv_up[here, :] = speed_y + planner
            adv_down[here, :] = speed_y - planner
            accel = ins[accel_at][pl.ds(pl.multiple_of(start + 8 * g, 8), 8), :] * wide(to_3)
            acc_up[here, :] = accel + wide(disturb_3)
            acc_down[here, :] = accel - wide(disturb_3)
        keep_outer = wide(keep - 2.0 * damp_1)
        keep, damp_1, control_2, control_3 = wide(keep), wide(damp_1), wide(control_2), wide(control_3)
        if full:
            damp_2, damp_3 = wide(damp_2), wide(damp_3)

        readers = {k: rows[k].reader(ins[row_at[k]], parity, half) for k in needed}
        base_readers = [b.reader(ins[a], parity, half) for b, a in zip(bases, base_at)] if heun else None
        sublane = lax.broadcasted_iota(jnp.int32, (8, width), 0)
        lane = lax.broadcasted_iota(jnp.int32, (8, LANES), 1)

        def neighbour(k, j, g, center):
            if k == -1:
                return jnp.where(edge_low, center, ins[halo_at[-1]][j, pl.ds(8 * g, 8), :])
            if k == 4:
                return jnp.where(edge_high, center, ins[halo_at[4]][j, pl.ds(8 * g, 8), :])
            return readers[k](j, g)

        def lane_pieces(x):
            return [x[:, start : start + LANES] for start in range(0, width, LANES)]

        def upwind(up, down, slope):
            return jnp.maximum(up * slope, down * slope)

        def tile(i, j, low_j, high_j):
            t = targets[i]
            flow = table_ref[4, j] * to_1
            drift = table_ref[t, j] * to_2
            flow_up, flow_down = wide(flow + planner), wide(flow - planner)
            drift_up, drift_down = wide(drift + disturb_2), wide(drift - disturb_2)
            below = readers[t](j, 0)[0:1]
            above = readers[t](j, groups - 1)[7:8]
            if full:
                beyond = ins[vy_at][3 - t, pl.ds(j, 1), :]
                below, above = jnp.where(is_even, below, beyond), jnp.where(is_even, beyond, above)
            below, above = jnp.broadcast_to(below, (8, width)), jnp.broadcast_to(above, (8, width))
            ups = [below] + [pltpu.roll(readers[t](j, g), 1, 0) for g in range(groups)]
            downs = [pltpu.roll(readers[t](j, g), 7, 0) for g in range(groups)] + [above]
            for g in range(groups):
                w = readers[t](j, g)
                here = pl.ds(8 * g, 8)
                if full or t in (1, 2):
                    low_1, high_1 = neighbour(t - 1, j, g, w), neighbour(t + 1, j, g, w)
                    total = keep * w - damp_1 * (low_1 + high_1)
                    total = total + upwind(flow_up, flow_down, high_1 - low_1)
                else:
                    total = keep_outer * w

                pieces = lane_pieces(w)
                right = [pltpu.roll(p, 1, 1) for p in pieces]
                left = [pltpu.roll(p, LANES - 1, 1) for p in pieces]
                parts = []
                for p in range(len(pieces)):
                    low_4 = jnp.where(lane == 0, right[p - 1] if p > 0 else pieces[0], right[p])
                    high_4 = jnp.where(lane == LANES - 1, left[p + 1] if p + 1 < len(pieces) else pieces[p], left[p])
                    parts.append(upwind(adv_up[here, :], adv_down[here, :], high_4 - low_4) - damp_4 * (low_4 + high_4))
                total = total + jnp.concatenate(parts, axis=1)

                if low_j is None:
                    low_2 = jnp.where(vx_first, w, ins[low_at][t, here, :]) if full else w
                else:
                    low_2 = readers[t](low_j, g)
                if high_j is None:
                    high_2 = jnp.where(vx_last, w, ins[high_at][t, here, :]) if full else w
                else:
                    high_2 = readers[t](high_j, g)
                slope = high_2 - low_2
                bent = control_2 * slope
                total = total + (jnp.where(slope > 0.0, drift_up, drift_down) - bent) * slope

                low_3 = jnp.where(sublane == 0, ups[g], ups[g + 1])
                high_3 = jnp.where(sublane == 7, downs[g + 1], downs[g])
                slope = high_3 - low_3
                bent = control_3 * slope
                total = total + (jnp.where(slope > 0.0, acc_up[here, :], acc_down[here, :]) - bent) * slope

                twice = w + w
                bend_2 = low_2 + high_2 - twice
                bend_3 = low_3 + high_3 - twice
                if heun:
                    total = total + 0.5 * base_readers[i](j, g)
                if full:
                    total = total - damp_2 * bend_2 - damp_3 * bend_3
                    outs[i][j, here, :] = total
                else:
                    outs[3 * i][j, here, :] = total
                    outs[3 * i + 1][j, here, :] = bend_2
                    outs[3 * i + 2][j, here, :] = bend_3

        for i in range(count):
            tile(i, 0, None, 1)

        together = 2 if count == 1 and cells_v % 2 == 0 else 1

        @pl.loop(1, cells_v - 1, step=together)
        def _(j):
            for ahead in range(together):
                for i in range(count):
                    tile(i, j + ahead, j + ahead - 1, j + ahead + 1)

        for i in range(count):
            tile(i, cells_v - 1, cells_v - 2, None)

    return pl.pallas_call(
        body,
        out_shape=[f32(cells_v, half, width)] * n_out,
        in_specs=[scalars()] + [whole()] * n_in,
        out_specs=[whole()] * n_out,
        scratch_shapes=[pltpu.VMEM((half, LANES), jnp.float32)] * 2 + [pltpu.VMEM((half, width), jnp.float32)] * 2,
        compiler_params=compiler_params(),
        cost_estimate=estimate(),
        name="advance_" + "".join(str(t) for t in targets),
    )(table, *ops.arrays)


def outer_terms(sizes, rows, halo_rows, maxima, stepper, heun, table):
    cells_v, half, width, _, _ = sizes
    groups = half // 8
    late = stepper is None
    arrays = [r.array for r in rows] + list(halo_rows) + ([] if late else [maxima, stepper])

    def body(table_ref, *refs):
        row_refs, before_ref, after_ref, out_refs = refs[:4], refs[4], refs[5], refs[-2:]
        edge_low, edge_high = table_ref[5, 1] > 0.5, table_ref[5, 2] > 0.5
        known = Rates(sizes)
        if late:
            scale = jnp.ones((8, LANES), jnp.float32)
        else:
            scale = known.time_step(known.rates(refs[6], refs[7])) * (0.5 if heun else 1.0)

        def wide(x):
            return jnp.concatenate([x] * (width // LANES), axis=1)

        damp = wide(scale * (0.5 * known.rate_1 / known.step_1))
        planner = scale * (PLANNER_SPEED / (2.0 * known.step_1))
        to_1 = scale / (2.0 * known.step_1)

        together = 2 if cells_v % 2 == 0 else 1

        @pl.loop(0, cells_v, step=together)
        def _(start):
            for j, g in [(start + ahead, g) for ahead in range(together) for g in range(groups)]:
                here = pl.ds(8 * g, 8)
                flow = table_ref[4, j] * to_1
                up, down = wide(flow + planner), wide(flow - planner)
                for i in range(2):
                    w = row_refs[3 * i][j, here, :]
                    inside = row_refs[1 + i][j, here, :]
                    if i == 0:
                        low, high = jnp.where(edge_low, w, before_ref[j, here, :]), inside
                    else:
                        low, high = inside, jnp.where(edge_high, w, after_ref[j, here, :])
                    slope = high - low
                    out_refs[i][j, here, :] = jnp.maximum(up * slope, down * slope) - damp * (low + high - (w + w))

    return pl.pallas_call(
        body,
        out_shape=[f32(cells_v, half, width)] * 2,
        in_specs=[scalars()] + [whole()] * len(arrays),
        out_specs=[whole()] * 2,
        compiler_params=compiler_params(),
        cost_estimate=estimate(),
        name="outer_terms",
    )(table, *arrays)


def mend(sizes, edges, vx_low, vx_high, vy_next, maxima, stepper, heun, accel_second, table):
    cells_v, half, width, _, _ = sizes
    late = stepper is None
    first, second, before, last, edge, inner, _ = edges
    arrays = [first, second, before, last, edge, inner, vx_low, vx_high, vy_next, accel_second] + ([] if late else [maxima, stepper])

    def body(table_ref, *refs):
        first_ref, second_ref, before_ref, last_ref, edge_ref, inner_ref, low_ref, high_ref, next_ref, accel_ref = refs[:10]
        update_2, bend_2, update_3, bend_3 = refs[-4:]
        is_odd, _, _, vx_first, vx_last = (table_ref[5, i] > 0.5 for i in range(5))
        is_even = jnp.logical_not(is_odd)
        known = Rates(sizes)
        if late:
            scale = jnp.ones((8, LANES), jnp.float32)
        else:
            scale = known.time_step(known.rates(refs[10], refs[11])) * (0.5 if heun else 1.0)

        def wide(x):
            return jnp.concatenate([x] * (width // LANES), axis=1)

        disturb_2 = scale * (DISTURBANCE / (2.0 * known.step_2))
        disturb_3 = wide(scale * (DISTURBANCE / (2.0 * known.step_3)))
        control_2 = wide(scale * (1.0 / (8.0 * CONTROL_COST * known.step_2 * known.step_2)))
        control_3 = wide(scale * (1.0 / (8.0 * CONTROL_COST * known.step_3 * known.step_3)))
        to_2, to_3 = scale / (2.0 * known.step_2), wide(scale / (2.0 * known.step_3))

        def term(up, down, control, slope):
            return (jnp.where(slope > 0.0, up, down) - control * slope) * slope

        for t in range(4):
            for e, j in ((0, 0), (1, cells_v - 1)):
                drift = table_ref[t, j] * to_2
                up, down = wide(drift + disturb_2), wide(drift - disturb_2)
                for start in range(0, half, 8):
                    here = pl.ds(start, 8)
                    if e == 0:
                        own, inside = first_ref[t, here, :], second_ref[t, here, :]
                        halo = jnp.where(vx_first, own, low_ref[t, here, :])
                        right, wrong = inside - halo, inside - own
                    else:
                        own, inside = last_ref[t, here, :], before_ref[t, here, :]
                        halo = jnp.where(vx_last, own, high_ref[t, here, :])
                        right, wrong = halo - inside, own - inside
                    update_2[t, e, here, :] = term(up, down, control_2, right) - term(up, down, control_2, wrong)
                    bend_2[t, e, here, :] = halo - own
        at = jnp.where(is_even, half - 1, half)
        accel = jnp.broadcast_to(accel_ref[pl.ds(at, 1), :], (8, width)) * to_3
        up, down = accel + disturb_3, accel - disturb_3
        for t in range(4):
            for start in range(0, cells_v, 8):
                here = pl.ds(start, 8)
                own, inside, halo = edge_ref[t, here, :], inner_ref[t, here, :], next_ref[3 - t, here, :]
                right = jnp.where(is_even, halo - inside, inside - halo)
                wrong = jnp.where(is_even, own - inside, inside - own)
                update_3[t, here, :] = term(up, down, control_3, right) - term(up, down, control_3, wrong)
                bend_3[t, here, :] = halo - own

    return pl.pallas_call(
        body,
        out_shape=[f32(4, 2, half, width)] * 2 + [f32(4, cells_v, width)] * 2,
        in_specs=[scalars()] + [whole()] * len(arrays),
        out_specs=[whole()] * 4,
        compiler_params=compiler_params(),
        cost_estimate=estimate(),
        name="mend",
    )(table, *arrays)


def settle(sizes, targets, updates, costs, flags, damping=None, fields=None, prior=None, with_edges=True, mended=None):
    cells_v, half, width, total_vx, total_vy = sizes
    count = len(targets)
    ops = Operands()
    update_at = [[ops.add(a) for a in u] for u in updates]
    cost_at = [ops.add(c.array) for c in costs]
    field_at = [ops.add(f.array) for f in fields] if fields is not None else []
    mended_at = [ops.add(m) for m in mended] if mended is not None else []
    maxima_at = [ops.add(m) for m in damping[:3]] if damping is not None else []
    before_targets, before_outs = prior if prior is not None else ((), ())
    prior_at = [ops.add(a) for a in before_outs]
    n_in = len(ops.arrays)
    every = sorted(tuple(before_targets) + tuple(targets))
    groups = half // 8

    def body(flags_ref, *refs):
        ins, outs = refs[:n_in], refs[n_in:]
        fields_out = outs[:count]
        parity = flags_ref[0]
        is_even = parity == 0
        if damping is not None:
            known = Rates(sizes)
            step_rates = known.rates(ins[maxima_at[0]], ins[maxima_at[1]])
            rates = step_rates if maxima_at[1] == maxima_at[2] else known.rates(ins[maxima_at[0]], ins[maxima_at[2]])
            scale = known.time_step(step_rates) * damping[3]
            if fields is None:
                damp_2, damp_3 = scale * 0.5 * rates[0], scale * 0.5 * rates[1]
            else:
                damp_2, damp_3 = 0.5 * rates[0], 0.5 * rates[1]
            damp_2, damp_3, scale = (jnp.concatenate([x] * (width // LANES), axis=1) for x in (damp_2, damp_3, scale))
        cost_readers = [c.reader(ins[a], parity, half) for c, a in zip(costs, cost_at)]
        field_readers = [f.reader(ins[a], parity, half) for f, a in zip(fields or (), field_at)]
        sublane = lax.broadcasted_iota(jnp.int32, (8, width), 0)

        row_low = jnp.where(is_even, -1, 0)
        row_high = jnp.where(is_even, 7, -1)

        def tile(i, j, end=None):
            t = targets[i]
            out = []
            if mended is not None:
                along_2, twice_2, along_3, twice_3 = (ins[a] for a in mended_at)
                here = pl.ds(j, 1)
                beside = jnp.broadcast_to(along_3[t, here, :] - damp_3[0:1] * twice_3[t, here, :], (8, width))
            for g in range(groups):
                here = pl.ds(8 * g, 8)
                total = ins[update_at[i][0]][j, here, :]
                if len(update_at[i]) > 3:
                    total = total + ins[update_at[i][3]][j, here, :]
                if damping is not None:
                    total = total - damp_2 * ins[update_at[i][1]][j, here, :] - damp_3 * ins[update_at[i][2]][j, here, :]
                if mended is not None:
                    if g == 0:
                        total = total + jnp.where(sublane == row_low, beside, 0.0)
                    if g == groups - 1:
                        total = total + jnp.where(sublane == row_high, beside, 0.0)
                    if end is not None:
                        total = total + along_2[t, end, here, :] - damp_2 * twice_2[t, end, here, :]
                if fields is not None:
                    total = field_readers[i](j, g) + scale * total
                y = jnp.maximum(cost_readers[i](j, g), total)
                fields_out[i][j, here, :] = y
                out.append(y)
            return out

        if not with_edges:
            least_ref = outs[count]
            least = [functools.reduce(jnp.minimum, tile(i, 0, 0) + tile(i, cells_v - 1, 1)) for i in range(count)]

            def lower(j, least):
                return tuple(jnp.minimum(least[i], functools.reduce(jnp.minimum, tile(i, j))) for i in range(count))

            least = lax.fori_loop(1, cells_v - 1, lower, tuple(least))
            for i in range(count):
                least_ref[pl.ds(i, 1), :] = jnp.min(least[i], axis=0, keepdims=True)
            return

        first_ref, second_ref, before_ref, last_ref, edge_ref, inner_ref, part_ref = outs[count : count + 7]
        send_at = jnp.where(is_even, half - 1, 0)
        inner_at = jnp.where(is_even, half - 2, 1)
        wall_at = jnp.where(is_even, 0, half - 1)
        next_at = jnp.where(is_even, 1, half - 2)
        for position, t in enumerate(sorted(before_targets)):
            slot = every.index(t)
            for ref, at in zip((first_ref, second_ref, before_ref, last_ref, edge_ref, inner_ref), prior_at):
                ref[slot] = ins[at][position]

        def one(i, j, end=None):
            slot = every.index(targets[i])
            out = tile(i, j, end)
            edge_ref[slot, pl.ds(j, 1), :] = fields_out[i][j, pl.ds(send_at, 1), :]
            inner_ref[slot, pl.ds(j, 1), :] = fields_out[i][j, pl.ds(inner_at, 1), :]
            wall = jnp.abs(fields_out[i][j, pl.ds(next_at, 1), :] - fields_out[i][j, pl.ds(wall_at, 1), :])
            rolled = [pltpu.roll(y, 2, 0) for y in out]
            slopes_3 = [jnp.broadcast_to(wall, (8, width))]
            for g in range(groups):
                apart = jnp.where(sublane < 2, rolled[g - 1] if g > 0 else out[0], rolled[g])
                slopes_3.append(jnp.abs(out[g] - apart))
            return out, functools.reduce(jnp.maximum, slopes_3)

        def both(i, j, end=None):
            out, most_3 = one(i, j, end)
            slopes_2 = [jnp.abs(out[g] - fields_out[i][j - 2, pl.ds(8 * g, 8), :]) for g in range(groups)]
            return functools.reduce(jnp.maximum, slopes_2), most_3

        starts = [jnp.maximum(one(i, 0, 0)[1], one(i, 1)[1]) for i in range(count)]
        zero = jnp.zeros((8, width), jnp.float32)

        def step(j, carry):
            found = [both(i, j) for i in range(count)]
            return tuple((jnp.maximum(carry[i][0], found[i][0]), jnp.maximum(carry[i][1], found[i][1])) for i in range(count))

        most = lax.fori_loop(2, cells_v - 1, step, tuple((zero, start) for start in starts))
        most = list(most) + [both(i, cells_v - 1, 1) for i in range(count)]
        if prior is not None:
            most.append((ins[prior_at[6]][0], ins[prior_at[6]][1]))
        part_ref[0] = functools.reduce(jnp.maximum, [m[0] for m in most])
        part_ref[1] = functools.reduce(jnp.maximum, [m[1] for m in most])
        for i in range(count):
            slot = every.index(targets[i])
            first_ref[slot] = fields_out[i][0]
            second_ref[slot] = fields_out[i][1]
            before_ref[slot] = fields_out[i][cells_v - 2]
            last_ref[slot] = fields_out[i][cells_v - 1]

    n = len(every)
    shapes = [f32(cells_v, half, width)] * count
    if with_edges:
        shapes += [f32(n, half, width)] * 4 + [f32(n, cells_v, width)] * 2 + [f32(2, 8, width)]
    else:
        shapes.append(f32(count, width))
    outs = pl.pallas_call(
        body,
        out_shape=shapes,
        in_specs=[scalars()] + [whole()] * n_in,
        out_specs=[whole()] * len(shapes),
        compiler_params=compiler_params(),
        cost_estimate=estimate(),
        name="settle_" + "".join(str(t) for t in targets),
    )(flags, *ops.arrays)
    return outs[:count], outs[count:]


def spread(values):
    position = lax.broadcasted_iota(jnp.int32, (8, LANES), 0)
    out = jnp.zeros((8, LANES), jnp.float32)
    for row, value in enumerate(values):
        out = jnp.where(position == row, value, out)
    return out


def first_maxima(value, vx_low, vx_high, accel_first, accel_second, flags):
    rows, cells_v, total_vy, width = value.shape

    def body(flags_ref, v_ref, low_ref, high_ref, first_ref, second_ref, out_ref):
        vx_first, vx_last = flags_ref[3], flags_ref[4]
        vy_row = lax.broadcasted_iota(jnp.int32, (total_vy, width), 0)

        def of_vy(x):
            inner = jnp.where(vy_row >= 2, jnp.abs(x - pltpu.roll(x, 2, 0)), 0.0)
            wall = jnp.maximum(jnp.abs(x[1:2] - x[0:1]), jnp.abs(x[total_vy - 1 : total_vy] - x[total_vy - 2 : total_vy - 1]))
            return jnp.maximum(fold(inner), wall)

        most_2 = jnp.zeros((8, width), jnp.float32)
        most_3 = jnp.zeros((8, width), jnp.float32)
        for r in range(rows):
            x = v_ref[r, 0]
            most_3 = jnp.maximum(most_3, of_vy(x))
            most_2 = jnp.maximum(most_2, fold(jnp.abs(v_ref[r, 1] - jnp.where(vx_first == 1, x, low_ref[r]))))
            x = v_ref[r, cells_v - 1]
            most_3 = jnp.maximum(most_3, of_vy(x))
            most_2 = jnp.maximum(most_2, fold(jnp.abs(v_ref[r, cells_v - 2] - jnp.where(vx_last == 1, x, high_ref[r]))))

            def step(j, carry, r=r):
                most_2, most_3 = carry
                most_3 = jnp.maximum(most_3, of_vy(v_ref[r, j]))
                most_2 = jnp.maximum(most_2, fold(jnp.abs(v_ref[r, j + 1] - v_ref[r, j - 1])))
                return most_2, most_3

            most_2, most_3 = lax.fori_loop(1, cells_v - 1, step, (most_2, most_3))
        values = (jnp.max(most_2), jnp.max(most_3), jnp.max(jnp.abs(first_ref[...])), jnp.max(jnp.abs(second_ref[...])))
        out_ref[...] = spread(values)

    return pl.pallas_call(
        body,
        out_shape=f32(8, LANES),
        in_specs=[scalars()] + [whole()] * 5,
        out_specs=whole(),
        compiler_params=compiler_params(),
        cost_estimate=estimate(),
        name="first_maxima",
    )(flags, value, vx_low, vx_high, accel_first, accel_second)


def edge_maxima(edges, vx_low, vx_high, vy_next, flags):
    first, second, before, last, _, inner, part = edges

    def body(flags_ref, first_ref, second_ref, before_ref, last_ref, low_ref, high_ref, inner_ref, next_ref, part_ref, out_ref):
        vx_first, vx_last = flags_ref[3], flags_ref[4]
        most_2, most_3 = part_ref[0], part_ref[1]
        for t in range(4):
            low = jnp.where(vx_first == 1, first_ref[t], low_ref[t])
            high = jnp.where(vx_last == 1, last_ref[t], high_ref[t])
            most_2 = jnp.maximum(most_2, fold(jnp.abs(second_ref[t] - low)))
            most_2 = jnp.maximum(most_2, fold(jnp.abs(high - before_ref[t])))
            most_3 = jnp.maximum(most_3, fold(jnp.abs(inner_ref[t] - next_ref[3 - t])))
        out_ref[...] = spread((jnp.max(most_2), jnp.max(most_3)))

    return pl.pallas_call(
        body,
        out_shape=f32(8, LANES),
        in_specs=[scalars()] + [whole()] * 9,
        out_specs=whole(),
        compiler_params=compiler_params(),
        cost_estimate=estimate(),
        name="edge_maxima",
    )(flags, first, second, before, last, vx_low, vx_high, inner, vy_next, part)


def copies(flags_ref, pieces, out_ref, sems, which):
    parity = flags_ref[0]
    half = out_ref.shape[2] // 2
    start = pl.multiple_of((parity if which == 0 else 1 - parity) * half, half)
    return [
        pltpu.make_async_copy(ref, out_ref.at[parity if outer else 1 - parity, :, pl.ds(start, half), :], sems.at[i])
        for i, (outer, ref) in enumerate(pieces)
    ]


def place(flags, pieces, result, shape, which=0):
    count = len(pieces)

    def body(flags_ref, *refs):
        moves = copies(flags_ref, [(pieces[i][0], refs[i]) for i in range(count)], refs[-2], refs[-1], which)
        for move in moves:
            move.start()
        for move in moves:
            move.wait()

    anywhere = pl.BlockSpec(memory_space=pl.ANY)
    extra = [] if result is None else [result]
    return pl.pallas_call(
        body,
        in_specs=[scalars()] + [whole()] * count + [anywhere] * len(extra),
        out_specs=anywhere,
        out_shape=f32(*shape),
        input_output_aliases={} if result is None else {1 + count: 0},
        scratch_shapes=[pltpu.SemaphoreType.DMA((count,))],
        compiler_params=compiler_params(),
        cost_estimate=estimate(),
        name="place",
    )(flags, *[p[1] for p in pieces], *extra)


def finish(flags, outer, least, least_got, result):
    def body(flags_ref, outer_ref, least_ref, got_ref, _, out_ref, funnel_ref, sems):
        parity = flags_ref[0]
        (move,) = copies(flags_ref, [(True, outer_ref)], out_ref, sems, 1)
        move.start()
        funnel_ref[pl.ds(parity, 1), :] = jnp.minimum(least_ref[0:1], got_ref[1:2])
        funnel_ref[pl.ds(1 - parity, 1), :] = jnp.minimum(least_ref[1:2], got_ref[0:1])
        move.wait()

    anywhere = pl.BlockSpec(memory_space=pl.ANY)
    return pl.pallas_call(
        body,
        in_specs=[scalars()] + [whole()] * 3 + [anywhere],
        out_specs=[anywhere, whole()],
        out_shape=[f32(*result.shape), f32(2, result.shape[3])],
        input_output_aliases={4: 0},
        scratch_shapes=[pltpu.SemaphoreType.DMA((1,))],
        compiler_params=compiler_params(),
        cost_estimate=estimate(),
        name="finish",
    )(flags, outer, least, least_got, result)


def per_device(value, cost, accel_first, accel_second):
    n_px, n_vx = lax.axis_size("px"), lax.axis_size("vx")
    rows, cells_v, total_vy, width = value.shape
    half = total_vy // 2
    total_vx = cells_v * n_vx
    sizes = (cells_v, half, width, total_vx, total_vy)
    px, vx = lax.axis_index("px"), lax.axis_index("vx")
    parity = px % 2
    flags = jnp.stack(
        [
            parity,
            ((px == 0) | (px == n_px - 1)).astype(jnp.int32),
            ((px == 1) | (px == n_px - 2)).astype(jnp.int32),
            (vx == 0).astype(jnp.int32),
            (vx == n_vx - 1).astype(jnp.int32),
        ]
    ).astype(jnp.int32)

    def partner(x):
        return lax.ppermute(x, "px", [(i, i ^ 1) for i in range(n_px)])

    def from_low_vx(x):
        return lax.ppermute(x, "vx", [(i, i + 1) for i in range(n_vx - 1)])

    def from_high_vx(x):
        return lax.ppermute(x, "vx", [(i + 1, i) for i in range(n_vx - 1)])

    def halo_before(outermost):
        moves = [(i, i + 2) for i in range(0, n_px - 2, 2)] + [(i, i - 2) for i in range(3, n_px, 2)]
        return lax.ppermute(outermost, "px", moves)

    def halo_after(outer):
        moves = [(i, i - 2) for i in range(2, n_px, 2)] + [(i, i + 2) for i in range(1, n_px - 2, 2)]
        return lax.ppermute(outer, "px", moves)

    def after(array, *others):
        return lax.optimization_barrier((array, *others))[0]

    def share(maxima, beside=None, partner_done=False):
        steps = [("vx", 1 << k) for k in range((n_vx - 1).bit_length())] + [("px", 1 << k) for k in range((n_px - 1).bit_length())]
        if partner_done:
            steps.remove(("px", 1))
        for place_at, (axis, apart) in enumerate(steps):
            other = lax.ppermute(maxima, axis, [(i, i ^ apart) for i in range(lax.axis_size(axis))])
            if beside is not None and place_at in beside:
                other = after(other, *beside[place_at])
            maxima = jnp.maximum(maxima, other)
        return maxima

    def half_of(array, row, which):
        return lax.dynamic_slice(array, (row, 0, which * half, 0), (1, cells_v, half, width))[0]

    value_outer = half_of(value, parity, 1 - parity)
    late = after(parity, value_outer)
    value_outer_got = partner(value_outer)
    push_got = partner(after(accel_first, value_outer))

    low_own = from_low_vx(after(value[:, cells_v - 1], value_outer))
    high_own = from_high_vx(after(value[:, 0], value_outer))
    row_needed = lax.dynamic_slice(value, (0, 0, half - parity, 0), (rows, cells_v, 1, width))[:, :, 0]
    row_given = lax.dynamic_slice(value, (0, 0, half - 1 + parity, 0), (rows, cells_v, 1, width))[:, :, 0]
    row_got = partner(after(row_given, value_outer))

    maxima = first_maxima(value, low_own, high_own, accel_first, accel_second, flags)
    maxima = jnp.maximum(maxima, partner(maxima))
    ahead = (maxima, row_got, push_got)
    value_inner_got = partner(after(half_of(value, 1 - late, 1 - late), *ahead))
    cost_outer_got = partner(after(half_of(cost, late, 1 - late), *ahead))
    cost_inner_got = partner(after(half_of(cost, 1 - late, 1 - late), *ahead))
    shared_first = share(maxima, partner_done=True)

    def pick(x, which):
        return lax.dynamic_index_in_dim(x, which, 0, keepdims=True)

    def in_chain(mine, others):
        return jnp.concatenate([pick(mine, parity), pick(mine, 1 - parity), pick(others, parity), pick(others, 1 - parity)], axis=0)

    def halo_chain(own, received):
        mine = lax.dynamic_slice(own, (0, parity * half, 0), (rows, half, width))
        return jnp.concatenate([pick(mine, parity), pick(mine, 1 - parity), received], axis=0)

    vx_low = halo_chain(low_own, from_low_vx(jnp.stack([value_inner_got[cells_v - 1], value_outer_got[cells_v - 1]])))
    vx_high = halo_chain(high_own, from_high_vx(jnp.stack([value_inner_got[0], value_outer_got[0]])))
    vy_next = jnp.concatenate([pick(row_got, 1 - parity), pick(row_got, parity), pick(row_needed, 1 - parity), pick(row_needed, parity)], axis=0)
    push = in_chain(accel_first, push_got)
    positions = (vx * cells_v + jnp.arange(cells_v, dtype=jnp.int32)).astype(jnp.float32)
    speed = (2.0 * positions + 1.0 - total_vx) * (VELOCITY_LIMIT / total_vx)
    speed = jnp.where(parity == 0, speed, -speed)
    table = jnp.concatenate([push, speed[None], jnp.pad(flags.astype(jnp.float32), (0, cells_v - flags.shape[0]))[None]], axis=0)

    chain = [Own(value, True), Own(value, False), Row(value_inner_got), Row(value_outer_got)]
    costs = [Own(cost, True), Own(cost, False), Row(cost_inner_got), Row(cost_outer_got)]
    halo_rows = (halo_before(value_outer_got), halo_after(half_of(value, late, late)))

    every = (0, 1, 2, 3)

    def advanced(targets, field, bases, halos, stepper, table=table):
        got = advance(sizes, targets, field, bases, halos, shared_first, stepper, accel_second, table)
        each = len(got) // len(targets)
        return {t: got[each * i : each * (i + 1)] for i, t in enumerate(targets)}

    def settled(targets, updates, **kw):
        return settle(sizes, targets, [updates[t] for t in targets], [costs[t] for t in targets], flags, **kw)

    def next_updates(field, edges, bases, stepper, halo_rows, outer_later=False):
        first, _, _, last, edge, _, _ = edges
        low, high, row = from_low_vx(last), from_high_vx(first), partner(edge)
        heun = bases is not None

        def ahead(targets, table=table):
            return advanced(targets, field, [bases[t] for t in targets] if heun else None, None, stepper, table)

        def terms(table=table):
            return outer_terms(sizes, field, halo_rows, shared_first, stepper, heun, table)

        updates = ahead((1, 2))
        low, high, row = lax.optimization_barrier((low, high, row, updates))[:3]
        mended = mend(sizes, edges, low, high, row, shared_first, stepper, heun, accel_second, table)
        maxima = edge_maxima(edges, low, high, row, flags)
        if outer_later:

            def outer_updates(settled):
                late_table = after(table, settled)
                got, outer = ahead((0, 3), late_table), terms(late_table)
                return {0: got[0] + outer[:1], 3: got[3] + outer[1:]}

            return updates, outer_updates, mended, share(maxima, {1: mended})
        updates.update(ahead((0,)))
        updates.update(ahead((3,)))
        outer = terms()
        maxima = share(maxima, {1: mended, 2: updates[0], 3: updates[3], 4: outer})
        return {**updates, 0: updates[0] + outer[:1], 3: updates[3] + outer[1:]}, mended, maxima

    def settled_all(updates, **kw):
        fields = kw.pop("fields", None)
        some = {} if fields is None else {"fields": [fields[0], fields[3]]}
        (outer, far), edges = settled((0, 3), updates, **some, **kw)
        halo_rows = (halo_before(far), halo_after(outer))
        some = {} if fields is None else {"fields": [fields[1], fields[2]]}
        (inner, near), edges = settled((1, 2), updates, prior=((0, 3), edges), **some, **kw)
        return [Row(f) for f in (outer, inner, near, far)], edges, halo_rows

    halos = (halo_rows, vx_low, vx_high, vy_next)
    updates = advanced((1, 2), chain, None, halos, shared_first)
    updates.update(advanced((0, 3), chain, None, halos, shared_first))
    (outer, inner), edges = settled((0, 1), updates)
    beyond = halo_after(outer)
    (far,), edges = settled((3,), updates, prior=((0, 1), edges))
    halo_rows = (halo_before(far), beyond)
    (near,), edges = settled((2,), updates, prior=((0, 1, 3), edges))
    middle = [Row(f) for f in (outer, inner, near, far)]

    updates, mended, shared = next_updates(middle, edges, chain, shared_first, halo_rows)
    chain, edges, halo_rows = settled_all(updates, mended=mended, damping=(shared_first, shared_first, shared, 0.5))

    updates, mended, shared_second = next_updates(chain, edges, None, None, halo_rows)
    middle, edges, halo_rows = settled_all(updates, mended=mended, damping=(shared_first, shared_second, shared_second, 1.0), fields=chain)

    updates, outer_updates, mended, shared = next_updates(middle, edges, chain, shared_second, halo_rows, outer_later=True)
    damping = (shared_first, shared_second, shared, 0.5)
    (near,), (least_near,) = settled((2,), updates, damping=damping, mended=mended, with_edges=False)
    inner_got = partner(near)
    updates.update(outer_updates(near))
    (outer, inner, far), (least,) = settled((0, 1, 3), updates, damping=damping, mended=mended, with_edges=False)
    outer_got = partner(far)
    least = jnp.concatenate([least[:2], least_near, least[2:]], axis=0)
    for k in range((n_vx - 1).bit_length()):
        least = jnp.minimum(least, lax.ppermute(least, "vx", [(i, i ^ (1 << k)) for i in range(n_vx)]))
    least_got = partner(after(least[2:], far))
    final = place(flags, [(True, outer), (False, inner)], None, value.shape)
    return finish(flags, outer_got, least, least_got, place(flags, [(False, inner_got)], final, value.shape, 1))


def solution(mesh):
    placed = (P("px", "vx", None, None), P("px", "vx", None, None), P("px", "vx"), P())
    return jax.shard_map(
        per_device,
        mesh=mesh,
        in_specs=placed,
        out_specs=(P("px", "vx", None, None), P("px", None)),
        check_vma=False,
    )
```

```python
import functools

import jax
import jax.numpy as jnp
from jax import lax
from jax.experimental import pallas as pl
from jax.experimental.pallas import tpu as pltpu
from jax.sharding import PartitionSpec as P

VELOCITY_LIMIT = 1.0
PLANNER_SPEED = 0.3
DISTURBANCE = 0.2
CONTROL_COST = 1.0
COURANT = 0.5

LANES = 128


def compiler_params():
    return pltpu.CompilerParams(vmem_limit_bytes=8 * 1024 * 1024)


def whole():
    return pl.BlockSpec(memory_space=pltpu.VMEM)


def scalars():
    return pl.BlockSpec(memory_space=pltpu.SMEM)


def fold(tile):
    rows = tile.shape[0]
    out = tile[0:8]
    for start in range(8, rows, 8):
        out = jnp.maximum(out, tile[start : start + 8])
    return out


def fold_min(tile):
    rows = tile.shape[0]
    out = tile[0:8]
    for start in range(8, rows, 8):
        out = jnp.minimum(out, tile[start : start + 8])
    return out


def maximum_row(ref, row):
    return jnp.broadcast_to(ref[pl.ds(row, 1), :], (8, LANES))


class Own:
    def __init__(self, array, outer):
        self.array, self.outer = array, outer

    def reader(self, ref, parity, half):
        row = parity if self.outer else 1 - parity
        start = pl.multiple_of(parity * half, half)
        return lambda j, g: ref[row, j, pl.ds(pl.multiple_of(start + 8 * g, 8), 8), :]


class Row:
    def __init__(self, array):
        self.array = array

    def reader(self, ref, parity, half):
        return lambda j, g: ref[j, pl.ds(8 * g, 8), :]


class Rates:
    def __init__(self, sizes):
        cells_v, half, width, total_vx, total_vy = sizes
        self.step_2 = 2.0 * VELOCITY_LIMIT / total_vx
        self.step_3 = 2.0 * VELOCITY_LIMIT / total_vy
        self.step_1 = self.step_2 * self.step_3
        self.rate_1 = VELOCITY_LIMIT * (total_vx - 1) / total_vx + PLANNER_SPEED
        self.rate_4 = VELOCITY_LIMIT * (total_vy - 1) / total_vy + PLANNER_SPEED

    def rates(self, limits, maxima):
        rate_2 = maximum_row(limits, 2) + DISTURBANCE + maximum_row(maxima, 0) * (0.5 / (self.step_2 * CONTROL_COST))
        rate_3 = maximum_row(limits, 3) + DISTURBANCE + maximum_row(maxima, 1) * (0.5 / (self.step_3 * CONTROL_COST))
        return rate_2 * (1.0 / self.step_2), rate_3 * (1.0 / self.step_3)

    def time_step(self, rates):
        total = rates[0] + rates[1] + (self.rate_1 + self.rate_4) / self.step_1
        return COURANT / total


class Operands:
    def __init__(self):
        self.arrays = []

    def add(self, array):
        for position, known in enumerate(self.arrays):
            if known is array:
                return position
        self.arrays.append(array)
        return len(self.arrays) - 1


def f32(*shape):
    return jax.ShapeDtypeStruct(shape, jnp.float32)


def estimate():
    return pl.CostEstimate(flops=0, bytes_accessed=0, transcendentals=0)


def advance(sizes, targets, rows, bases, halos, maxima, stepper, accel_second, table):
    cells_v, half, width, total_vx, total_vy = sizes
    count = len(targets)
    heun = bases is not None
    late = stepper is None
    full = halos is not None
    ops = Operands()
    needed = sorted({k for t in targets for k in (t - 1, t, t + 1) if 0 <= k <= 3})
    row_at = {k: ops.add(rows[k].array) for k in needed}
    base_at = [ops.add(b.array) for b in bases] if heun else []
    accel_at = ops.add(accel_second)
    if full:
        halo_rows, vx_low, vx_high, vy_next = halos
        halo_at = {k: ops.add(halo_rows[i]) for i, k in enumerate((-1, 4)) if any(abs(t - k) == 1 for t in targets)}
        low_at, high_at, vy_at = ops.add(vx_low), ops.add(vx_high), ops.add(vy_next)
    maxima_at = [] if late else [ops.add(maxima), ops.add(stepper)]
    n_in = len(ops.arrays)
    n_out = count * (1 if full else 3)
    groups = half // 8

    def body(table_ref, *refs):
        ins, outs = refs[:n_in], refs[n_in : n_in + n_out]
        adv_up, adv_down, acc_up, acc_down = refs[n_in + n_out :]
        is_odd, edge_low, edge_high, vx_first, vx_last = (table_ref[5, i] > 0.5 for i in range(5))
        is_even = jnp.logical_not(is_odd)
        parity = jnp.where(is_odd, 1, 0)
        known = Rates(sizes)
        step_1, step_2, step_3 = known.step_1, known.step_2, known.step_3
        if late:
            scale = jnp.ones((8, LANES), jnp.float32)
        else:
            rates = known.rates(ins[maxima_at[0]], ins[maxima_at[1]])
            scale = known.time_step(rates) * (0.5 if heun else 1.0)
        damp_1 = scale * (0.5 * known.rate_1 / step_1)
        damp_4 = scale * (0.5 * known.rate_4 / step_1)
        keep = 2.0 * (damp_1 + damp_4)
        if not late:
            keep = keep + (0.5 if heun else 1.0)
        if full:
            damp_2, damp_3 = scale * 0.5 * rates[0], scale * 0.5 * rates[1]
        planner = scale * (PLANNER_SPEED / (2.0 * step_1))
        disturb_2 = scale * (DISTURBANCE / (2.0 * step_2))
        disturb_3 = scale * (DISTURBANCE / (2.0 * step_3))
        control_2 = scale * (1.0 / (8.0 * CONTROL_COST * step_2 * step_2))
        control_3 = scale * (1.0 / (8.0 * CONTROL_COST * step_3 * step_3))
        to_1, to_2, to_3 = scale / (2.0 * step_1), scale / (2.0 * step_2), scale / (2.0 * step_3)

        def wide(x):
            return jnp.concatenate([x] * (width // LANES), axis=1)

        start = pl.multiple_of(parity * half, half)
        for g in range(groups):
            here = pl.ds(8 * g, 8)
            vy = (parity * half + 8 * g + lax.broadcasted_iota(jnp.int32, (8, LANES), 0)).astype(jnp.float32)
            speed_y = (2.0 * vy + (1.0 - total_vy)) * (VELOCITY_LIMIT / total_vy) * to_1
            adv_up[here, :] = speed_y + planner
            adv_down[here, :] = speed_y - planner
            accel = ins[accel_at][pl.ds(pl.multiple_of(start + 8 * g, 8), 8), :] * wide(to_3)
            acc_up[here, :] = accel + wide(disturb_3)
            acc_down[here, :] = accel - wide(disturb_3)
        keep_outer = wide(keep - 2.0 * damp_1)
        keep, damp_1, control_2, control_3 = wide(keep), wide(damp_1), wide(control_2), wide(control_3)
        if full:
            damp_2, damp_3 = wide(damp_2), wide(damp_3)

        readers = {k: rows[k].reader(ins[row_at[k]], parity, half) for k in needed}
        base_readers = [b.reader(ins[a], parity, half) for b, a in zip(bases, base_at)] if heun else None
        sublane = lax.broadcasted_iota(jnp.int32, (8, width), 0)
        lane = lax.broadcasted_iota(jnp.int32, (8, LANES), 1)

        def neighbour(k, j, g, center):
            if k == -1:
                return jnp.where(edge_low, center, ins[halo_at[-1]][j, pl.ds(8 * g, 8), :])
            if k == 4:
                return jnp.where(edge_high, center, ins[halo_at[4]][j, pl.ds(8 * g, 8), :])
            return readers[k](j, g)

        def lane_pieces(x):
            return [x[:, start : start + LANES] for start in range(0, width, LANES)]

        def upwind(up, down, slope):
            return jnp.maximum(up * slope, down * slope)

        def tile(i, j, low_j, high_j):
            t = targets[i]
            flow = table_ref[4, j] * to_1
            drift = table_ref[t, j] * to_2
            flow_up, flow_down = wide(flow + planner), wide(flow - planner)
            drift_up, drift_down = wide(drift + disturb_2), wide(drift - disturb_2)
            below = readers[t](j, 0)[0:1]
            above = readers[t](j, groups - 1)[7:8]
            if full:
                beyond = ins[vy_at][3 - t, pl.ds(j, 1), :]
                below, above = jnp.where(is_even, below, beyond), jnp.where(is_even, beyond, above)
            below, above = jnp.broadcast_to(below, (8, width)), jnp.broadcast_to(above, (8, width))
            ups = [below] + [pltpu.roll(readers[t](j, g), 1, 0) for g in range(groups)]
            downs = [pltpu.roll(readers[t](j, g), 7, 0) for g in range(groups)] + [above]
            for g in range(groups):
                w = readers[t](j, g)
                here = pl.ds(8 * g, 8)
                if full or t in (1, 2):
                    low_1, high_1 = neighbour(t - 1, j, g, w), neighbour(t + 1, j, g, w)
                    total = keep * w - damp_1 * (low_1 + high_1)
                    total = total + upwind(flow_up, flow_down, high_1 - low_1)
                else:
                    total = keep_outer * w

                pieces = lane_pieces(w)
                right = [pltpu.roll(p, 1, 1) for p in pieces]
                left = [pltpu.roll(p, LANES - 1, 1) for p in pieces]
                parts = []
                for p in range(len(pieces)):
                    low_4 = jnp.where(lane == 0, right[p - 1] if p > 0 else pieces[0], right[p])
                    high_4 = jnp.where(lane == LANES - 1, left[p + 1] if p + 1 < len(pieces) else pieces[p], left[p])
                    parts.append(upwind(adv_up[here, :], adv_down[here, :], high_4 - low_4) - damp_4 * (low_4 + high_4))
                total = total + jnp.concatenate(parts, axis=1)

                if low_j is None:
                    low_2 = jnp.where(vx_first, w, ins[low_at][t, here, :]) if full else w
                else:
                    low_2 = readers[t](low_j, g)
                if high_j is None:
                    high_2 = jnp.where(vx_last, w, ins[high_at][t, here, :]) if full else w
                else:
                    high_2 = readers[t](high_j, g)
                slope = high_2 - low_2
                bent = control_2 * slope
                total = total + (jnp.where(slope > 0.0, drift_up, drift_down) - bent) * slope

                low_3 = jnp.where(sublane == 0, ups[g], ups[g + 1])
                high_3 = jnp.where(sublane == 7, downs[g + 1], downs[g])
                slope = high_3 - low_3
                bent = control_3 * slope
                total = total + (jnp.where(slope > 0.0, acc_up[here, :], acc_down[here, :]) - bent) * slope

                twice = w + w
                bend_2 = low_2 + high_2 - twice
                bend_3 = low_3 + high_3 - twice
                if heun:
                    total = total + 0.5 * base_readers[i](j, g)
                if full:
                    total = total - damp_2 * bend_2 - damp_3 * bend_3
                    outs[i][j, here, :] = total
                else:
                    outs[3 * i][j, here, :] = total
                    outs[3 * i + 1][j, here, :] = bend_2
                    outs[3 * i + 2][j, here, :] = bend_3

        for i in range(count):
            tile(i, 0, None, 1)

        together = 2 if count == 1 and cells_v % 2 == 0 else 1

        @pl.loop(1, cells_v - 1, step=together)
        def _(j):
            for ahead in range(together):
                for i in range(count):
                    tile(i, j + ahead, j + ahead - 1, j + ahead + 1)

        for i in range(count):
            tile(i, cells_v - 1, cells_v - 2, None)

    return pl.pallas_call(
        body,
        out_shape=[f32(cells_v, half, width)] * n_out,
        in_specs=[scalars()] + [whole()] * n_in,
        out_specs=[whole()] * n_out,
        scratch_shapes=[pltpu.VMEM((half, LANES), jnp.float32)] * 2 + [pltpu.VMEM((half, width), jnp.float32)] * 2,
        compiler_params=compiler_params(),
        cost_estimate=estimate(),
        name="advance_" + "".join(str(t) for t in targets),
    )(table, *ops.arrays)


def outer_terms(sizes, rows, halo_rows, parts, maxima, stepper, heun, table):
    cells_v, half, width, _, _ = sizes
    groups = half // 8
    late = stepper is None
    arrays = [r.array for r in rows] + list(halo_rows) + list(parts) + ([] if late else [maxima, stepper])

    def body(table_ref, *refs):
        row_refs, before_ref, after_ref, part_refs, out_refs = refs[:4], refs[4], refs[5], refs[6:8], refs[-2:]
        edge_low, edge_high = table_ref[5, 1] > 0.5, table_ref[5, 2] > 0.5
        known = Rates(sizes)
        if late:
            scale = jnp.ones((8, LANES), jnp.float32)
        else:
            scale = known.time_step(known.rates(refs[8], refs[9])) * (0.5 if heun else 1.0)

        def wide(x):
            return jnp.concatenate([x] * (width // LANES), axis=1)

        damp = wide(scale * (0.5 * known.rate_1 / known.step_1))
        planner = scale * (PLANNER_SPEED / (2.0 * known.step_1))
        to_1 = scale / (2.0 * known.step_1)

        together = 2 if cells_v % 2 == 0 else 1

        @pl.loop(0, cells_v, step=together)
        def _(start):
            for j, g in [(start + ahead, g) for ahead in range(together) for g in range(groups)]:
                here = pl.ds(8 * g, 8)
                flow = table_ref[4, j] * to_1
                up, down = wide(flow + planner), wide(flow - planner)
                for i in range(2):
                    w = row_refs[3 * i][j, here, :]
                    inside = row_refs[1 + i][j, here, :]
                    if i == 0:
                        low, high = jnp.where(edge_low, w, before_ref[j, here, :]), inside
                    else:
                        low, high = inside, jnp.where(edge_high, w, after_ref[j, here, :])
                    slope = high - low
                    total = part_refs[i][j, here, :] + jnp.maximum(up * slope, down * slope)
                    out_refs[i][j, here, :] = total - damp * (low + high - (w + w))

    return pl.pallas_call(
        body,
        out_shape=[f32(cells_v, half, width)] * 2,
        in_specs=[scalars()] + [whole()] * len(arrays),
        out_specs=[whole()] * 2,
        compiler_params=compiler_params(),
        cost_estimate=estimate(),
        name="outer_terms",
    )(table, *arrays)


def mend(sizes, edges, vx_low, vx_high, vy_next, maxima, stepper, heun, accel_second, table):
    cells_v, half, width, _, _ = sizes
    late = stepper is None
    first, second, before, last, edge, inner, _ = edges
    arrays = [first, second, before, last, edge, inner, vx_low, vx_high, vy_next, accel_second] + ([] if late else [maxima, stepper])

    def body(table_ref, *refs):
        first_ref, second_ref, before_ref, last_ref, edge_ref, inner_ref, low_ref, high_ref, next_ref, accel_ref = refs[:10]
        update_2, bend_2, update_3, bend_3 = refs[-4:]
        is_odd, _, _, vx_first, vx_last = (table_ref[5, i] > 0.5 for i in range(5))
        is_even = jnp.logical_not(is_odd)
        known = Rates(sizes)
        if late:
            scale = jnp.ones((8, LANES), jnp.float32)
        else:
            scale = known.time_step(known.rates(refs[10], refs[11])) * (0.5 if heun else 1.0)

        def wide(x):
            return jnp.concatenate([x] * (width // LANES), axis=1)

        disturb_2 = scale * (DISTURBANCE / (2.0 * known.step_2))
        disturb_3 = wide(scale * (DISTURBANCE / (2.0 * known.step_3)))
        control_2 = wide(scale * (1.0 / (8.0 * CONTROL_COST * known.step_2 * known.step_2)))
        control_3 = wide(scale * (1.0 / (8.0 * CONTROL_COST * known.step_3 * known.step_3)))
        to_2, to_3 = scale / (2.0 * known.step_2), wide(scale / (2.0 * known.step_3))

        def term(up, down, control, slope):
            return (jnp.where(slope > 0.0, up, down) - control * slope) * slope

        for t in range(4):
            for e, j in ((0, 0), (1, cells_v - 1)):
                drift = table_ref[t, j] * to_2
                up, down = wide(drift + disturb_2), wide(drift - disturb_2)
                for start in range(0, half, 8):
                    here = pl.ds(start, 8)
                    if e == 0:
                        own, inside = first_ref[t, here, :], second_ref[t, here, :]
                        halo = jnp.where(vx_first, own, low_ref[t, here, :])
                        right, wrong = inside - halo, inside - own
                    else:
                        own, inside = last_ref[t, here, :], before_ref[t, here, :]
                        halo = jnp.where(vx_last, own, high_ref[t, here, :])
                        right, wrong = halo - inside, own - inside
                    update_2[t, e, here, :] = term(up, down, control_2, right) - term(up, down, control_2, wrong)
                    bend_2[t, e, here, :] = halo - own
        at = jnp.where(is_even, half - 1, half)
        accel = jnp.broadcast_to(accel_ref[pl.ds(at, 1), :], (8, width)) * to_3
        up, down = accel + disturb_3, accel - disturb_3
        for t in range(4):
            for start in range(0, cells_v, 8):
                here = pl.ds(start, 8)
                own, inside, halo = edge_ref[t, here, :], inner_ref[t, here, :], next_ref[3 - t, here, :]
                right = jnp.where(is_even, halo - inside, inside - halo)
                wrong = jnp.where(is_even, own - inside, inside - own)
                update_3[t, here, :] = term(up, down, control_3, right) - term(up, down, control_3, wrong)
                bend_3[t, here, :] = halo - own

    return pl.pallas_call(
        body,
        out_shape=[f32(4, 2, half, width)] * 2 + [f32(4, cells_v, width)] * 2,
        in_specs=[scalars()] + [whole()] * len(arrays),
        out_specs=[whole()] * 4,
        compiler_params=compiler_params(),
        cost_estimate=estimate(),
        name="mend",
    )(table, *arrays)


def settle(sizes, targets, updates, costs, flags, damping=None, fields=None, prior=None, with_edges=True, mended=None):
    cells_v, half, width, total_vx, total_vy = sizes
    count = len(targets)
    ops = Operands()
    update_at = [[ops.add(a) for a in u] for u in updates]
    cost_at = [ops.add(c.array) for c in costs]
    field_at = [ops.add(f.array) for f in fields] if fields is not None else []
    mended_at = [ops.add(m) for m in mended] if mended is not None else []
    maxima_at = [ops.add(m) for m in damping[:3]] if damping is not None else []
    before_targets, before_outs = prior if prior is not None else ((), ())
    prior_at = [ops.add(a) for a in before_outs]
    n_in = len(ops.arrays)
    every = sorted(tuple(before_targets) + tuple(targets))
    groups = half // 8

    def body(flags_ref, *refs):
        ins, outs = refs[:n_in], refs[n_in:]
        fields_out = outs[:count]
        parity = flags_ref[0]
        is_even = parity == 0
        if damping is not None:
            known = Rates(sizes)
            step_rates = known.rates(ins[maxima_at[0]], ins[maxima_at[1]])
            rates = step_rates if maxima_at[1] == maxima_at[2] else known.rates(ins[maxima_at[0]], ins[maxima_at[2]])
            scale = known.time_step(step_rates) * damping[3]
            if fields is None:
                damp_2, damp_3 = scale * 0.5 * rates[0], scale * 0.5 * rates[1]
            else:
                damp_2, damp_3 = 0.5 * rates[0], 0.5 * rates[1]
            damp_2, damp_3, scale = (jnp.concatenate([x] * (width // LANES), axis=1) for x in (damp_2, damp_3, scale))
        cost_readers = [c.reader(ins[a], parity, half) for c, a in zip(costs, cost_at)]
        field_readers = [f.reader(ins[a], parity, half) for f, a in zip(fields or (), field_at)]
        sublane = lax.broadcasted_iota(jnp.int32, (8, width), 0)

        row_low = jnp.where(is_even, -1, 0)
        row_high = jnp.where(is_even, 7, -1)

        def tile(i, j, end=None):
            t = targets[i]
            out = []
            if mended is not None:
                along_2, twice_2, along_3, twice_3 = (ins[a] for a in mended_at)
                here = pl.ds(j, 1)
                beside = jnp.broadcast_to(along_3[t, here, :] - damp_3[0:1] * twice_3[t, here, :], (8, width))
            for g in range(groups):
                here = pl.ds(8 * g, 8)
                total = ins[update_at[i][0]][j, here, :]
                if damping is not None:
                    total = total - damp_2 * ins[update_at[i][1]][j, here, :] - damp_3 * ins[update_at[i][2]][j, here, :]
                if mended is not None:
                    if g == 0:
                        total = total + jnp.where(sublane == row_low, beside, 0.0)
                    if g == groups - 1:
                        total = total + jnp.where(sublane == row_high, beside, 0.0)
                    if end is not None:
                        total = total + along_2[t, end, here, :] - damp_2 * twice_2[t, end, here, :]
                if fields is not None:
                    total = field_readers[i](j, g) + scale * total
                y = jnp.maximum(cost_readers[i](j, g), total)
                fields_out[i][j, here, :] = y
                out.append(y)
            return out

        if not with_edges:
            least_ref = outs[count]
            least = [functools.reduce(jnp.minimum, tile(i, 0, 0) + tile(i, cells_v - 1, 1)) for i in range(count)]

            def lower(j, least):
                return tuple(jnp.minimum(least[i], functools.reduce(jnp.minimum, tile(i, j))) for i in range(count))

            least = lax.fori_loop(1, cells_v - 1, lower, tuple(least))
            for i in range(count):
                least_ref[pl.ds(i, 1), :] = jnp.min(least[i], axis=0, keepdims=True)
            return

        first_ref, second_ref, before_ref, last_ref, edge_ref, inner_ref, part_ref = outs[count : count + 7]
        send_at = jnp.where(is_even, half - 1, 0)
        inner_at = jnp.where(is_even, half - 2, 1)
        wall_at = jnp.where(is_even, 0, half - 1)
        next_at = jnp.where(is_even, 1, half - 2)
        for position, t in enumerate(sorted(before_targets)):
            slot = every.index(t)
            for ref, at in zip((first_ref, second_ref, before_ref, last_ref, edge_ref, inner_ref), prior_at):
                ref[slot] = ins[at][position]

        def one(i, j, end=None):
            slot = every.index(targets[i])
            out = tile(i, j, end)
            edge_ref[slot, pl.ds(j, 1), :] = fields_out[i][j, pl.ds(send_at, 1), :]
            inner_ref[slot, pl.ds(j, 1), :] = fields_out[i][j, pl.ds(inner_at, 1), :]
            wall = jnp.abs(fields_out[i][j, pl.ds(next_at, 1), :] - fields_out[i][j, pl.ds(wall_at, 1), :])
            rolled = [pltpu.roll(y, 2, 0) for y in out]
            slopes_3 = [jnp.broadcast_to(wall, (8, width))]
            for g in range(groups):
                apart = jnp.where(sublane < 2, rolled[g - 1] if g > 0 else out[0], rolled[g])
                slopes_3.append(jnp.abs(out[g] - apart))
            return out, functools.reduce(jnp.maximum, slopes_3)

        def both(i, j, end=None):
            out, most_3 = one(i, j, end)
            slopes_2 = [jnp.abs(out[g] - fields_out[i][j - 2, pl.ds(8 * g, 8), :]) for g in range(groups)]
            return functools.reduce(jnp.maximum, slopes_2), most_3

        starts = [jnp.maximum(one(i, 0, 0)[1], one(i, 1)[1]) for i in range(count)]
        zero = jnp.zeros((8, width), jnp.float32)

        def step(j, carry):
            found = [both(i, j) for i in range(count)]
            return tuple((jnp.maximum(carry[i][0], found[i][0]), jnp.maximum(carry[i][1], found[i][1])) for i in range(count))

        most = lax.fori_loop(2, cells_v - 1, step, tuple((zero, start) for start in starts))
        most = list(most) + [both(i, cells_v - 1, 1) for i in range(count)]
        if prior is not None:
            most.append((ins[prior_at[6]][0], ins[prior_at[6]][1]))
        part_ref[0] = functools.reduce(jnp.maximum, [m[0] for m in most])
        part_ref[1] = functools.reduce(jnp.maximum, [m[1] for m in most])
        for i in range(count):
            slot = every.index(targets[i])
            first_ref[slot] = fields_out[i][0]
            second_ref[slot] = fields_out[i][1]
            before_ref[slot] = fields_out[i][cells_v - 2]
            last_ref[slot] = fields_out[i][cells_v - 1]

    n = len(every)
    shapes = [f32(cells_v, half, width)] * count
    if with_edges:
        shapes += [f32(n, half, width)] * 4 + [f32(n, cells_v, width)] * 2 + [f32(2, 8, width)]
    else:
        shapes.append(f32(count, width))
    outs = pl.pallas_call(
        body,
        out_shape=shapes,
        in_specs=[scalars()] + [whole()] * n_in,
        out_specs=[whole()] * len(shapes),
        compiler_params=compiler_params(),
        cost_estimate=estimate(),
        name="settle_" + "".join(str(t) for t in targets),
    )(flags, *ops.arrays)
    return outs[:count], outs[count:]


def spread(values):
    position = lax.broadcasted_iota(jnp.int32, (8, LANES), 0)
    out = jnp.zeros((8, LANES), jnp.float32)
    for row, value in enumerate(values):
        out = jnp.where(position == row, value, out)
    return out


def first_maxima(value, vx_low, vx_high, accel_first, accel_second, flags):
    rows, cells_v, total_vy, width = value.shape

    def body(flags_ref, v_ref, low_ref, high_ref, first_ref, second_ref, out_ref):
        vx_first, vx_last = flags_ref[3], flags_ref[4]
        vy_row = lax.broadcasted_iota(jnp.int32, (total_vy, width), 0)

        def of_vy(x):
            inner = jnp.where(vy_row >= 2, jnp.abs(x - pltpu.roll(x, 2, 0)), 0.0)
            wall = jnp.maximum(jnp.abs(x[1:2] - x[0:1]), jnp.abs(x[total_vy - 1 : total_vy] - x[total_vy - 2 : total_vy - 1]))
            return jnp.maximum(fold(inner), wall)

        most_2 = jnp.zeros((8, width), jnp.float32)
        most_3 = jnp.zeros((8, width), jnp.float32)
        for r in range(rows):
            x = v_ref[r, 0]
            most_3 = jnp.maximum(most_3, of_vy(x))
            most_2 = jnp.maximum(most_2, fold(jnp.abs(v_ref[r, 1] - jnp.where(vx_first == 1, x, low_ref[r]))))
            x = v_ref[r, cells_v - 1]
            most_3 = jnp.maximum(most_3, of_vy(x))
            most_2 = jnp.maximum(most_2, fold(jnp.abs(v_ref[r, cells_v - 2] - jnp.where(vx_last == 1, x, high_ref[r]))))

            def step(j, carry, r=r):
                most_2, most_3 = carry
                most_3 = jnp.maximum(most_3, of_vy(v_ref[r, j]))
                most_2 = jnp.maximum(most_2, fold(jnp.abs(v_ref[r, j + 1] - v_ref[r, j - 1])))
                return most_2, most_3

            most_2, most_3 = lax.fori_loop(1, cells_v - 1, step, (most_2, most_3))
        values = (jnp.max(most_2), jnp.max(most_3), jnp.max(jnp.abs(first_ref[...])), jnp.max(jnp.abs(second_ref[...])))
        out_ref[...] = spread(values)

    return pl.pallas_call(
        body,
        out_shape=f32(8, LANES),
        in_specs=[scalars()] + [whole()] * 5,
        out_specs=whole(),
        compiler_params=compiler_params(),
        cost_estimate=estimate(),
        name="first_maxima",
    )(flags, value, vx_low, vx_high, accel_first, accel_second)


def edge_maxima(edges, vx_low, vx_high, vy_next, flags):
    first, second, before, last, _, inner, part = edges

    def body(flags_ref, first_ref, second_ref, before_ref, last_ref, low_ref, high_ref, inner_ref, next_ref, part_ref, out_ref):
        vx_first, vx_last = flags_ref[3], flags_ref[4]
        most_2, most_3 = part_ref[0], part_ref[1]
        for t in range(4):
            low = jnp.where(vx_first == 1, first_ref[t], low_ref[t])
            high = jnp.where(vx_last == 1, last_ref[t], high_ref[t])
            most_2 = jnp.maximum(most_2, fold(jnp.abs(second_ref[t] - low)))
            most_2 = jnp.maximum(most_2, fold(jnp.abs(high - before_ref[t])))
            most_3 = jnp.maximum(most_3, fold(jnp.abs(inner_ref[t] - next_ref[3 - t])))
        out_ref[...] = spread((jnp.max(most_2), jnp.max(most_3)))

    return pl.pallas_call(
        body,
        out_shape=f32(8, LANES),
        in_specs=[scalars()] + [whole()] * 9,
        out_specs=whole(),
        compiler_params=compiler_params(),
        cost_estimate=estimate(),
        name="edge_maxima",
    )(flags, first, second, before, last, vx_low, vx_high, inner, vy_next, part)


def copies(flags_ref, pieces, out_ref, sems, which):
    parity = flags_ref[0]
    half = out_ref.shape[2] // 2
    start = pl.multiple_of((parity if which == 0 else 1 - parity) * half, half)
    return [
        pltpu.make_async_copy(ref, out_ref.at[parity if outer else 1 - parity, :, pl.ds(start, half), :], sems.at[i])
        for i, (outer, ref) in enumerate(pieces)
    ]


def place(flags, pieces, result, shape, which=0):
    count = len(pieces)

    def body(flags_ref, *refs):
        moves = copies(flags_ref, [(pieces[i][0], refs[i]) for i in range(count)], refs[-2], refs[-1], which)
        for move in moves:
            move.start()
        for move in moves:
            move.wait()

    anywhere = pl.BlockSpec(memory_space=pl.ANY)
    extra = [] if result is None else [result]
    return pl.pallas_call(
        body,
        in_specs=[scalars()] + [whole()] * count + [anywhere] * len(extra),
        out_specs=anywhere,
        out_shape=f32(*shape),
        input_output_aliases={} if result is None else {1 + count: 0},
        scratch_shapes=[pltpu.SemaphoreType.DMA((count,))],
        compiler_params=compiler_params(),
        cost_estimate=estimate(),
        name="place",
    )(flags, *[p[1] for p in pieces], *extra)


def finish(flags, outer, least, least_got, result):
    def body(flags_ref, outer_ref, least_ref, got_ref, _, out_ref, funnel_ref, sems):
        parity = flags_ref[0]
        (move,) = copies(flags_ref, [(True, outer_ref)], out_ref, sems, 1)
        move.start()
        funnel_ref[pl.ds(parity, 1), :] = jnp.minimum(least_ref[0:1], got_ref[1:2])
        funnel_ref[pl.ds(1 - parity, 1), :] = jnp.minimum(least_ref[1:2], got_ref[0:1])
        move.wait()

    anywhere = pl.BlockSpec(memory_space=pl.ANY)
    return pl.pallas_call(
        body,
        in_specs=[scalars()] + [whole()] * 3 + [anywhere],
        out_specs=[anywhere, whole()],
        out_shape=[f32(*result.shape), f32(2, result.shape[3])],
        input_output_aliases={4: 0},
        scratch_shapes=[pltpu.SemaphoreType.DMA((1,))],
        compiler_params=compiler_params(),
        cost_estimate=estimate(),
        name="finish",
    )(flags, outer, least, least_got, result)


def per_device(value, cost, accel_first, accel_second):
    n_px, n_vx = lax.axis_size("px"), lax.axis_size("vx")
    rows, cells_v, total_vy, width = value.shape
    half = total_vy // 2
    total_vx = cells_v * n_vx
    sizes = (cells_v, half, width, total_vx, total_vy)
    px, vx = lax.axis_index("px"), lax.axis_index("vx")
    parity = px % 2
    flags = jnp.stack(
        [
            parity,
            ((px == 0) | (px == n_px - 1)).astype(jnp.int32),
            ((px == 1) | (px == n_px - 2)).astype(jnp.int32),
            (vx == 0).astype(jnp.int32),
            (vx == n_vx - 1).astype(jnp.int32),
        ]
    ).astype(jnp.int32)

    def partner(x):
        return lax.ppermute(x, "px", [(i, i ^ 1) for i in range(n_px)])

    def from_low_vx(x):
        return lax.ppermute(x, "vx", [(i, i + 1) for i in range(n_vx - 1)])

    def from_high_vx(x):
        return lax.ppermute(x, "vx", [(i + 1, i) for i in range(n_vx - 1)])

    def halo_before(outermost):
        moves = [(i, i + 2) for i in range(0, n_px - 2, 2)] + [(i, i - 2) for i in range(3, n_px, 2)]
        return lax.ppermute(outermost, "px", moves)

    def halo_after(outer):
        moves = [(i, i - 2) for i in range(2, n_px, 2)] + [(i, i + 2) for i in range(1, n_px - 2, 2)]
        return lax.ppermute(outer, "px", moves)

    def after(array, *others):
        return lax.optimization_barrier((array, *others))[0]

    def share(maxima, beside=None, partner_done=False):
        steps = [("vx", 1 << k) for k in range((n_vx - 1).bit_length())] + [("px", 1 << k) for k in range((n_px - 1).bit_length())]
        if partner_done:
            steps.remove(("px", 1))
        for place_at, (axis, apart) in enumerate(steps):
            other = lax.ppermute(maxima, axis, [(i, i ^ apart) for i in range(lax.axis_size(axis))])
            if beside is not None and place_at in beside:
                other = after(other, *beside[place_at])
            maxima = jnp.maximum(maxima, other)
        return maxima

    def half_of(array, row, which):
        return lax.dynamic_slice(array, (row, 0, which * half, 0), (1, cells_v, half, width))[0]

    value_outer = half_of(value, parity, 1 - parity)
    late = after(parity, value_outer)
    value_outer_got = partner(value_outer)
    push_got = partner(after(accel_first, value_outer))

    low_own = from_low_vx(after(value[:, cells_v - 1], value_outer))
    high_own = from_high_vx(after(value[:, 0], value_outer))
    row_needed = lax.dynamic_slice(value, (0, 0, half - parity, 0), (rows, cells_v, 1, width))[:, :, 0]
    row_given = lax.dynamic_slice(value, (0, 0, half - 1 + parity, 0), (rows, cells_v, 1, width))[:, :, 0]
    row_got = partner(after(row_given, value_outer))

    maxima = first_maxima(value, low_own, high_own, accel_first, accel_second, flags)
    maxima = jnp.maximum(maxima, partner(maxima))
    ahead = (maxima, row_got, push_got)
    value_inner_got = partner(after(half_of(value, 1 - late, 1 - late), *ahead))
    cost_outer_got = partner(after(half_of(cost, late, 1 - late), *ahead))
    cost_inner_got = partner(after(half_of(cost, 1 - late, 1 - late), *ahead))
    shared_first = share(maxima, partner_done=True)

    def pick(x, which):
        return lax.dynamic_index_in_dim(x, which, 0, keepdims=True)

    def in_chain(mine, others):
        return jnp.concatenate([pick(mine, parity), pick(mine, 1 - parity), pick(others, parity), pick(others, 1 - parity)], axis=0)

    def halo_chain(own, received):
        mine = lax.dynamic_slice(own, (0, parity * half, 0), (rows, half, width))
        return jnp.concatenate([pick(mine, parity), pick(mine, 1 - parity), received], axis=0)

    vx_low = halo_chain(low_own, from_low_vx(jnp.stack([value_inner_got[cells_v - 1], value_outer_got[cells_v - 1]])))
    vx_high = halo_chain(high_own, from_high_vx(jnp.stack([value_inner_got[0], value_outer_got[0]])))
    vy_next = jnp.concatenate([pick(row_got, 1 - parity), pick(row_got, parity), pick(row_needed, 1 - parity), pick(row_needed, parity)], axis=0)
    push = in_chain(accel_first, push_got)
    positions = (vx * cells_v + jnp.arange(cells_v, dtype=jnp.int32)).astype(jnp.float32)
    speed = (2.0 * positions + 1.0 - total_vx) * (VELOCITY_LIMIT / total_vx)
    speed = jnp.where(parity == 0, speed, -speed)
    table = jnp.concatenate([push, speed[None], jnp.pad(flags.astype(jnp.float32), (0, cells_v - flags.shape[0]))[None]], axis=0)

    chain = [Own(value, True), Own(value, False), Row(value_inner_got), Row(value_outer_got)]
    costs = [Own(cost, True), Own(cost, False), Row(cost_inner_got), Row(cost_outer_got)]
    halo_rows = (halo_before(value_outer_got), halo_after(half_of(value, late, late)))

    every = (0, 1, 2, 3)

    def advanced(targets, field, bases, halos, stepper, table=table):
        got = advance(sizes, targets, field, bases, halos, shared_first, stepper, accel_second, table)
        each = len(got) // len(targets)
        return {t: got[each * i : each * (i + 1)] for i, t in enumerate(targets)}

    def settled(targets, updates, **kw):
        return settle(sizes, targets, [updates[t] for t in targets], [costs[t] for t in targets], flags, **kw)

    def next_updates(field, edges, bases, stepper, halo_rows, outer_later=False):
        first, _, _, last, edge, _, _ = edges
        low, high, row = from_low_vx(last), from_high_vx(first), partner(edge)
        heun = bases is not None

        def ahead(targets, table=table):
            return advanced(targets, field, [bases[t] for t in targets] if heun else None, None, stepper, table)

        def with_terms(some, table=table):
            parts = (some[0][0], some[3][0])
            outer = outer_terms(sizes, field, halo_rows, parts, shared_first, stepper, heun, table)
            return {0: [outer[0], *some[0][1:]], 3: [outer[1], *some[3][1:]]}

        updates = ahead((1, 2))
        low, high, row = lax.optimization_barrier((low, high, row, updates))[:3]
        mended = mend(sizes, edges, low, high, row, shared_first, stepper, heun, accel_second, table)
        maxima = edge_maxima(edges, low, high, row, flags)
        if outer_later:

            def outer_updates(settled):
                late_table = after(table, settled)
                return with_terms(ahead((0, 3), late_table), late_table)

            return updates, outer_updates, mended, share(maxima, {1: mended})
        updates.update(ahead((0,)))
        updates.update(ahead((3,)))
        outer = with_terms(updates)
        maxima = share(maxima, {1: mended, 2: updates[0], 3: updates[3], 4: (outer[0][0], outer[3][0])})
        return {**updates, **outer}, mended, maxima

    def settled_all(updates, **kw):
        (outer, inner, near, far), edges = settled(every, updates, **kw)
        halo_rows = (halo_before(far), halo_after(outer))
        return [Row(f) for f in (outer, inner, near, far)], edges, halo_rows

    halos = (halo_rows, vx_low, vx_high, vy_next)
    updates = advanced((1, 2), chain, None, halos, shared_first)
    updates.update(advanced((0, 3), chain, None, halos, shared_first))
    (outer, inner), edges = settled((0, 1), updates)
    beyond = halo_after(outer)
    (far,), edges = settled((3,), updates, prior=((0, 1), edges))
    halo_rows = (halo_before(far), beyond)
    (near,), edges = settled((2,), updates, prior=((0, 1, 3), edges))
    middle = [Row(f) for f in (outer, inner, near, far)]

    updates, mended, shared = next_updates(middle, edges, chain, shared_first, halo_rows)
    chain, edges, halo_rows = settled_all(updates, mended=mended, damping=(shared_first, shared_first, shared, 0.5))

    updates, mended, shared_second = next_updates(chain, edges, None, None, halo_rows)
    middle, edges, halo_rows = settled_all(updates, mended=mended, damping=(shared_first, shared_second, shared_second, 1.0), fields=chain)

    updates, outer_updates, mended, shared = next_updates(middle, edges, chain, shared_second, halo_rows, outer_later=True)
    damping = (shared_first, shared_second, shared, 0.5)
    (near,), (least_near,) = settled((2,), updates, damping=damping, mended=mended, with_edges=False)
    inner_got = partner(near)
    updates.update(outer_updates(near))
    (outer, inner, far), (least,) = settled((0, 1, 3), updates, damping=damping, mended=mended, with_edges=False)
    outer_got = partner(far)
    least = jnp.concatenate([least[:2], least_near, least[2:]], axis=0)
    for k in range((n_vx - 1).bit_length()):
        least = jnp.minimum(least, lax.ppermute(least, "vx", [(i, i ^ (1 << k)) for i in range(n_vx)]))
    least_got = partner(after(least[2:], far))
    final = place(flags, [(True, outer), (False, inner)], None, value.shape)
    return finish(flags, outer_got, least, least_got, place(flags, [(False, inner_got)], final, value.shape, 1))


def solution(mesh):
    placed = (P("px", "vx", None, None), P("px", "vx", None, None), P("px", "vx"), P())
    return jax.shard_map(
        per_device,
        mesh=mesh,
        in_specs=placed,
        out_specs=(P("px", "vx", None, None), P("px", None)),
        check_vma=False,
    )
```
